32 devices in a mesh: fsdp: 4 (over z), context: 4 (over x, core), tensor: 2 (over y).
Axes of the slice: x: 2, y: 2, z: 4, core: 2. Of those that a mesh axis runs over, the one named last changes fastest.
Arguments:
- tokens: bfloat16 [2, 4, 2048, 1024], P(None, 'fsdp', 'context'), may hold values from -6 to 6
- cotangent: bfloat16 [2, 4, 2048, 1024], P(None, 'fsdp', 'context'), may hold values from -6 to 6
- doc_lengths: int32 [2, 4, 4], P(None, 'fsdp'), may hold values from 1 to 2045, as said below
- mixer_gain: bfloat16 [1024], P('fsdp'), may hold values from 0.5 to 1.5
- w_query: bfloat16 [1024, 512], P('fsdp', 'tensor'), may hold values from -0.1875 to 0.1875
- key_matrix: bfloat16 [1024, 128], P('fsdp', 'tensor'), may hold values from -0.1875 to 0.1875
- value_matrix: bfloat16 [1024, 128], P('fsdp', 'tensor'), may hold values from -0.1875 to 0.1875
- mamba_gate_weight: bfloat16 [1024, 1536], P('fsdp', 'tensor'), may hold values from -0.1875 to 0.1875
- mamba_input_weight: bfloat16 [1024, 1536], P('fsdp', 'tensor'), may hold values from -0.1875 to 0.1875
- w_bproj: bfloat16 [1024, 128], P('fsdp'), may hold values from -0.09375 to 0.09375
- w_cproj: bfloat16 [1024, 128], P('fsdp'), may hold values from -0.09375 to 0.09375
- w_dt: bfloat16 [1024, 24], P('fsdp', 'tensor'), may hold values from -0.1875 to 0.1875
- a_log: float32 [24], P('tensor'), may hold values from -6 to 0
- dt_bias: float32 [24], P('tensor'), may hold values from -5 to -1
- d_skip: float32 [24], P('tensor'), may hold values from 0.5 to 1.5
- w_attn_out: bfloat16 [512, 1024], P('tensor', 'fsdp'), may hold values from -0.25 to 0.25
- w_mixer_out: bfloat16 [1536, 1024], P('tensor', 'fsdp'), may hold values from -0.15625 to 0.15625
- ffn_gain: bfloat16 [1024], P('fsdp'), may hold values from 0.5 to 1.5
- w_gate: bfloat16 [1024, 2048], P('fsdp', 'tensor'), may hold values from -0.1875 to 0.1875
- w_up: bfloat16 [1024, 2048], P('fsdp', 'tensor'), may hold values from -0.1875 to 0.1875
- w_down: bfloat16 [2048, 1024], P('tensor', 'fsdp'), may hold values from -0.25 to 0.25
Outputs:
- layer_out: bfloat16 [2, 4, 2048, 1024], P(None, 'fsdp', 'context')
- grad_tokens: float32 [2, 4, 2048, 1024], P(None, 'fsdp', 'context')
- grad_mixer_gain: float32 [1024], P('fsdp')
- grad_query: float32 [1024, 512], P('fsdp', 'tensor')
- grad_key: float32 [1024, 128], P('fsdp', 'tensor')
- grad_value: float32 [1024, 128], P('fsdp', 'tensor')
- grad_z: float32 [1024, 1536], P('fsdp', 'tensor')
- grad_xin: float32 [1024, 1536], P('fsdp', 'tensor')
- grad_bproj: float32 [1024, 128], P('fsdp')
- grad_cproj: float32 [1024, 128], P('fsdp')
- grad_dt: float32 [1024, 24], P('fsdp', 'tensor')
- grad_a_log: float32 [24], P('tensor')
- grad_dt_bias: float32 [24], P('tensor')
- grad_d_skip: float32 [24], P('tensor')
- grad_attn_out: float32 [512, 1024], P('tensor', 'fsdp')
- grad_mixer_out: float32 [1536, 1024], P('tensor', 'fsdp')
- grad_ffn_gain: float32 [1024], P('fsdp')
- grad_gate: float32 [1024, 2048], P('fsdp', 'tensor')
- grad_up: float32 [1024, 2048], P('fsdp', 'tensor')
- grad_down: float32 [2048, 1024], P('tensor', 'fsdp')
The draws below stay inside these ranges and needn't reach their ends.
Inputs may be any that keep to these rules, and one draw needn't show every extreme that they name: `doc_lengths`: the 4 lengths of a sequence sum to 2048.
All inputs are finite; a program needn't handle non-finite values.
Results may differ from the reference program's by a relative error of at most 0.019.
Values may be sent and summed in bfloat16 or wider, within the bound.
No kernel may reach another device: no remote copies, remote signals or barrier semaphores. Data moves between devices by JAX's collectives and lax.ppermute only.
A program may use at most 160 MiB of HBM per device.

```python
from functools import partial
import jax
import jax.numpy as jnp
from jax import lax

MODEL_WIDTH = 1024
QUERY_HEADS = 8
KEY_VALUE_HEADS = 2
HEAD_WIDTH = 64
MAMBA_HEADS = 24
MAMBA_HEAD_SIZE = 64
NSTATE = 128
FF = 2048
DSSM = 1536
SEQUENCE_LENGTH = 2048
NDOC = 4
MICRO = 2
SEQ_MB = 4
SEQ_DEV = 512


def draw_doc_lengths(key, part):
    grid_shape = (MICRO, SEQ_MB)
    sub_keys = jax.random.split(jax.random.fold_in(key, 17), 4)
    first_doc = jax.random.randint(sub_keys[0], grid_shape, 1, SEQ_DEV)
    third_doc = jax.random.randint(sub_keys[1], grid_shape, 1, SEQ_DEV // 2 + 1)
    last_doc = jax.random.randint(sub_keys[2], grid_shape, 1, SEQ_DEV // 2)
    chosen = jax.random.randint(sub_keys[3], (), 0, MICRO * SEQ_MB)
    picked = jnp.arange(MICRO * SEQ_MB).reshape(grid_shape) == chosen
    first_doc = jnp.where(picked, 1, first_doc)
    third_doc = jnp.where(picked, 1, third_doc)
    last_doc = jnp.where(picked, 1, last_doc)
    long_doc = SEQUENCE_LENGTH - first_doc - third_doc - last_doc
    return jnp.stack([first_doc, long_doc, third_doc, last_doc], axis=-1).astype(jnp.int32)


def level_of(key, shape, cuts, smallest, high):
    def one(position, parts):
        heights = jax.random.uniform(jax.random.fold_in(jax.random.fold_in(key, 6), position), (parts,), jnp.float32, smallest / len(cuts), high / len(cuts))
        return jnp.repeat(jnp.exp(heights), shape[position] // parts).reshape((-1,) + (1,) * (len(shape) - position - 1))

    gain = one(*cuts[0])
    for cut in cuts[1:]:
        gain = gain * one(*cut)
    return gain


def normal_values(own_key, shape, scale, reach, cuts=(), kind=jnp.bfloat16):
    gain = level_of(own_key, shape, cuts, -0.22, 0.18) if cuts else 1.0
    drawn = jax.random.normal(own_key, shape, jnp.float32) * scale * gain
    return jnp.minimum(jnp.maximum(drawn, -reach), reach).astype(kind)


def setup_inputs(seed: int = 0) -> dict:
    splits = jax.random.split(jax.random.key(seed), 22)
    tokens = normal_values(splits[0], (MICRO, SEQ_MB, SEQUENCE_LENGTH, MODEL_WIDTH), 1.0, 6.0, ((1, 4), (2, 4)))
    cotangent = normal_values(splits[1], (MICRO, SEQ_MB, SEQUENCE_LENGTH, MODEL_WIDTH), 1.0, 6.0, ((1, 4), (2, 4)))
    doc_lengths = draw_doc_lengths(jax.random.fold_in(splits[21], 71), 0)
    mixer_gain = jnp.clip(1.0 + 0.1 * jax.random.normal(splits[3], (MODEL_WIDTH,), jnp.float32), 0.5, 1.5).astype(jnp.bfloat16)
    w_query = normal_values(splits[4], (MODEL_WIDTH, QUERY_HEADS * HEAD_WIDTH), MODEL_WIDTH ** -0.5, 0.1875, ((0, 4), (1, 2)))
    key_matrix = normal_values(splits[5], (MODEL_WIDTH, KEY_VALUE_HEADS * HEAD_WIDTH), MODEL_WIDTH ** -0.5, 0.1875, ((0, 4), (1, 2)))
    value_matrix = normal_values(splits[6], (MODEL_WIDTH, KEY_VALUE_HEADS * HEAD_WIDTH), MODEL_WIDTH ** -0.5, 0.1875, ((0, 4), (1, 2)))
    mamba_gate_weight = normal_values(splits[7], (MODEL_WIDTH, DSSM), MODEL_WIDTH ** -0.5, 0.1875, ((0, 4), (1, 2)))
    mamba_input_weight = normal_values(splits[8], (MODEL_WIDTH, DSSM), MODEL_WIDTH ** -0.5, 0.1875, ((0, 4), (1, 2)))
    w_bproj = normal_values(splits[9], (MODEL_WIDTH, NSTATE), (4 * MODEL_WIDTH) ** -0.5, 0.09375, ((0, 4),))
    w_cproj = normal_values(splits[10], (MODEL_WIDTH, NSTATE), (4 * MODEL_WIDTH) ** -0.5, 0.09375, ((0, 4),))
    w_dt = normal_values(splits[11], (MODEL_WIDTH, MAMBA_HEADS), MODEL_WIDTH ** -0.5, 0.1875, ((0, 4), (1, 2)))
    a_log = jnp.clip(-6.0 + 6.0 * jax.random.uniform(splits[12], (MAMBA_HEADS,), jnp.float32) ** level_of(splits[12], (MAMBA_HEADS,), ((0, 2),), -0.2, 0.2), -6.0, 0.0)
    dt_bias = jnp.clip(-5.0 + 4.0 * jax.random.uniform(splits[13], (MAMBA_HEADS,), jnp.float32) ** level_of(splits[13], (MAMBA_HEADS,), ((0, 2),), -0.2, 0.2), -5.0, -1.0)
    d_skip = jnp.clip(0.5 + 1.0 * jax.random.uniform(splits[14], (MAMBA_HEADS,), jnp.float32) ** level_of(splits[14], (MAMBA_HEADS,), ((0, 2),), -0.2, 0.2), 0.5, 1.5)
    w_attn_out = normal_values(splits[15], (QUERY_HEADS * HEAD_WIDTH, MODEL_WIDTH), (QUERY_HEADS * HEAD_WIDTH) ** -0.5, 0.25, ((0, 2), (1, 4)))
    w_mixer_out = normal_values(splits[16], (DSSM, MODEL_WIDTH), DSSM ** -0.5, 0.15625, ((0, 2), (1, 4)))
    ffn_gain = jnp.clip(1.0 + 0.1 * jax.random.normal(splits[17], (MODEL_WIDTH,), jnp.float32), 0.5, 1.5).astype(jnp.bfloat16)
    w_gate = normal_values(splits[18], (MODEL_WIDTH, FF), MODEL_WIDTH ** -0.5, 0.1875, ((0, 4), (1, 2)))
    w_up = normal_values(splits[19], (MODEL_WIDTH, FF), MODEL_WIDTH ** -0.5, 0.1875, ((0, 4), (1, 2)))
    w_down = normal_values(splits[20], (FF, MODEL_WIDTH), (FF // 4) ** -0.5, 0.25, ((0, 2), (1, 4)))
    return dict(tokens=tokens, cotangent=cotangent, doc_lengths=doc_lengths, mixer_gain=mixer_gain, w_query=w_query, key_matrix=key_matrix, value_matrix=value_matrix, mamba_gate_weight=mamba_gate_weight, mamba_input_weight=mamba_input_weight, w_bproj=w_bproj, w_cproj=w_cproj, w_dt=w_dt, a_log=a_log, dt_bias=dt_bias, d_skip=d_skip, w_attn_out=w_attn_out, w_mixer_out=w_mixer_out, ffn_gain=ffn_gain, w_gate=w_gate, w_up=w_up, w_down=w_down)


EPSILON = 1e-06
PRECISE = lax.Precision.HIGHEST

@jax.custom_vjp
def precision_cast(v):
    return lax.optimization_barrier(v.astype(jnp.bfloat16)).astype(jnp.float32)

@jax.custom_vjp
def precision_cast_grad(v):
    return v

def low_keep(v):
    return (precision_cast(v), None)

def low_pass(kept, grad):
    return (grad,)

def back_keep(v):
    return (v, None)

def back_low(kept, grad):
    return (precision_cast(grad),)
precision_cast.defvjp(low_keep, low_pass)
precision_cast_grad.defvjp(back_keep, back_low)

def rms_norm(hidden, gain_vec):
    inv_scale = lax.rsqrt(lax.optimization_barrier(jnp.mean(hidden * hidden, axis=-1, keepdims=True)) + EPSILON)
    return hidden * inv_scale * gain_vec

def apply_projection(left, right):
    return jnp.dot(left, right, precision=PRECISE)

def one_sequence(params, inputs, doc_lens):
    mixer_gain, w_query, key_matrix, value_matrix, mamba_gate_weight, mamba_input_weight, w_bproj, w_cproj, w_dt, a_log, dt_bias, d_skip, w_attn_out, w_mixer_out, ffn_gain, w_gate, w_up, w_down = params
    positions = jnp.arange(SEQUENCE_LENGTH)
    doc_ends = jnp.cumsum(doc_lens)
    segment = lax.optimization_barrier(jnp.sum((doc_ends[None, :] <= positions[:, None]).astype(jnp.int32), axis=1))
    allowed = (positions[None, :] <= positions[:, None]) & (segment[None, :] == segment[:, None])
    first_normed_input = precision_cast(rms_norm(inputs, mixer_gain))
    queries = precision_cast(precision_cast_grad(apply_projection(first_normed_input, w_query))).reshape(SEQUENCE_LENGTH, QUERY_HEADS, HEAD_WIDTH)
    projected_keys = precision_cast(precision_cast_grad(apply_projection(first_normed_input, key_matrix))).reshape(SEQUENCE_LENGTH, KEY_VALUE_HEADS, HEAD_WIDTH)
    projected_values = precision_cast(precision_cast_grad(apply_projection(first_normed_input, value_matrix))).reshape(SEQUENCE_LENGTH, KEY_VALUE_HEADS, HEAD_WIDTH)
    projected_keys = jnp.repeat(projected_keys, QUERY_HEADS // KEY_VALUE_HEADS, axis=1)
    projected_values = jnp.repeat(projected_values, QUERY_HEADS // KEY_VALUE_HEADS, axis=1)

    def head_attention(head_args):
        head_q, head_k, head_v = head_args
        scores = precision_cast_grad(apply_projection(head_q, head_k.T) * 0.125)
        masked = jnp.where(allowed, scores, -1e+30)
        row_max = lax.optimization_barrier(jnp.max(masked, axis=-1, keepdims=True))
        exp_scores = jnp.exp(masked - row_max)
        attn_prob = precision_cast(exp_scores / lax.optimization_barrier(jnp.sum(exp_scores, axis=-1, keepdims=True)))
        return apply_projection(attn_prob, head_v)
    per_head = lax.map(jax.checkpoint(head_attention), (jnp.swapaxes(queries, 0, 1), jnp.swapaxes(projected_keys, 0, 1), jnp.swapaxes(projected_values, 0, 1)))
    attended = precision_cast(precision_cast_grad(jnp.swapaxes(per_head, 0, 1).reshape(SEQUENCE_LENGTH, QUERY_HEADS * HEAD_WIDTH)))
    mamba_gate_rows = precision_cast_grad(apply_projection(first_normed_input, mamba_gate_weight)).reshape(SEQUENCE_LENGTH, MAMBA_HEADS, MAMBA_HEAD_SIZE)
    mamba_input_rows = precision_cast_grad(apply_projection(first_normed_input, mamba_input_weight)).reshape(SEQUENCE_LENGTH, MAMBA_HEADS, MAMBA_HEAD_SIZE)
    b_state = precision_cast_grad(apply_projection(first_normed_input, w_bproj))
    c_state = precision_cast_grad(apply_projection(first_normed_input, w_cproj))
    step_size = jax.nn.softplus(precision_cast_grad(apply_projection(first_normed_input, w_dt)) + dt_bias)
    inner_prod = apply_projection(c_state, b_state.T)

    def one_head(head_args):
        head_in, head_step, head_rate = head_args
        log_decay = jnp.cumsum(-head_rate * head_step)
        log_gap = jnp.where(allowed, log_decay[:, None] - log_decay[None, :], -10000.0)
        kernel = jnp.exp(log_gap) * inner_prod * head_step[None, :]
        return apply_projection(kernel, head_in)
    ssm_core = lax.map(jax.checkpoint(one_head), (jnp.swapaxes(mamba_input_rows, 0, 1), step_size.T, jnp.exp(a_log)))
    ssm_out = jnp.swapaxes(ssm_core, 0, 1) + d_skip[:, None] * mamba_input_rows
    gated = precision_cast((ssm_out * jax.nn.silu(mamba_gate_rows)).reshape(SEQUENCE_LENGTH, DSSM))
    mixed = precision_cast_grad(apply_projection(attended, w_attn_out) + apply_projection(gated, w_mixer_out))
    hidden_one = inputs + mixed
    normed_two = precision_cast(rms_norm(hidden_one, ffn_gain))
    gate_pre = precision_cast_grad(apply_projection(normed_two, w_gate))
    up_pre = precision_cast_grad(apply_projection(normed_two, w_up))
    activated = precision_cast(jax.nn.silu(gate_pre) * up_pre)
    return hidden_one + apply_projection(activated, w_down)

def reference(tokens, cotangent, doc_lengths, mixer_gain, w_query, key_matrix, value_matrix, mamba_gate_weight, mamba_input_weight, w_bproj, w_cproj, w_dt, a_log, dt_bias, d_skip, w_attn_out, w_mixer_out, ffn_gain, w_gate, w_up, w_down):
    params = tuple((weight.astype(jnp.float32) for weight in (mixer_gain, w_query, key_matrix, value_matrix, mamba_gate_weight, mamba_input_weight, w_bproj, w_cproj, w_dt, a_log, dt_bias, d_skip, w_attn_out, w_mixer_out, ffn_gain, w_gate, w_up, w_down)))
    sequences = tokens.astype(jnp.float32).reshape(MICRO * SEQ_MB, SEQUENCE_LENGTH, MODEL_WIDTH)
    doc_table = doc_lengths.reshape(MICRO * SEQ_MB, NDOC)

    def forward(weights, layer_in):
        single = jax.checkpoint(partial(one_sequence, weights))

        def scan_step(scan_carry, seq_item):
            return (scan_carry, single(seq_item[0], seq_item[1]))
        return lax.scan(scan_step, None, (layer_in, doc_table))[1]
    results, pull_back = jax.vjp(forward, params, sequences)
    grad_params, grad_inputs = pull_back(cotangent.astype(jnp.float32).reshape(MICRO * SEQ_MB, SEQUENCE_LENGTH, MODEL_WIDTH))
    full_shape = tokens.shape
    return (results.reshape(full_shape).astype(jnp.bfloat16), grad_inputs.reshape(full_shape), grad_params[0], grad_params[1], grad_params[2], grad_params[3], grad_params[4], grad_params[5], grad_params[6], grad_params[7], grad_params[8], grad_params[9], grad_params[10], grad_params[11], grad_params[12], grad_params[13], grad_params[14], grad_params[15], grad_params[16], grad_params[17])
```

```python
import jax
import jax.numpy as jnp
from jax import lax
from jax.sharding import PartitionSpec as P

HEAD_WIDTH = 64
EPSILON = 1e-06
LOW = jnp.bfloat16
F32 = jnp.float32


def swap_context(x, bit):
    size = lax.axis_size("context")
    return lax.ppermute(x, "context", [(i, i ^ bit) for i in range(size)])


def from_next(x, axis, step=1):
    size = lax.axis_size(axis)
    return lax.ppermute(x, axis, [((i + step) % size, i) for i in range(size)])


def context_bits():
    size = lax.axis_size("context")
    return [1 << k for k in range(size.bit_length() - 1)]


def spread_context(x):
    held = [(0, x)]
    for bit in reversed(context_bits()):
        held = held + [(off ^ bit, swap_context(part, bit)) for off, part in held]
    return held


def gather_context(x):
    size, index = lax.axis_size("context"), lax.axis_index("context")
    out = jnp.zeros((size,) + x.shape, x.dtype)
    for off, part in spread_context(x):
        out = lax.dynamic_update_index_in_dim(out, part, index ^ off, 0)
    return out


def gather_rows(shard, stacked):
    nf, nc = lax.axis_size("fsdp"), lax.axis_size("context")
    fi, ci = lax.axis_index("fsdp"), lax.axis_index("context")
    rows, cols = shard.shape
    part = rows // nc
    full = jnp.zeros((nf, nc, part, cols), shard.dtype)
    full = lax.dynamic_update_slice(full, shard.reshape(1, nc, part, cols), (fi, 0, 0, 0))
    cur = lax.dynamic_slice(shard, (ci * part, 0), (part, cols))
    steps = []
    for k in range(1, nf):
        cur = from_next(cur, "fsdp")
        steps.append((k, cur))
    if stacked:
        pieces = spread_context(jnp.stack([cur for _, cur in steps]))
        pieces = [(k, off, arr[k - 1]) for off, arr in pieces for k, _ in steps]
    else:
        pieces = [(k, off, arr) for k, cur in steps for off, arr in spread_context(cur)]
    for k, off, arr in pieces:
        full = lax.dynamic_update_slice(full, arr[None, None], ((fi + k) % nf, ci ^ off, 0, 0))
    return full.reshape(nf * rows, cols)


def scatter_rows(grad):
    nf, nc = lax.axis_size("fsdp"), lax.axis_size("context")
    fi, ci = lax.axis_index("fsdp"), lax.axis_index("context")
    rows, cols = grad.shape
    part = rows // (nf * nc)
    acc = grad
    left = nc
    for bit in context_bits():
        left //= 2
        view = acc.reshape(nf, left, 2, part, cols)
        mine = (ci & bit) // bit
        away = lax.dynamic_index_in_dim(view, 1 - mine, 2, keepdims=False)
        keep = lax.dynamic_index_in_dim(view, mine, 2, keepdims=False)
        acc = (keep.astype(F32) + swap_context(away, bit).astype(F32)).astype(LOW)
    acc = acc.reshape(nf, part, cols)
    total = lax.dynamic_index_in_dim(acc, fi, 0, keepdims=False).astype(F32)
    for k in range(1, nf):
        away = lax.dynamic_index_in_dim(acc, (fi - k) % nf, 0, keepdims=False)
        total = total + from_next(away, "fsdp", k).astype(F32)
    done = gather_context(total.astype(LOW))
    return done.reshape(rows // nf, cols).astype(F32)


def all_sum(x):
    for bit in context_bits():
        x = x + swap_context(x, bit)
    size, bit = lax.axis_size("fsdp"), 1
    while bit < size:
        x = x + lax.ppermute(x, "fsdp", [(i, i ^ bit) for i in range(size)])
        bit *= 2
    return x


def tensor_sum(x):
    low = x.astype(LOW)
    size = lax.axis_size("tensor")
    other = lax.ppermute(low, "tensor", [(i, (i + 1) % size) for i in range(size)])
    return low.astype(F32) + other.astype(F32)


def mat_mul(left, right):
    return jnp.dot(left, right, preferred_element_type=F32)


def mat_mul_t(left, right):
    return lax.dot_general(left, right, (((1,), (1,)), ((), ())), preferred_element_type=F32)


def outer_sum(left, right):
    return lax.dot_general(left, right, (((0,), (0,)), ((), ())), preferred_element_type=F32)


def norm_forward(hidden, gain_vec):
    inv_scale = lax.rsqrt(jnp.mean(hidden * hidden, axis=-1, keepdims=True) + EPSILON)
    return inv_scale, (hidden * inv_scale * gain_vec).astype(LOW)


def norm_backward(hidden, inv_scale, gain_vec, d_normed):
    weighted = gain_vec * d_normed
    return inv_scale * weighted - hidden * inv_scale**3 * jnp.mean(
        weighted * hidden, axis=-1, keepdims=True
    )


def segment_ids(doc_lens, positions):
    count = doc_lens.shape[-1]
    upto = jnp.arange(count)[:, None] >= jnp.arange(count)[None, :]
    ends = jnp.sum(jnp.where(upto, doc_lens[:, None, :], 0), axis=-1)
    return jnp.sum((ends[:, None, :] <= positions[None, :, None]).astype(jnp.int32), axis=2)


def decay_terms(raw_step, a_log, dt_bias):
    step_size = jax.nn.softplus(raw_step + dt_bias)
    log_rate = -jnp.exp(a_log) * step_size
    block_len = raw_step.shape[0]
    lower = (jnp.arange(block_len)[:, None] >= jnp.arange(block_len)[None, :]).astype(F32)
    log_decay = jnp.einsum("tu,uh->ht", lower, log_rate, precision=lax.Precision.HIGHEST)
    return step_size.T, log_decay


def mixer_values(x_in, b_in, c_in, step_in, z_in, log_a, bias_in, skip_in, state_in, inside, carried):
    step_size, log_decay = decay_terms(step_in, log_a, bias_in)
    log_gap = jnp.where(inside[None], log_decay[:, :, None] - log_decay[:, None, :], -10000.0)
    inner = jnp.einsum("tn,un->tu", c_in, b_in)
    kernel = jnp.exp(log_gap) * inner[None] * step_size[:, None, :]
    result = jnp.einsum("htu,uhp->thp", kernel, x_in)
    entering = jnp.where(carried[None, :], jnp.exp(log_decay), 0.0)
    state_read = jnp.einsum("tn,hpn->thp", c_in, state_in)
    result = result + state_read * entering.T[..., None] + skip_in[:, None] * x_in
    return result * jax.nn.silu(z_in)


def mixer_state(x_in, b_in, step_in, log_a, bias_in, closing, carried_last):
    step_size, log_decay = decay_terms(step_in, log_a, bias_in)
    final_log = log_decay[:, -1:]
    weights = jnp.where(closing[None, :], jnp.exp(final_log - log_decay), 0.0) * step_size
    span_state = jnp.einsum("ht,thp,tn->hpn", weights, x_in, b_in)
    passing = jnp.where(carried_last, jnp.exp(final_log[:, 0]), 0.0)
    return passing, span_state


def masked_scores(queries, keys, allowed):
    scores = jnp.einsum("tgqd,jgd->gqtj", queries, keys, preferred_element_type=F32) * 0.125
    return jnp.where(allowed[None, None], scores, -1e30)


def per_device(
    tokens, cotangent, doc_lengths, mixer_gain, w_query, key_matrix, value_matrix, mamba_gate_weight,
    mamba_input_weight, w_bproj, w_cproj, w_dt, a_log, dt_bias, d_skip, w_attn_out, w_mixer_out,
    ffn_gain, w_gate, w_up, w_down,
):
    micro_count, seq_count, block_len, model_dim = tokens.shape
    rows_here = mixer_gain.shape[0]
    heads = w_dt.shape[1]
    ssm_dim = mamba_gate_weight.shape[1]
    head_dim = ssm_dim // heads
    q_dim = w_query.shape[1]
    kv_dim = key_matrix.shape[1]
    kv_heads = kv_dim // HEAD_WIDTH
    q_group = q_dim // kv_dim
    state_dim = w_bproj.shape[1]
    ff_dim = w_gate.shape[1]
    ci = lax.axis_index("context")
    nc = lax.axis_size("context")
    full_len = nc * block_len
    units = [(m, s) for m in range(micro_count) for s in range(seq_count)]

    pad = -(heads + 2) % 128
    first = jnp.concatenate(
        [w_query, key_matrix, value_matrix, w_bproj, w_cproj, w_dt, mixer_gain[:, None], ffn_gain[:, None],
         jnp.zeros((rows_here, pad), LOW)], axis=1)
    second = jnp.concatenate([mamba_gate_weight, mamba_input_weight], axis=1)
    third = jnp.concatenate([w_attn_out.T, w_mixer_out.T], axis=1)
    fourth = jnp.concatenate([w_gate, w_up, w_down.T], axis=1)
    first = gather_rows(first, False)
    second = gather_rows(second, False)
    third = gather_rows(third, True)
    fourth = gather_rows(fourth, True)
    at_b = q_dim + 2 * kv_dim
    at_dt = at_b + 2 * state_dim
    gain_one = first[:, at_dt + heads].astype(F32)
    gain_two = first[:, at_dt + heads + 1].astype(F32)
    gate_up = fourth[:, : 2 * ff_dim]
    down_t = fourth[:, 2 * ff_dim :]

    saved = {}
    positions = jnp.arange(full_len)
    q_pos = ci * block_len + jnp.arange(block_len)
    tri = jnp.arange(block_len)[:, None] >= jnp.arange(block_len)[None, :]
    nothing = (jnp.ones((heads,), F32), jnp.zeros((heads, head_dim, state_dim), F32))

    for u in units:
        v = saved[u] = {}
        v["x"] = tokens[u].astype(F32)
        v["r1"], v["n1"] = norm_forward(v["x"], gain_one)
        p_one = mat_mul(v["n1"], first)
        v["q"] = p_one[:, :q_dim].astype(LOW)
        kv = p_one[:, q_dim:at_b].astype(LOW)
        v["b"] = p_one[:, at_b : at_b + state_dim]
        v["c"] = p_one[:, at_b + state_dim : at_dt]
        v["dr"] = p_one[:, at_dt : at_dt + heads]
        p_two = mat_mul(v["n1"], second)
        v["z"] = p_two[:, :ssm_dim].reshape(block_len, heads, head_dim)
        v["xs"] = p_two[:, ssm_dim:].reshape(block_len, heads, head_dim)
        kv_all = gather_context(kv).reshape(full_len, 2 * kv_dim)
        v["k_all"] = kv_all[:, :kv_dim].reshape(full_len, kv_heads, HEAD_WIDTH)
        v["v_all"] = kv_all[:, kv_dim:].reshape(full_len, kv_heads, HEAD_WIDTH)
        doc_lens = doc_lengths[u][None]
        seg_all = segment_ids(doc_lens, positions)[0]
        seg_here = lax.dynamic_slice_in_dim(seg_all, ci * block_len, block_len, 0)
        seg_prev = segment_ids(doc_lens, jnp.reshape(ci * block_len - 1, (1,)))[0]
        v["allowed"] = (positions[None, :] <= q_pos[:, None]) & (seg_all[None, :] == seg_here[:, None])
        v["inside"] = tri & (seg_here[:, None] == seg_here[None, :])
        v["carried"] = seg_here == seg_prev
        v["closing"] = seg_here == seg_here[-1:]
        v["passing"], v["span"] = mixer_state(
            v["xs"], v["b"], v["dr"], a_log, dt_bias, v["closing"], v["carried"][-1])
        passes = gather_context(v["passing"])
        spans = gather_context(v["span"].astype(LOW))
        v["passes"] = passes
        state = nothing[1]
        for k in range(nc - 1):
            new = passes[k][:, None, None] * state + spans[k].astype(F32)
            state = jnp.where(k < ci, new, state)
        v["state"] = state
    for u in units:
        v = saved[u]
        scores = masked_scores(v["q"].reshape(block_len, kv_heads, q_group, HEAD_WIDTH), v["k_all"], v["allowed"])
        row_max = jnp.max(scores, axis=-1, keepdims=True)
        v["lse"] = row_max + jnp.log(jnp.sum(jnp.exp(scores - row_max), axis=-1, keepdims=True))
        prob = jnp.exp(scores - v["lse"]).astype(LOW)
        v["o"] = jnp.einsum("gqtj,jgd->tgqd", prob, v["v_all"], preferred_element_type=F32).astype(LOW).reshape(block_len, q_dim)
        gated = mixer_values(v["xs"], v["b"], v["c"], v["dr"], v["z"], a_log, dt_bias, d_skip, v["state"], v["inside"], v["carried"])
        v["og"] = jnp.concatenate([v["o"], gated.reshape(block_len, ssm_dim).astype(LOW)], axis=1)
        v["m"] = tensor_sum(mat_mul_t(v["og"], third))

    layer_outs = []
    for u in units:
        v = saved[u]
        v["h1"] = v["x"] + v["m"]
        v["r2"], v["n2"] = norm_forward(v["h1"], gain_two)
        ab = mat_mul(v["n2"], gate_up)
        a, b = ab[:, :ff_dim], ab[:, ff_dim:]
        sig = jax.nn.sigmoid(a)
        v["f"] = (a * sig * b).astype(LOW)
        out = tensor_sum(mat_mul_t(v["f"], down_t))
        layer_outs.append((v["h1"] + out).astype(LOW))
        v["dy"] = cotangent[u]
        df = mat_mul(v["dy"], down_t)
        v["dab"] = jnp.concatenate(
            [(df * b * sig * (1.0 + a * (1.0 - sig))).astype(LOW), (df * a * sig).astype(LOW)], axis=1)
        v["dn2"] = tensor_sum(mat_mul_t(v["dab"], gate_up))
    g_gate_up = sum(outer_sum(saved[u]["n2"], saved[u]["dab"]) for u in units).astype(LOW)
    g_down = sum(outer_sum(saved[u]["dy"], saved[u]["f"]) for u in units).astype(LOW)
    g_fourth = scatter_rows(jnp.concatenate([g_gate_up, g_down], axis=1))

    g_gain_two = 0.0
    for u in units:
        v = saved[u]
        d_hidden = norm_backward(v["h1"], v["r2"], gain_two, v["dn2"]) + v["dy"].astype(F32)
        g_gain_two = g_gain_two + jnp.sum(v["dn2"] * v["h1"] * v["r2"], axis=0)
        v["dh"] = d_hidden
        v["dm"] = d_hidden.astype(LOW)
        v["dog"] = mat_mul(v["dm"], third)
    g_third = scatter_rows(sum(outer_sum(saved[u]["dm"], saved[u]["og"]) for u in units).astype(LOW))
    head_grads = 0.0
    for u in units:
        v = saved[u]
        d_att = v["dog"][:, :q_dim].astype(LOW).reshape(block_len, kv_heads, q_group, HEAD_WIDTH)
        d_gated = v["dog"][:, q_dim:].reshape(block_len, heads, head_dim)

        def values_of(x_in, b_in, c_in, step_in, z_in, log_a, bias_in, skip_in, state_in):
            return mixer_values(x_in, b_in, c_in, step_in, z_in, log_a, bias_in, skip_in, state_in, v["inside"], v["carried"])

        pull = jax.vjp(values_of, v["xs"], v["b"], v["c"], v["dr"], v["z"], a_log, dt_bias, d_skip, v["state"])[1]
        gx1, gb1, gc1, gdr1, gz, ga1, gbias1, gskip, local = pull(d_gated)
        locals_ = gather_context(local.astype(LOW))
        later = nothing[1]
        for k in range(nc - 1, 0, -1):
            new = v["passes"][k][:, None, None] * later + locals_[k].astype(F32)
            later = jnp.where(k > ci, new, later)
        d_pass = jnp.sum(later * v["state"], axis=(1, 2))

        def state_of(x_in, b_in, step_in, log_a, bias_in):
            return mixer_state(x_in, b_in, step_in, log_a, bias_in, v["closing"], v["carried"][-1])

        gx2, gb2, gdr2, ga2, gbias2 = jax.vjp(state_of, v["xs"], v["b"], v["dr"], a_log, dt_bias)[1]((d_pass, later))
        head_grads = head_grads + jnp.stack([ga1 + ga2, gbias1 + gbias2, gskip])
        v["dzx"] = jnp.concatenate([gz.reshape(block_len, ssm_dim), (gx1 + gx2).reshape(block_len, ssm_dim)], axis=1).astype(LOW)
        v["ddr"] = (gdr1 + gdr2).astype(LOW)
        v["dbc"] = tensor_sum(jnp.concatenate([gb1 + gb2, gc1], axis=1)).astype(LOW)
        v["dbc_part"] = jnp.concatenate([gb1 + gb2, gc1], axis=1).astype(LOW)

        q4 = v["q"].reshape(block_len, kv_heads, q_group, HEAD_WIDTH)
        prob = jnp.exp(masked_scores(q4, v["k_all"], v["allowed"]) - v["lse"])
        d_prob = jnp.einsum("tgqd,jgd->gqtj", d_att, v["v_all"], preferred_element_type=F32)
        d_values = jnp.einsum("gqtj,tgqd->jgd", prob.astype(LOW), d_att, preferred_element_type=F32)
        d_scores = (prob * (d_prob - jnp.sum(prob * d_prob, axis=-1, keepdims=True))).astype(LOW)
        dq = jnp.einsum("gqtj,jgd->tgqd", d_scores, v["k_all"], preferred_element_type=F32) * 0.125
        d_keys = jnp.einsum("gqtj,tgqd->jgd", d_scores, q4, preferred_element_type=F32) * 0.125
        v["dq"] = dq.astype(LOW).reshape(block_len, q_dim)
        part = jnp.concatenate([d_keys.reshape(full_len, kv_dim), d_values.reshape(full_len, kv_dim)], axis=1)
        part = part.astype(LOW).reshape(nc, block_len, 2 * kv_dim)
        left = nc
        for bit in context_bits():
            left //= 2
            view = part.reshape(left, 2, block_len, 2 * kv_dim)
            mine = (ci & bit) // bit
            away = lax.dynamic_index_in_dim(view, 1 - mine, 1, keepdims=False)
            keep = lax.dynamic_index_in_dim(view, mine, 1, keepdims=False)
            part = (keep.astype(F32) + swap_context(away, bit).astype(F32)).astype(LOW)
        v["dkv"] = part.reshape(block_len, 2 * kv_dim)
        zeros = jnp.zeros((block_len, pad + 2), LOW)
        v["d_first"] = jnp.concatenate([v["dq"], v["dkv"], v["dbc"], v["ddr"], zeros], axis=1)
        v["d_first_part"] = jnp.concatenate([v["dq"], v["dkv"], v["dbc_part"], v["ddr"], zeros], axis=1)
    g_second = scatter_rows(sum(outer_sum(saved[u]["n1"], saved[u]["dzx"]) for u in units).astype(LOW))
    input_grads = []
    g_gain_one = 0.0
    for u in units:
        v = saved[u]
        dn1 = tensor_sum(mat_mul_t(v["d_first_part"], first) + mat_mul_t(v["dzx"], second))
        g_gain_one = g_gain_one + jnp.sum(dn1 * v["x"] * v["r1"], axis=0)
        input_grads.append(v["dh"] + norm_backward(v["x"], v["r1"], gain_one, dn1))
    g_first = sum(outer_sum(saved[u]["n1"], saved[u]["d_first"]) for u in units)
    at_gain = at_dt + heads
    g_first = jnp.concatenate(
        [g_first[:, :at_gain], g_gain_one[:, None], g_gain_two[:, None], g_first[:, at_gain + 2 :]], axis=1)
    g_first = scatter_rows(g_first.astype(LOW))
    head_grads = all_sum(head_grads)

    shape = (micro_count, seq_count, block_len, model_dim)
    at_k, at_v = q_dim, q_dim + kv_dim
    return (
        jnp.stack(layer_outs).reshape(shape),
        jnp.stack(input_grads).reshape(shape),
        g_first[:, at_gain],
        g_first[:, :at_k],
        g_first[:, at_k:at_v],
        g_first[:, at_v:at_b],
        g_second[:, :ssm_dim],
        g_second[:, ssm_dim:],
        g_first[:, at_b : at_b + state_dim],
        g_first[:, at_b + state_dim : at_dt],
        g_first[:, at_dt:at_gain],
        head_grads[0],
        head_grads[1],
        head_grads[2],
        g_third[:, :q_dim].T,
        g_third[:, q_dim:].T,
        g_first[:, at_gain + 1],
        g_fourth[:, :ff_dim],
        g_fourth[:, ff_dim : 2 * ff_dim],
        g_fourth[:, 2 * ff_dim :].T,
    )


def solution(mesh):
    rows, cols = P("fsdp", "tensor"), P("tensor", "fsdp")
    acts = P(None, "fsdp", "context", None)
    return jax.shard_map(
        per_device,
        mesh=mesh,
        in_specs=(
            acts, acts, P(None, "fsdp", None), P("fsdp"), rows, rows, rows, rows, rows, P("fsdp", None),
            P("fsdp", None), rows, P("tensor"), P("tensor"), P("tensor"), cols, cols, P("fsdp"), rows, rows, cols,
        ),
        out_specs=(
            acts, acts, P("fsdp"), rows, rows, rows, rows, rows, P("fsdp", None), P("fsdp", None), rows,
            P("tensor"), P("tensor"), P("tensor"), cols, cols, P("fsdp"), rows, rows, cols,
        ),
        check_vma=False,
    )
```

```python
import jax
import jax.numpy as jnp
from jax import lax
from jax.experimental import pallas as pl
from jax.experimental.pallas import tpu as pltpu
from jax.sharding import PartitionSpec as P

HEAD_WIDTH = 64
EPSILON = 1e-06
LOW = jnp.bfloat16
F32 = jnp.float32
NEGATIVE = -1e30
PRECISE = lax.Precision.HIGHEST


def swap_context(x, bit):
    size = lax.axis_size("context")
    return lax.ppermute(x, "context", [(i, i ^ bit) for i in range(size)])


def from_next(x, axis, step=1):
    size = lax.axis_size(axis)
    return lax.ppermute(x, axis, [((i + step) % size, i) for i in range(size)])


def context_bits():
    size = lax.axis_size("context")
    return [1 << k for k in range(size.bit_length() - 1)]


def spread_context(x):
    held = [(0, x)]
    for bit in reversed(context_bits()):
        held = held + [(off ^ bit, swap_context(part, bit)) for off, part in held]
    return held


def gather_context(x):
    size, index = lax.axis_size("context"), lax.axis_index("context")
    out = jnp.zeros((size,) + x.shape, x.dtype)
    for off, part in spread_context(x):
        out = lax.dynamic_update_index_in_dim(out, part, index ^ off, 0)
    return out


def gather_rows(shard, stacked):
    nf, nc = lax.axis_size("fsdp"), lax.axis_size("context")
    fi, ci = lax.axis_index("fsdp"), lax.axis_index("context")
    rows, cols = shard.shape
    part = rows // nc
    full = jnp.zeros((nf, nc, part, cols), shard.dtype)
    full = lax.dynamic_update_slice(full, shard.reshape(1, nc, part, cols), (fi, 0, 0, 0))
    cur = lax.dynamic_slice(shard, (ci * part, 0), (part, cols))
    steps = []
    for k in range(1, nf):
        cur = from_next(cur, "fsdp")
        steps.append((k, cur))
    if stacked:
        pieces = spread_context(jnp.stack([cur for _, cur in steps]))
        pieces = [(k, off, arr[k - 1]) for off, arr in pieces for k, _ in steps]
    else:
        pieces = [(k, off, arr) for k, cur in steps for off, arr in spread_context(cur)]
    for k, off, arr in pieces:
        full = lax.dynamic_update_slice(full, arr[None, None], ((fi + k) % nf, ci ^ off, 0, 0))
    return full.reshape(nf * rows, cols)


def reduce_rows(grad):
    nf, nc = lax.axis_size("fsdp"), lax.axis_size("context")
    fi, ci = lax.axis_index("fsdp"), lax.axis_index("context")
    rows, cols = grad.shape
    part = rows // (nf * nc)
    acc = grad
    left = nc
    for bit in context_bits():
        left //= 2
        view = acc.reshape(nf, left, 2, part, cols)
        mine = (ci & bit) // bit
        away = lax.dynamic_index_in_dim(view, 1 - mine, 2, keepdims=False)
        keep = lax.dynamic_index_in_dim(view, mine, 2, keepdims=False)
        acc = (keep.astype(F32) + swap_context(away, bit).astype(F32)).astype(LOW)
    acc = acc.reshape(nf, part, cols)
    total = lax.dynamic_index_in_dim(acc, fi, 0, keepdims=False).astype(F32)
    for k in range(1, nf):
        away = lax.dynamic_index_in_dim(acc, (fi - k) % nf, 0, keepdims=False)
        total = total + from_next(away, "fsdp", k).astype(F32)
    return total


def share_rows(part):
    done = gather_context(part.astype(LOW))
    return done.reshape(-1, part.shape[1])


def scatter_rows(grad):
    return share_rows(reduce_rows(grad)).astype(F32)


def all_sum(x):
    for bit in context_bits():
        x = x + swap_context(x, bit)
    size, bit = lax.axis_size("fsdp"), 1
    while bit < size:
        x = x + lax.ppermute(x, "fsdp", [(i, i ^ bit) for i in range(size)])
        bit *= 2
    return x


def tensor_sum(x):
    low = x.astype(LOW)
    size = lax.axis_size("tensor")
    other = lax.ppermute(low, "tensor", [(i, (i + 1) % size) for i in range(size)])
    return low.astype(F32) + other.astype(F32)


def mat_mul(left, right):
    return jnp.dot(left, right, preferred_element_type=F32)


def mat_mul_t(left, right):
    return lax.dot_general(left, right, (((1,), (1,)), ((), ())), preferred_element_type=F32)


def outer_sum(left, right):
    return lax.dot_general(left, right, (((0,), (0,)), ((), ())), preferred_element_type=F32)


def norm_forward(hidden, gain_vec):
    inv_scale = lax.rsqrt(jnp.mean(hidden * hidden, axis=-1, keepdims=True) + EPSILON)
    return inv_scale, (hidden * inv_scale * gain_vec).astype(LOW)


def norm_backward(hidden, inv_scale, gain_vec, d_normed):
    weighted = gain_vec * d_normed
    return inv_scale * weighted - hidden * inv_scale**3 * jnp.mean(
        weighted * hidden, axis=-1, keepdims=True
    )


def segment_ids(doc_lens, positions):
    count = doc_lens.shape[-1]
    upto = jnp.arange(count)[:, None] >= jnp.arange(count)[None, :]
    ends = jnp.sum(jnp.where(upto, doc_lens[:, None, :], 0), axis=-1)
    return jnp.sum((ends[:, None, :] <= positions[None, :, None]).astype(jnp.int32), axis=2)


def kernel_params(limit=48):
    return pltpu.CompilerParams(vmem_limit_bytes=limit * 2**20)


def nt_dot(left, right):
    return lax.dot_general(left, right, (((1,), (1,)), ((), ())), preferred_element_type=F32)


def tn_dot(left, right):
    return lax.dot_general(left, right, (((0,), (0,)), ((), ())), preferred_element_type=F32)


def nn_dot(left, right):
    return jnp.dot(left, right, preferred_element_type=F32)


def attention_forward(q, kv_all, seg_here, seg_all, span):
    rows, q_dim = q.shape
    heads = q_dim // HEAD_WIDTH
    length = kv_all.shape[0]

    def body(span_ref, q_ref, kv_ref, seg_q_ref, seg_k_ref, o_ref, lse_ref, bias, top, low, acc):
        top[...] = jnp.full_like(top, NEGATIVE)
        low[...] = jnp.zeros_like(low)
        acc[...] = jnp.zeros_like(acc)
        own = span_ref[1]

        def step(i, carry):
            j = own - i
            at = pl.multiple_of(j * rows, rows)
            keys = kv_ref[pl.ds(at, rows), :HEAD_WIDTH]
            turned = kv_ref[pl.ds(at, rows), :].astype(F32).T[HEAD_WIDTH:].astype(LOW)
            u = lax.broadcasted_iota(jnp.int32, (rows, rows), 0)
            t = lax.broadcasted_iota(jnp.int32, (rows, rows), 1)
            seen = (seg_k_ref[pl.ds(at, rows), :] == seg_q_ref[...]) & ((u <= t) | (j < own))
            bias[...] = jnp.where(seen, 0.0, NEGATIVE)
            for h in range(heads):
                lanes = slice(h * HEAD_WIDTH, (h + 1) * HEAD_WIDTH)
                s = nt_dot(keys, q_ref[:, lanes]) + bias[...]
                before = top[h : h + 1, :]
                now = jnp.maximum(before, jnp.max(s, axis=0, keepdims=True))
                p = jnp.exp(s - now)
                scale = jnp.exp(before - now)
                top[h : h + 1, :] = now
                low[h : h + 1, :] = low[h : h + 1, :] * scale + jnp.sum(p, axis=0, keepdims=True)
                acc[lanes, :] = acc[lanes, :] * scale + nn_dot(turned, p.astype(LOW))
            return carry

        lax.fori_loop(0, own - span_ref[0] + 1, step, 0)
        for h in range(heads):
            lanes = slice(h * HEAD_WIDTH, (h + 1) * HEAD_WIDTH)
            acc[lanes, :] = acc[lanes, :] / low[h : h + 1, :]
        o_ref[...] = acc[...].T.astype(LOW)
        lse_ref[...] = top[...] + jnp.log(low[...])

    return pl.pallas_call(
        body,
        out_shape=(jax.ShapeDtypeStruct((rows, q_dim), LOW), jax.ShapeDtypeStruct((8, rows), F32)),
        in_specs=[pl.BlockSpec(memory_space=pltpu.SMEM)] + [pl.BlockSpec(memory_space=pltpu.VMEM)] * 4,
        out_specs=[pl.BlockSpec(memory_space=pltpu.VMEM)] * 2,
        scratch_shapes=[
            pltpu.VMEM((rows, rows), F32),
            pltpu.VMEM((8, rows), F32),
            pltpu.VMEM((8, rows), F32),
            pltpu.VMEM((q_dim, rows), F32),
        ],
        compiler_params=kernel_params(),
        cost_estimate=pl.CostEstimate(flops=16 * rows * length * q_dim, bytes_accessed=4 * rows * q_dim, transcendentals=heads * rows * length),
        name="attention_forward",
    )(span, q, kv_all, seg_here.reshape(1, rows), seg_all.reshape(length, 1))


def attention_backward(q, do, o, kv_all, lse, seg_here, seg_all, span):
    rows, q_dim = q.shape
    heads = q_dim // HEAD_WIDTH
    length = kv_all.shape[0]
    sub = min(256, rows)

    def body(span_ref, q_ref, do_ref, o_ref, kv_ref, lse_ref, seg_q_ref, seg_k_ref, dq_ref, dkv_ref, bias, dq_acc, dk_acc, dv_acc, delta):
        own = span_ref[1]
        dq_acc[...] = jnp.zeros_like(dq_acc)
        dkv_ref[...] = jnp.zeros_like(dkv_ref)
        both = do_ref[...].astype(F32) * o_ref[...].astype(F32)
        lane = lax.broadcasted_iota(jnp.int32, (rows, 128), 1)
        columns = jnp.zeros((rows, 128), F32)
        for h in range(heads):
            total = jnp.sum(both[:, h * HEAD_WIDTH : (h + 1) * HEAD_WIDTH], axis=1, keepdims=True)
            columns = jnp.where(lane == h, total, columns)
        delta[...] = columns.T[:8]

        def step(i, carry):
            j = own - i
            at = pl.multiple_of(j * rows, rows)
            same = seg_k_ref[pl.ds(at, rows), :] == seg_q_ref[...]
            u = lax.broadcasted_iota(jnp.int32, (rows, rows), 0)
            t = lax.broadcasted_iota(jnp.int32, (rows, rows), 1)
            seen = same & ((u <= t) | (j < own))
            bias[...] = jnp.where(seen, 0.0, NEGATIVE)
            for r in range(0, rows, sub):
                keys = kv_ref[pl.ds(pl.multiple_of(at + r, sub), sub), :HEAD_WIDTH]
                values = kv_ref[pl.ds(pl.multiple_of(at + r, sub), sub), HEAD_WIDTH:]
                dk = jnp.zeros((sub, HEAD_WIDTH), F32)
                dv = jnp.zeros((sub, HEAD_WIDTH), F32)
                for h in range(heads):
                    lanes = slice(h * HEAD_WIDTH, (h + 1) * HEAD_WIDTH)
                    q_h, do_h = q_ref[:, lanes], do_ref[:, lanes]
                    p = jnp.exp(nt_dot(keys, q_h) + (bias[r : r + sub, :] - lse_ref[h : h + 1, :]))
                    ds = (p * (nt_dot(values, do_h) - delta[h : h + 1, :])).astype(LOW)
                    dv = dv + nn_dot(p.astype(LOW), do_h)
                    dk = dk + nn_dot(ds, q_h)
                    dq_acc[:, lanes] = dq_acc[:, lanes] + tn_dot(ds, keys)
                dkv_ref[pl.ds(pl.multiple_of(at + r, sub), sub), :HEAD_WIDTH] = dk.astype(LOW)
                dkv_ref[pl.ds(pl.multiple_of(at + r, sub), sub), HEAD_WIDTH:] = dv.astype(LOW)
            return carry

        lax.fori_loop(0, own - span_ref[0] + 1, step, 0)
        dq_ref[...] = (dq_acc[...] * 0.125).astype(LOW)

    return pl.pallas_call(
        body,
        out_shape=(jax.ShapeDtypeStruct((rows, q_dim), LOW), jax.ShapeDtypeStruct((length, 2 * HEAD_WIDTH), LOW)),
        in_specs=[pl.BlockSpec(memory_space=pltpu.SMEM)] + [pl.BlockSpec(memory_space=pltpu.VMEM)] * 7,
        out_specs=[pl.BlockSpec(memory_space=pltpu.VMEM)] * 2,
        scratch_shapes=[
            pltpu.VMEM((rows, rows), F32),
            pltpu.VMEM((rows, q_dim), F32),
            pltpu.VMEM((rows, HEAD_WIDTH), F32),
            pltpu.VMEM((rows, HEAD_WIDTH), F32),
            pltpu.VMEM((8, rows), F32),
        ],
        compiler_params=kernel_params(),
        cost_estimate=pl.CostEstimate(flops=40 * rows * length * q_dim, bytes_accessed=4 * rows * q_dim, transcendentals=heads * rows * length),
        name="attention_backward",
    )(span, q, do, o, kv_all, lse, seg_here.reshape(1, rows), seg_all.reshape(length, 1))


def halves(columns, first, lane):
    return jnp.where(lane < 64, columns[:, first : first + 1], columns[:, first + 1 : first + 2])


def mamba_state(per_head, at, left, right, gate=None):
    rows, width = right.shape
    state = left.shape[1]
    pairs = width // 128
    gates = () if gate is None else (gate,)

    def body(head_ref, left_ref, right_ref, *rest):
        out_ref = rest[-1]
        lane = lax.broadcasted_iota(jnp.int32, (rows, 128), 1)
        turned = left_ref[...].astype(F32).T.astype(LOW)
        for i in range(pairs):
            lanes = slice(i * 128, (i + 1) * 128)
            value = right_ref[:, lanes].astype(F32)
            if gates:
                z = rest[0][:, lanes].astype(F32)
                value = value * z * jax.nn.sigmoid(z)
            weight = halves(head_ref[i].T, at, lane)
            out_ref[:, lanes] = nn_dot(turned, (value * weight).astype(LOW)).astype(LOW)

    return pl.pallas_call(
        body,
        out_shape=jax.ShapeDtypeStruct((state, width), LOW),
        in_specs=[pl.BlockSpec(memory_space=pltpu.VMEM)] * (3 + len(gates)),
        out_specs=pl.BlockSpec(memory_space=pltpu.VMEM),
        compiler_params=kernel_params(),
        cost_estimate=pl.CostEstimate(flops=2 * rows * width * state, bytes_accessed=4 * rows * width, transcendentals=0),
        name="mamba_state",
    )(per_head, left, right, *gates)


def pair_spec(rows):
    return pl.BlockSpec((rows, 128), lambda i: (0, i))


def whole_spec(shape):
    return pl.BlockSpec(shape, lambda i: (0,) * len(shape))


def mamba_forward(per_head, xs, z, b, c, state_in, skip, seg_col, seg_row):
    rows, width = xs.shape
    pairs = width // 128
    blk = min(256, rows)

    def body(head_ref, xs_ref, z_ref, b_ref, c_ref, state_ref, skip_ref, seg_col_ref, seg_row_ref, y_ref, g_ref, inner, x_dt):
        @pl.when(pl.program_id(0) == 0)
        def _():
            t = lax.broadcasted_iota(jnp.int32, (rows, rows), 0)
            u = lax.broadcasted_iota(jnp.int32, (rows, rows), 1)
            seen = (seg_col_ref[...] == seg_row_ref[...]) & (u <= t)
            inner[...] = jnp.where(seen, nt_dot(c_ref[...], b_ref[...]), 0.0)

        lane = lax.broadcasted_iota(jnp.int32, (rows, 128), 1)
        by_row = head_ref[0]
        by_col = by_row.T
        xs_f = xs_ref[...].astype(F32)
        x_dt[...] = (xs_f * halves(by_col, 2, lane)).astype(LOW)
        read = nn_dot(c_ref[...], state_ref[...]) * halves(by_col, 4, lane)
        for i in range(rows // blk):
            part = slice(i * blk, (i + 1) * blk)
            sums = []
            for h in range(2):
                total = None
                for j in range(i + 1):
                    other = slice(j * blk, (j + 1) * blk)
                    gap = by_col[part, h : h + 1] - by_row[h : h + 1, other]
                    kernel = jnp.exp(jnp.minimum(gap, 0.0)) * inner[part, other]
                    term = nn_dot(kernel.astype(LOW), x_dt[other, :])
                    total = term if total is None else total + term
                sums.append(total)
            y = jnp.where(lane[part] < 64, sums[0], sums[1]) + read[part]
            y_ref[part, :] = y
            z_f = z_ref[part, :].astype(F32)
            g_ref[part, :] = ((y + skip_ref[...] * xs_f[part]) * z_f * jax.nn.sigmoid(z_f)).astype(LOW)

    state = b.shape[1]
    return pl.pallas_call(
        body,
        grid=(pairs,),
        out_shape=(jax.ShapeDtypeStruct((rows, width), F32), jax.ShapeDtypeStruct((rows, width), LOW)),
        in_specs=[
            pl.BlockSpec((1, 8, rows), lambda i: (i, 0, 0)), pair_spec(rows), pair_spec(rows), whole_spec((rows, state)),
            whole_spec((rows, state)), pair_spec(state), pair_spec(1), whole_spec((rows, 1)), whole_spec((1, rows)),
        ],
        out_specs=[pair_spec(rows), pair_spec(rows)],
        scratch_shapes=[pltpu.VMEM((rows, rows), F32), pltpu.VMEM((rows, 128), LOW)],
        compiler_params=kernel_params(),
        cost_estimate=pl.CostEstimate(flops=8 * rows * rows * width, bytes_accessed=10 * rows * width, transcendentals=rows * rows * width // 64),
        name="mamba_forward",
    )(per_head, xs, z, b, c, state_in, skip, seg_col, seg_row)


def mamba_backward(per_head, xs, z, y, dg, b, c, state_in, later, skip, seg_col, seg_row):
    rows, width = xs.shape
    pairs = width // 128
    blk = min(256, rows)
    state = b.shape[1]

    def body(head_ref, xs_ref, z_ref, y_ref, dg_ref, b_ref, c_ref, state_ref, later_ref, skip_ref, seg_col_ref, seg_row_ref,
             dxs_ref, dz_ref, db_ref, dc_ref, stats_ref, inner, d_inner, dy_low, x_low):
        @pl.when(pl.program_id(0) == 0)
        def _():
            u = lax.broadcasted_iota(jnp.int32, (rows, rows), 0)
            t = lax.broadcasted_iota(jnp.int32, (rows, rows), 1)
            seen = (seg_col_ref[...] == seg_row_ref[...]) & (u <= t)
            inner[...] = jnp.where(seen, nt_dot(b_ref[...], c_ref[...]), 0.0)
            d_inner[...] = jnp.zeros_like(d_inner)
            db_ref[...] = jnp.zeros_like(db_ref)
            dc_ref[...] = jnp.zeros_like(dc_ref)

        lane = lax.broadcasted_iota(jnp.int32, (rows, 128), 1)
        by_row = head_ref[0]
        by_col = by_row.T
        xs_f = xs_ref[...].astype(F32)
        z_f = z_ref[...].astype(F32)
        sig = jax.nn.sigmoid(z_f)
        d_gate = dg_ref[...].astype(F32)
        d_y = d_gate * z_f * sig
        y_core = y_ref[...]
        dz_ref[...] = (d_gate * (y_core + skip_ref[...] * xs_f) * sig * (1.0 + z_f * (1.0 - sig))).astype(LOW)
        dy_low[...] = d_y.astype(LOW)
        dt = halves(by_col, 2, lane)
        x_dt = xs_f * dt
        x_low[...] = x_dt.astype(LOW)
        closing = halves(by_col, 6, lane)
        from_later = nn_dot(b_ref[...], later_ref[...]) * closing
        db_ref[...] += nt_dot((x_dt * closing).astype(LOW), later_ref[...])
        dc_ref[...] += nt_dot((d_y * halves(by_col, 4, lane)).astype(LOW), state_ref[...])
        count = rows // blk
        columns = jnp.zeros((rows, 128), F32)
        d_x_parts = []
        for j in range(count):
            part = slice(j * blk, (j + 1) * blk)
            sums = []
            for h in range(2):
                own = (lane[part] < 64) if h == 0 else (lane[part] >= 64)
                x_h = jnp.where(own, x_low[part, :].astype(F32), 0.0).astype(LOW)
                total = None
                for i in range(j, count):
                    other = slice(i * blk, (i + 1) * blk)
                    gap = by_row[h : h + 1, other] - by_col[part, h : h + 1]
                    decay = jnp.exp(jnp.minimum(gap, 0.0))
                    term = nn_dot((decay * inner[part, other]).astype(LOW), dy_low[other, :])
                    total = term if total is None else total + term
                    d_inner[part, other] += decay * nt_dot(x_h, dy_low[other, :])
                sums.append(total)
            d_x_parts.append(jnp.where(lane[part] < 64, sums[0], sums[1]))
        d_x = jnp.concatenate(d_x_parts, axis=0) if count > 1 else d_x_parts[0]
        d_x = d_x + from_later
        dxs_ref[...] = (d_x * dt + skip_ref[...] * d_y).astype(LOW)
        rounded_x = x_low[...].astype(F32)
        rounded_dy = dy_low[...].astype(F32)
        for at, value in enumerate((d_x * xs_f, rounded_dy * y_core - rounded_x * d_x, rounded_x * from_later, d_y * xs_f)):
            for h in range(2):
                own = (lane < 64) if h == 0 else (lane >= 64)
                total = jnp.sum(jnp.where(own, value, 0.0), axis=1, keepdims=True)
                columns = jnp.where(lane == 2 * at + h, total, columns)
        stats_ref[0] = columns.T[:8]

        @pl.when(pl.program_id(0) == pairs - 1)
        def _():
            u = lax.broadcasted_iota(jnp.int32, (rows, rows), 0)
            t = lax.broadcasted_iota(jnp.int32, (rows, rows), 1)
            seen = (seg_col_ref[...] == seg_row_ref[...]) & (u <= t)
            low = jnp.where(seen, d_inner[...], 0.0).astype(LOW)
            db_ref[...] += nn_dot(low, c_ref[...])
            dc_ref[...] += tn_dot(low, b_ref[...])

    return pl.pallas_call(
        body,
        grid=(pairs,),
        out_shape=(
            jax.ShapeDtypeStruct((rows, width), LOW), jax.ShapeDtypeStruct((rows, width), LOW),
            jax.ShapeDtypeStruct((rows, state), F32), jax.ShapeDtypeStruct((rows, state), F32),
            jax.ShapeDtypeStruct((pairs, 8, rows), F32),
        ),
        in_specs=[
            pl.BlockSpec((1, 8, rows), lambda i: (i, 0, 0)), pair_spec(rows), pair_spec(rows), pair_spec(rows), pair_spec(rows),
            whole_spec((rows, state)), whole_spec((rows, state)), pair_spec(state), pair_spec(state), pair_spec(1),
            whole_spec((rows, 1)), whole_spec((1, rows)),
        ],
        out_specs=[
            pair_spec(rows), pair_spec(rows), whole_spec((rows, state)), whole_spec((rows, state)),
            pl.BlockSpec((1, 8, rows), lambda i: (i, 0, 0)),
        ],
        scratch_shapes=[
            pltpu.VMEM((rows, rows), F32), pltpu.VMEM((rows, rows), F32), pltpu.VMEM((rows, 128), LOW), pltpu.VMEM((rows, 128), LOW),
        ],
        compiler_params=kernel_params(),
        cost_estimate=pl.CostEstimate(flops=24 * rows * rows * width, bytes_accessed=16 * rows * width, transcendentals=rows * rows * width // 64),
        name="mamba_backward",
    )(per_head, xs, z, y, dg, b, c, state_in, later, skip, seg_col, seg_row)

def per_device(
    tokens, cotangent, doc_lengths, mixer_gain, w_query, key_matrix, value_matrix, mamba_gate_weight,
    mamba_input_weight, w_bproj, w_cproj, w_dt, a_log, dt_bias, d_skip, w_attn_out, w_mixer_out,
    ffn_gain, w_gate, w_up, w_down,
):
    micro_count, seq_count, block_len, model_dim = tokens.shape
    rows_here = mixer_gain.shape[0]
    heads = w_dt.shape[1]
    ssm_dim = mamba_gate_weight.shape[1]
    head_dim = ssm_dim // heads
    q_dim = w_query.shape[1]
    kv_dim = key_matrix.shape[1]
    state_dim = w_bproj.shape[1]
    ff_dim = w_gate.shape[1]
    ci = lax.axis_index("context")
    nc = lax.axis_size("context")
    full_len = nc * block_len
    units = micro_count * seq_count
    pairs = heads // 2

    def fill(width):
        return jnp.zeros((rows_here, -width % 128), LOW)

    first = jnp.concatenate(
        [w_query, key_matrix, value_matrix, mixer_gain[:, None], ffn_gain[:, None], fill(q_dim + 2 * kv_dim + 2)], axis=1)
    second = jnp.concatenate([mamba_gate_weight, mamba_input_weight, w_bproj, w_cproj, w_dt, fill(heads)], axis=1)
    third = jnp.concatenate([w_attn_out.T, w_mixer_out.T], axis=1)
    fourth = jnp.concatenate([w_gate, w_up, w_down.T], axis=1)
    first = gather_rows(first, False)
    second = gather_rows(second, False)
    third = gather_rows(third, True)
    fourth = gather_rows(fourth, True)
    at_gain = q_dim + 2 * kv_dim
    at_b = 2 * ssm_dim
    at_dt = at_b + 2 * state_dim
    gain_one = first[:, at_gain].astype(F32)
    gain_two = first[:, at_gain + 1].astype(F32)
    gate_up = fourth[:, : 2 * ff_dim]
    down_t = fourth[:, 2 * ff_dim :]
    both = (units, block_len)

    positions = jnp.arange(full_len)
    doc_lens = doc_lengths.reshape(units, -1)
    seg_all = segment_ids(doc_lens, positions)
    seg_here = lax.dynamic_slice_in_dim(seg_all, ci * block_len, block_len, 1)
    seg_prev = segment_ids(doc_lens, jnp.reshape(ci * block_len - 1, (1,)))
    lowest = jnp.min(jnp.where(seg_all == seg_here[:, :1], positions, full_len), axis=1) // block_len
    spans = jnp.stack([lowest, jnp.broadcast_to(ci, lowest.shape)], axis=1).astype(jnp.int32)
    carried = (seg_here == seg_prev)[:, None, :]
    closing = (seg_here == seg_here[:, -1:])[:, None, :]
    tri = (jnp.arange(block_len)[:, None] <= jnp.arange(block_len)[None, :]).astype(F32)
    skip_row = jnp.repeat(d_skip, head_dim)[None]

    x = tokens.reshape(units * block_len, model_dim).astype(F32)
    r1, n1 = norm_forward(x, gain_one)
    p_one = mat_mul(n1, first)
    q = (p_one[:, :q_dim].astype(LOW) * jnp.asarray(0.125, LOW)).reshape(both + (q_dim,))
    kv = p_one[:, q_dim:at_gain].astype(LOW).reshape(both + (2 * kv_dim,))
    kv_all = jnp.swapaxes(gather_context(kv), 0, 1).reshape(units, full_len, 2 * kv_dim)
    p_two = mat_mul(n1, second)
    zx = p_two[:, :at_b].astype(LOW).reshape(both + (at_b,))
    bc = p_two[:, at_b:at_dt].astype(LOW).reshape(both + (2 * state_dim,))
    dr = jnp.swapaxes(p_two[:, at_dt : at_dt + heads].reshape(both + (heads,)), 1, 2) + dt_bias[:, None]
    dt = jax.nn.softplus(dr)
    rate = -jnp.exp(a_log)[:, None]
    decay = jnp.einsum("sht,tu->shu", rate * dt, tri, precision=PRECISE)
    last = decay[:, :, -1:]
    entering = jnp.where(carried, jnp.exp(decay), 0.0)
    leaving = jnp.where(closing, jnp.exp(last - decay), 0.0)
    passing = entering[:, :, -1]

    def packed(*parts):
        stacked = jnp.stack([part.reshape(units, pairs, 2, block_len) for part in parts], axis=2)
        return stacked.reshape(units, pairs, 8, block_len)

    per_head = packed(decay, dt, entering, leaving)
    per_head_two = packed(decay, dt, entering, leaving * dt)
    x_of = [zx[u, :, ssm_dim:] for u in range(units)]
    z_of = [zx[u, :, :ssm_dim] for u in range(units)]
    b_of = [bc[u, :, :state_dim] for u in range(units)]
    c_of = [bc[u, :, state_dim:] for u in range(units)]
    seg_col = [seg_here[u][:, None] for u in range(units)]
    seg_row = [seg_here[u][None] for u in range(units)]
    span = jnp.stack([mamba_state(per_head_two[u], 6, b_of[u], x_of[u]) for u in range(units)])
    pass_row = jnp.repeat(passing, head_dim, axis=1)[:, None, :]
    pass_high = pass_row.astype(LOW)
    pass_low = (pass_row - pass_high.astype(F32)).astype(LOW)
    sent = jnp.concatenate([span, pass_high, pass_low, jnp.zeros((units, 14, ssm_dim), LOW)], axis=1)
    spans_all = gather_context(sent).astype(F32)
    passes_all = spans_all[:, :, state_dim : state_dim + 1] + spans_all[:, :, state_dim + 1 : state_dim + 2]
    state = jnp.zeros((units, state_dim, ssm_dim), F32)
    for k in range(nc - 1):
        state = jnp.where(k < ci, passes_all[k] * state + spans_all[k, :, :state_dim], state)
    state_low = state.astype(LOW)

    o, lse, y, og, m = [], [], [], [], []
    for u in range(units):
        o_u, lse_u = attention_forward(q[u], kv_all[u], seg_here[u], seg_all[u], spans[u])
        y_u, g_u = mamba_forward(per_head[u], x_of[u], z_of[u], b_of[u], c_of[u], state_low[u], skip_row, seg_col[u], seg_row[u])
        o.append(o_u)
        lse.append(lse_u)
        y.append(y_u)
        og.append(jnp.concatenate([o_u, g_u], axis=1))
        m.append(tensor_sum(mat_mul_t(og[u], third)))

    layer_outs, h1, r2, n2, f, dab, dn2 = [], [], [], [], [], [], []
    dy = [cotangent.reshape(both + (model_dim,))[u] for u in range(units)]
    for u in range(units):
        h1.append(x[u * block_len : (u + 1) * block_len] + m[u])
        r2_u, n2_u = norm_forward(h1[u], gain_two)
        r2.append(r2_u)
        n2.append(n2_u)
        ab = mat_mul(n2[u], gate_up)
        a, b = ab[:, :ff_dim], ab[:, ff_dim:]
        sig = jax.nn.sigmoid(a)
        f.append((a * sig * b).astype(LOW))
        df = mat_mul(dy[u], down_t)
        dab.append(jnp.concatenate(
            [(df * b * sig * (1.0 + a * (1.0 - sig))).astype(LOW), (df * a * sig).astype(LOW)], axis=1))
        dn2.append(tensor_sum(mat_mul_t(dab[u], gate_up)))
    for u in range(units):
        layer_outs.append((h1[u] + tensor_sum(mat_mul_t(f[u], down_t))).astype(LOW))
    g_gate_up = sum(outer_sum(n2[u], dab[u]) for u in range(units)).astype(LOW)
    g_down = sum(outer_sum(dy[u], f[u]) for u in range(units)).astype(LOW)
    g_fourth = scatter_rows(jnp.concatenate([g_gate_up, g_down], axis=1))

    g_gain_two = 0.0
    dh, dm, dog, local = [], [], [], []
    for u in range(units):
        dh.append(norm_backward(h1[u], r2[u], gain_two, dn2[u]) + dy[u].astype(F32))
        g_gain_two = g_gain_two + jnp.sum(dn2[u] * h1[u] * r2[u], axis=0)
        dm.append(dh[u].astype(LOW))
        dog.append(mat_mul(dm[u], third).astype(LOW))
        local.append(mamba_state(per_head[u], 4, c_of[u], dog[u][:, q_dim:], z_of[u]))
    g_third = scatter_rows(sum(outer_sum(dm[u], og[u]) for u in range(units)).astype(LOW))
    locals_all = gather_context(jnp.stack(local)).astype(F32)
    later = jnp.zeros((units, state_dim, ssm_dim), F32)
    for k in range(nc - 1, 0, -1):
        later = jnp.where(k > ci, passes_all[k] * later + locals_all[k], later)
    later_low = later.astype(LOW)
    d_pass = jnp.sum((later * state).reshape(units, state_dim, heads, head_dim), axis=(1, 3))
    d_second, stats, dq, dkv = [], [], [], []
    for u in range(units):
        dxs, dz, db, dc, stat = mamba_backward(
            per_head[u], x_of[u], z_of[u], y[u], dog[u][:, q_dim:], b_of[u], c_of[u], state_low[u], later_low[u],
            skip_row, seg_col[u], seg_row[u])
        d_second.append((dz, dxs, db, dc))
        stats.append(stat)
    stats = jnp.stack(stats).reshape(units, pairs, 4, 2, block_len)
    stats = jnp.swapaxes(stats, 1, 2).reshape(units, 4, heads, block_len)
    d_end = jnp.sum(stats[:, 2], axis=2) + d_pass * passing
    d_decay = stats[:, 1] + jnp.where(jnp.arange(block_len) == block_len - 1, d_end[:, :, None], 0.0)
    d_rate = jnp.einsum("shu,tu->sht", d_decay, tri, precision=PRECISE)
    ddr = (stats[:, 0] + rate * d_rate) * jax.nn.sigmoid(dr)
    head_grads = all_sum(jnp.stack([
        jnp.sum(d_rate * rate * dt, axis=(0, 2)), jnp.sum(ddr, axis=(0, 2)), jnp.sum(stats[:, 3], axis=(0, 2))]))
    ddr = jnp.swapaxes(ddr, 1, 2).astype(LOW)
    d_second = [
        jnp.concatenate([dz, dxs, db.astype(LOW), dc.astype(LOW), ddr[u], jnp.zeros((block_len, -heads % 128), LOW)], axis=1)
        for u, (dz, dxs, db, dc) in enumerate(d_second)]
    g_second = reduce_rows(sum(outer_sum(n1[u * block_len : (u + 1) * block_len], d_second[u]) for u in range(units)).astype(LOW))
    g_second = jnp.concatenate(
        [g_second[:, :at_b], tensor_sum(g_second[:, at_b:at_dt]), g_second[:, at_dt:]], axis=1)
    g_second = share_rows(g_second).astype(F32)
    for u in range(units):
        dq_u, part = attention_backward(
            q[u], dog[u][:, :q_dim], o[u], kv_all[u], lse[u], seg_here[u], seg_all[u], spans[u])
        part = part.reshape(nc, block_len, 2 * kv_dim)
        left = nc
        for bit in context_bits():
            left //= 2
            view = part.reshape(left, 2, block_len, 2 * kv_dim)
            mine = (ci & bit) // bit
            away = lax.dynamic_index_in_dim(view, 1 - mine, 1, keepdims=False)
            keep = lax.dynamic_index_in_dim(view, mine, 1, keepdims=False)
            part = (keep.astype(F32) + swap_context(away, bit).astype(F32)).astype(LOW)
        dq.append(dq_u)
        dkv.append(part.reshape(block_len, 2 * kv_dim))
    input_grads = []
    g_gain_one = 0.0
    d_first = []
    for u in range(units):
        at = slice(u * block_len, (u + 1) * block_len)
        d_first.append(jnp.concatenate([dq[u], dkv[u], jnp.zeros((block_len, first.shape[1] - at_gain), LOW)], axis=1))
        part = mat_mul_t(d_first[u], first) + mat_mul_t(d_second[u], second)
        g_gain_one = g_gain_one + jnp.sum(part * x[at] * r1[at], axis=0)
        input_grads.append(dh[u] + norm_backward(x[at], r1[at], gain_one, tensor_sum(part)))
    g_first = sum(outer_sum(n1[u * block_len : (u + 1) * block_len], d_first[u][:, :at_gain]) for u in range(units))
    g_first = jnp.concatenate(
        [g_first, g_gain_one[:, None], g_gain_two[:, None], jnp.zeros((model_dim, first.shape[1] - at_gain - 2), F32)], axis=1)
    g_first = reduce_rows(g_first.astype(LOW))
    gains = g_first[:, at_gain:]
    lane = jnp.arange(gains.shape[1])[None]
    gains = jnp.where(lane == 0, tensor_sum(gains), gains)
    g_first = share_rows(jnp.concatenate([g_first[:, :at_gain], gains], axis=1)).astype(F32)

    shape = (micro_count, seq_count, block_len, model_dim)
    at_k, at_v = q_dim, q_dim + kv_dim
    return (
        jnp.stack(layer_outs).reshape(shape),
        jnp.stack(input_grads).reshape(shape),
        g_first[:, at_gain],
        g_first[:, :at_k],
        g_first[:, at_k:at_v],
        g_first[:, at_v:at_gain],
        g_second[:, :ssm_dim],
        g_second[:, ssm_dim:at_b],
        g_second[:, at_b : at_b + state_dim],
        g_second[:, at_b + state_dim : at_dt],
        g_second[:, at_dt : at_dt + heads],
        head_grads[0],
        head_grads[1],
        head_grads[2],
        g_third[:, :q_dim].T,
        g_third[:, q_dim:].T,
        g_first[:, at_gain + 1],
        g_fourth[:, :ff_dim],
        g_fourth[:, ff_dim : 2 * ff_dim],
        g_fourth[:, 2 * ff_dim :].T,
    )


def solution(mesh):
    rows, cols = P("fsdp", "tensor"), P("tensor", "fsdp")
    acts = P(None, "fsdp", "context", None)
    return jax.shard_map(
        per_device,
        mesh=mesh,
        in_specs=(
            acts, acts, P(None, "fsdp", None), P("fsdp"), rows, rows, rows, rows, rows, P("fsdp", None),
            P("fsdp", None), rows, P("tensor"), P("tensor"), P("tensor"), cols, cols, P("fsdp"), rows, rows, cols,
        ),
        out_specs=(
            acts, acts, P("fsdp"), rows, rows, rows, rows, rows, P("fsdp", None), P("fsdp", None), rows,
            P("tensor"), P("tensor"), P("tensor"), cols, cols, P("fsdp"), rows, rows, cols,
        ),
        check_vma=False,
    )
```

```python
import jax
import jax.numpy as jnp
from jax import lax
from jax.experimental import pallas as pl
from jax.experimental.pallas import tpu as pltpu
from jax.sharding import PartitionSpec as P

HEAD_WIDTH = 64
EPSILON = 1e-06
LOW = jnp.bfloat16
F32 = jnp.float32
NEGATIVE = -1e30
PRECISE = lax.Precision.HIGHEST


def swap_context(x, bit):
    size = lax.axis_size("context")
    return lax.ppermute(x, "context", [(i, i ^ bit) for i in range(size)])


def from_next(x, axis, step=1):
    size = lax.axis_size(axis)
    return lax.ppermute(x, axis, [((i + step) % size, i) for i in range(size)])


def swap_tensor(x):
    size = lax.axis_size("tensor")
    return lax.ppermute(x, "tensor", [(i, (i + 1) % size) for i in range(size)])


def context_bits():
    size = lax.axis_size("context")
    return [1 << k for k in range(size.bit_length() - 1)]


def reverse_bits(index):
    bits = context_bits()
    return sum(((index // low) % 2) * high for low, high in zip(bits, reversed(bits)))


CHAIN = []
SCALE = 0.4e9


def anywhere(arrays):
    return [pl.BlockSpec(memory_space=pl.ANY)] * len(arrays)


def whole_spec(shape):
    return pl.BlockSpec(shape, lambda i: (0,) * len(shape))


def pair_spec(rows):
    return pl.BlockSpec((rows, 128), lambda i: (0, i))


SCALARS = pl.BlockSpec(memory_space=pltpu.SMEM)


def wait_for(*arrays):
    CHAIN.extend(arrays)


def launch(body, *, out_shape, in_specs, out_specs, name, us, grid=(1,), scratch_shapes=(), input_output_aliases=None):
    single = not isinstance(out_shape, tuple)
    outs = (out_shape,) if single else out_shape
    specs = [out_specs] if single else list(out_specs)

    def call(*args):
        waits = tuple(CHAIN)
        n_in, n_out = len(args), len(outs)
        at = n_in + len(waits)

        def run(*refs):
            body(*refs[:n_in], *refs[at : at + n_out], *refs[at + n_out + 1 :])

        made = pl.pallas_call(
            run,
            grid=grid,
            out_shape=outs + (jax.ShapeDtypeStruct((8, 128), F32),),
            in_specs=list(in_specs) + anywhere(waits),
            out_specs=specs + anywhere((0,)),
            scratch_shapes=list(scratch_shapes),
            input_output_aliases=input_output_aliases or {},
            compiler_params=pltpu.CompilerParams(vmem_limit_bytes=48 * 2**20),
            cost_estimate=pl.CostEstimate(flops=int(us * SCALE), bytes_accessed=1, transcendentals=0),
            name=name,
        )(*args, *waits)
        CHAIN[:] = made[-1:]
        return made[0] if single else made[:-1]

    return call


def column_block(cols):
    return next(blk for blk in (512, 256, 128) if cols % blk == 0)


def join(parts, axis_new):
    if axis_new:
        parts = [part[None] for part in parts]
    counts = [part.shape[0] for part in parts]
    shape = parts[0].shape[1:]
    cols = shape[-1]
    blk = column_block(cols)

    def spec(count):
        return pl.BlockSpec((count, *shape[:-1], blk), lambda j: (0,) * len(shape) + (j,))

    def body(*refs):
        at = 0
        for ref, count in zip(refs, counts):
            refs[-1][at : at + count] = ref[...]
            at += count

    return launch(
        body, grid=(cols // blk,), out_shape=jax.ShapeDtypeStruct((sum(counts), *shape), parts[0].dtype),
        in_specs=[spec(count) for count in counts], out_specs=spec(sum(counts)), name="join", us=2,
    )(*parts)


def send_near(own):
    return [from_next(own, "fsdp", k) for k in range(1, lax.axis_size("fsdp"))]


def far_bits():
    return list(reversed(context_bits()[1:]))


def spread_far(held):
    for bit in far_bits():
        held = join([held, swap_context(held, bit)], False)
    return held


def place_rows(place, shard, mine, other):
    nc, part, cols = shard.shape
    nf = lax.axis_size("fsdp")
    offsets = [reverse_bits(m) for m in range(nc)][: nc // 2]
    blk = column_block(cols)

    def body(place_ref, shard_ref, mine_ref, other_ref, out_ref):
        fi, ci = place_ref[0], place_ref[1]
        out_ref[fi] = shard_ref[...]
        for k in range(1, nf):
            z = lax.rem(fi + k, nf)
            for m, off in enumerate(offsets):
                at = m * (nf - 1) + k - 1
                out_ref[z, lax.bitwise_xor(ci, off)] = mine_ref[at]
                out_ref[z, lax.bitwise_xor(ci, off ^ 1)] = other_ref[at]

    def columns(*leading):
        return pl.BlockSpec((*leading, blk), lambda j: (0,) * len(leading) + (j,))

    count = mine.shape[0]
    full = launch(
        body,
        grid=(cols // blk,),
        out_shape=jax.ShapeDtypeStruct((nf, nc, part, cols), shard.dtype),
        in_specs=[SCALARS, columns(nc, part), columns(count, part), columns(count, part)],
        out_specs=columns(nf, nc, part),
        name="place_rows",
        us=cols / 600,
    )(place, shard, mine, other)
    return full.reshape(nf * nc * part, cols)


def place_blocks(place, mine, other):
    half, units, rows, cols = mine.shape
    nc = 2 * half
    offsets = [reverse_bits(m) for m in range(nc)][:half]

    def body(place_ref, mine_ref, other_ref, out_ref):
        ci = place_ref[1]
        for u in range(units):
            for m, off in enumerate(offsets):
                for ref, bit in ((mine_ref, 0), (other_ref, 1)):
                    at = pl.multiple_of(lax.bitwise_xor(ci, off ^ bit) * rows, rows)
                    out_ref[u, pl.ds(at, rows), :] = ref[m, u]

    return launch(
        body,
        out_shape=jax.ShapeDtypeStruct((units, nc * rows, cols), mine.dtype),
        in_specs=[SCALARS, whole_spec(mine.shape), whole_spec(other.shape)],
        out_specs=whole_spec((units, nc * rows, cols)),
        name="place_blocks",
        us=1,
    )(place, mine, other)


def at_offset(ref_pair, ci, k, nc):
    off = lax.bitwise_xor(ci, k)
    entry, weight, rest = 0, nc // 2, off
    half = lax.div(off, 2)
    width = nc // 2
    index, bit = 0, width // 2
    low = 1
    while bit:
        index = index + lax.rem(lax.div(half, low), 2) * bit
        bit, low = bit // 2, low * 2
    same = lax.rem(off, 2) == 0
    mine, other = ref_pair
    return index, same, mine, other


def chain_states(place, spans, state_dim, local=None, unit=None):
    half, units, height, width = spans[0].shape
    nc = 2 * half
    blk = column_block(width)
    count = units if local is None else 1
    extra = () if local is None else tuple(local)

    def body(place_ref, *refs):
        ci = place_ref[1]
        out_ref = refs[-1]
        for n in range(count):
            u = n if local is None else unit
            total = jnp.zeros((state_dim, blk), F32)
            for k in range(nc - 1) if local is None else range(nc - 1, 0, -1):
                index, same, mine, other = at_offset(refs[:2], ci, k, nc)
                passing = jnp.where(same, mine[index, u, state_dim:].astype(F32), other[index, u, state_dim:].astype(F32))
                if local is None:
                    term = jnp.where(same, mine[index, u, :state_dim].astype(F32), other[index, u, :state_dim].astype(F32))
                    active = k < ci
                else:
                    term = jnp.where(same, refs[2][index, 0].astype(F32), refs[3][index, 0].astype(F32))
                    active = k > ci
                new = (passing[0:1] + passing[1:2]) * total + term
                total = jnp.where(active, new, total)
            out_ref[n] = total.astype(LOW)

    def columns(shape):
        return pl.BlockSpec((*shape[:-1], blk), lambda j: (0,) * (len(shape) - 1) + (j,))

    out = (count, state_dim, width)
    return launch(
        body,
        grid=(width // blk,),
        out_shape=jax.ShapeDtypeStruct(out, LOW),
        in_specs=[SCALARS] + [columns(arr.shape) for arr in (*spans, *extra)],
        out_specs=columns(out),
        name="chain_states",
        us=1.2,
    )(place, *spans, *extra)


def outer(place, left, right, into, at, width):
    nf, nc = lax.axis_size("fsdp"), lax.axis_size("context")
    tokens, model = left.shape
    cols = right.shape[1]
    part = model // (nf * nc)
    blk = next(b for b in (512, 256, 128) if cols % b == 0 and at % b == 0)
    given = () if into is None else tuple(into)

    def body(place_ref, left_ref, right_ref, *rest):
        away_ref, keep_ref, turned, made = rest[-4:]

        @pl.when(pl.program_id(0) == 0)
        def _():
            turned[...] = left_ref[...].T

        made[...] = nn_dot(turned[...], right_ref[...])
        mine = lax.rem(place_ref[1], 2)
        for z in range(nf):
            for x in range(nc // 2):
                first = (z * nc + 2 * x) * part
                keep_ref[z, x] = made[pl.ds(pl.multiple_of(first + mine * part, part), part), :].astype(LOW)
                away_ref[z, x] = made[pl.ds(pl.multiple_of(first + (1 - mine) * part, part), part), :].astype(LOW)

    shape = jax.ShapeDtypeStruct((nf, nc // 2, part, width), LOW)
    spec = pl.BlockSpec((nf, nc // 2, part, blk), lambda j: (0, 0, 0, at // blk + j))
    return launch(
        body,
        grid=(cols // blk,),
        out_shape=(shape, shape),
        in_specs=[SCALARS, whole_spec((tokens, model)), pl.BlockSpec((tokens, blk), lambda j: (0, j))] + anywhere(given),
        out_specs=[spec, spec],
        input_output_aliases={3: 0, 4: 1} if given else {},
        scratch_shapes=[pltpu.VMEM((model, tokens), LOW), pltpu.VMEM((model, blk), F32)],
        name="outer",
        us=cols / 230,
    )(place, left, right, *given)


def split_sum(place, keep, got, bit):
    n, left, rows, cols = keep.shape
    blk = column_block(cols)

    def body(place_ref, keep_ref, got_ref, away_ref, stay_ref):
        mine = lax.rem(lax.div(place_ref[1], bit), 2)
        for z in range(n):
            for j in range(left // 2):
                for ref, b in ((stay_ref, mine), (away_ref, 1 - mine)):
                    i = 2 * j + b
                    ref[z, j] = (keep_ref[z, i].astype(F32) + got_ref[z, i].astype(F32)).astype(LOW)

    def spec(count):
        return pl.BlockSpec((n, count, rows, blk), lambda j: (0, 0, 0, j))

    shape = jax.ShapeDtypeStruct((n, left // 2, rows, cols), LOW)
    return launch(
        body, grid=(cols // blk,), out_shape=(shape, shape), in_specs=[SCALARS, spec(left), spec(left)],
        out_specs=[spec(left // 2)] * 2, name="split_sum", us=cols / 900,
    )(place, keep, got)


def split_fsdp(place, keep, got):
    nf, _, part, cols = keep.shape
    blk = column_block(cols)

    def body(place_ref, keep_ref, got_ref, *outs):
        for k in range(nf):
            z = lax.rem(place_ref[0] + (nf - k), nf)
            outs[k][...] = (keep_ref[z, 0].astype(F32) + got_ref[z, 0].astype(F32)).astype(LOW)

    spec = pl.BlockSpec((nf, 1, part, blk), lambda j: (0, 0, 0, j))
    return launch(
        body, grid=(cols // blk,), out_shape=(jax.ShapeDtypeStruct((part, cols), LOW),) * nf, in_specs=[SCALARS, spec, spec],
        out_specs=[pl.BlockSpec((part, blk), lambda j: (0, j))] * nf, name="split_fsdp", us=cols / 1200,
    )(place, keep, got)


def sum_parts(parts, shared=()):
    cols = parts[0].shape[1]
    blk = column_block(cols)

    def body(*refs):
        total = refs[0][...].astype(F32)
        for ref in refs[1:-1]:
            total = total + ref[...].astype(F32)
        refs[-1][...] = total.astype(LOW)

    spec = pl.BlockSpec((parts[0].shape[0], blk), lambda j: (0, j))
    total = launch(
        body, grid=(cols // blk,), out_shape=jax.ShapeDtypeStruct(parts[0].shape, LOW), in_specs=[spec] * len(parts),
        out_specs=spec, name="sum_parts", us=1.3,
    )(*parts)
    if shared:
        mid = total[:, shared[0] : shared[1]]
        mid = (mid.astype(F32) + swap_tensor(mid).astype(F32)).astype(LOW)
        total = jnp.concatenate([total[:, : shared[0]], mid, total[:, shared[1] :]], axis=1)
    return total


def share_rows(total):
    held = total[None]
    for bit in reversed(context_bits()):
        held = jnp.concatenate([held, swap_context(held, bit)])
    ci = lax.axis_index("context")
    order = [reverse_bits(k) ^ reverse_bits(ci) for k in range(lax.axis_size("context"))]
    rows = jnp.stack([lax.dynamic_index_in_dim(held, m, 0, keepdims=False) for m in order])
    return rows.astype(F32).reshape(-1, total.shape[1])


def reduce_far(place, keep, got, bits):
    for bit in bits:
        away, keep = split_sum(place, keep, got, bit)
        got = swap_context(away, bit)
    return keep, got


def all_sum(x):
    for bit in context_bits():
        x = x + swap_context(x, bit)
    size, bit = lax.axis_size("fsdp"), 1
    while bit < size:
        x = x + lax.ppermute(x, "fsdp", [(i, i ^ bit) for i in range(size)])
        bit *= 2
    return x


def tensor_sum(x):
    low = lax.reduce_precision(x, 8, 7).astype(LOW)
    return low.astype(F32) + swap_tensor(low).astype(F32)


def nt_dot(left, right):
    return lax.dot_general(left, right, (((1,), (1,)), ((), ())), preferred_element_type=F32)


def tn_dot(left, right):
    return lax.dot_general(left, right, (((0,), (0,)), ((), ())), preferred_element_type=F32)


def nn_dot(left, right):
    return jnp.dot(left, right, preferred_element_type=F32)


def document_start(lens_ref, unit, position):
    start, end = jnp.zeros_like(position), 0
    for d in range(lens_ref.shape[1]):
        end = end + lens_ref[unit, d]
        start = jnp.where(position >= end, end, start)
    return start


def lower_from(rows):
    u = lax.broadcasted_iota(jnp.int32, (rows, rows), 0)
    t = lax.broadcasted_iota(jnp.int32, (rows, rows), 1)
    return jnp.where(u <= t, 1.0, 0.0)


def project(place, lens, tokens, first, aux, q_dim, kv_dim, state, pairs):
    units = lens.shape[0]
    total, model = tokens.shape
    rows = total // units
    width = first.shape[1]
    at_b = q_dim + 2 * kv_dim
    at_dt = at_b + 2 * state

    def body(place_ref, lens_ref, x_ref, first_ref, aux_ref, n1_ref, q_ref, kv_ref, b_ref, c_ref, head_ref, gains_ref):
        unit = pl.program_id(0)

        @pl.when(unit == 0)
        def _():
            gains_ref[...] = first_ref[:, at_dt:].astype(F32).T[2 * pairs : 2 * pairs + 8]

        x = x_ref[...].astype(F32)
        scale = lax.rsqrt(jnp.mean(x * x, axis=1, keepdims=True) + EPSILON)
        n1_ref[...] = (x * scale * gains_ref[0:1, :]).astype(LOW)
        made = nn_dot(n1_ref[...], first_ref[...])
        q_ref[...] = (made[:, :q_dim].astype(LOW).astype(F32) * 0.125).astype(LOW)
        kv_ref[...] = made[:, q_dim:at_b].astype(LOW)
        b_ref[...] = made[:, at_b : at_b + state].astype(LOW)
        c_ref[...] = made[:, at_b + state : at_dt].astype(LOW)
        raw = made[:, at_dt:].T[:16] + aux_ref[:, 1:2]
        dt = jnp.maximum(raw, 0.0) + jnp.log1p(jnp.exp(-jnp.abs(raw)))
        decay = jnp.dot(-jnp.exp(aux_ref[:, 0:1]) * dt, lower_from(rows), precision=PRECISE, preferred_element_type=F32)
        base = place_ref[1] * rows
        position = base + lax.broadcasted_iota(jnp.int32, (1, rows), 1)
        carried = document_start(lens_ref, unit, position) < base
        closing = position >= document_start(lens_ref, unit, base + rows - 1)
        entering = jnp.where(carried, jnp.exp(decay), 0.0)
        leaving = jnp.where(closing, jnp.exp(decay[:, rows - 1 :] - decay), 0.0)
        for i in range(pairs):
            for at, value in enumerate((decay, dt, entering, leaving)):
                head_ref[i, 2 * at : 2 * at + 2, :] = value[2 * i : 2 * i + 2]

    def of_unit(cols):
        return pl.BlockSpec((rows, cols), lambda u: (u, 0))

    def made_as(cols):
        return jax.ShapeDtypeStruct((total, cols), LOW)

    return launch(
        body,
        grid=(units,),
        out_shape=(
            made_as(model), made_as(q_dim), made_as(2 * kv_dim), made_as(state), made_as(state),
            jax.ShapeDtypeStruct((units, pairs, 8, rows), F32), jax.ShapeDtypeStruct((8, model), F32),
        ),
        in_specs=[SCALARS, SCALARS, of_unit(model), whole_spec((model, width)), whole_spec((16, 2))],
        out_specs=[
            of_unit(model), of_unit(q_dim), of_unit(2 * kv_dim), of_unit(state), of_unit(state),
            pl.BlockSpec((None, pairs, 8, rows), lambda u: (u, 0, 0, 0)), whole_spec((8, model)),
        ],
        us=6.5, name="project",
    )(place, lens, tokens, first, aux)


def attention_forward(unit, place, lens, q, kv_all, into, width):
    units, length, _ = kv_all.shape
    rows, q_dim = q.shape[0] // units, q.shape[1]
    heads = q_dim // HEAD_WIDTH
    given = () if into is None else (into,)

    def body(place_ref, lens_ref, q_ref, kv_ref, *rest):
        o_ref, lse_ref, bias, top, low, acc = rest[-6:]
        top[...] = jnp.full_like(top, NEGATIVE)
        low[...] = jnp.zeros_like(low)
        acc[...] = jnp.zeros_like(acc)
        own = place_ref[1]
        base = own * rows
        start = document_start(lens_ref, unit, base + lax.broadcasted_iota(jnp.int32, (1, rows), 1))
        blocks = own - document_start(lens_ref, unit, base) // rows + 1

        def step(i, carry):
            j = own - i
            at = pl.multiple_of(j * rows, rows)
            keys = kv_ref[pl.ds(at, rows), :HEAD_WIDTH]
            turned = kv_ref[pl.ds(at, rows), :].astype(F32).T[HEAD_WIDTH:].astype(LOW)
            u = at + lax.broadcasted_iota(jnp.int32, (rows, rows), 0)
            t = base + lax.broadcasted_iota(jnp.int32, (rows, rows), 1)
            seen = (u <= t) & (u >= start)
            bias[...] = jnp.where(seen, 0.0, NEGATIVE)
            for h in range(heads):
                lanes = slice(h * HEAD_WIDTH, (h + 1) * HEAD_WIDTH)
                s = nt_dot(keys, q_ref[:, lanes]) + bias[...]
                before = top[h : h + 1, :]
                now = jnp.maximum(before, jnp.max(s, axis=0, keepdims=True))
                p = jnp.exp(s - now)
                scale = jnp.exp(before - now)
                top[h : h + 1, :] = now
                low[h : h + 1, :] = low[h : h + 1, :] * scale + jnp.sum(p, axis=0, keepdims=True)
                acc[lanes, :] = acc[lanes, :] * scale + nn_dot(turned, p.astype(LOW))
            return carry

        lax.fori_loop(0, blocks, step, 0)
        for h in range(heads):
            lanes = slice(h * HEAD_WIDTH, (h + 1) * HEAD_WIDTH)
            acc[lanes, :] = acc[lanes, :] / low[h : h + 1, :]
        o_ref[...] = acc[...].T.astype(LOW)
        lse_ref[...] = top[...] + jnp.log(low[...])

    return launch(
        body,
        grid=(1,),
        out_shape=(jax.ShapeDtypeStruct((units * rows, width), LOW), jax.ShapeDtypeStruct((8, rows), F32)),
        in_specs=[
            SCALARS, SCALARS, pl.BlockSpec((rows, q_dim), lambda i: (unit, 0)),
            pl.BlockSpec((None, length, 2 * HEAD_WIDTH), lambda i: (unit, 0, 0)),
        ] + anywhere(given),
        out_specs=[pl.BlockSpec((rows, q_dim), lambda i: (unit, 0)), whole_spec((8, rows))],
        input_output_aliases={4: 0} if given else {},
        scratch_shapes=[
            pltpu.VMEM((rows, rows), F32),
            pltpu.VMEM((8, rows), F32),
            pltpu.VMEM((8, rows), F32),
            pltpu.VMEM((q_dim, rows), F32),
        ],
        us=10.5, name="attention_forward",
    )(place, lens, q, kv_all, *given)


def attention_backward(unit, place, lens, q, dog, og, kv_all, lse):
    units, length, _ = kv_all.shape
    rows, q_dim = q.shape[0] // units, q.shape[1]
    heads = q_dim // HEAD_WIDTH
    half = (1, length // rows // 2, rows, 2 * HEAD_WIDTH)
    sub = min(256, rows)

    def body(place_ref, lens_ref, q_ref, do_ref, o_ref, kv_ref, lse_ref, *rest):
        dq_ref, away_ref, keep_ref, bias, dq_acc, delta = rest[-6:]
        own = place_ref[1]
        base = own * rows
        start = document_start(lens_ref, unit, base + lax.broadcasted_iota(jnp.int32, (1, rows), 1))
        blocks = own - document_start(lens_ref, unit, base) // rows + 1
        dq_acc[...] = jnp.zeros_like(dq_acc)
        away_ref[...] = jnp.zeros_like(away_ref)
        keep_ref[...] = jnp.zeros_like(keep_ref)
        both = do_ref[...].astype(F32) * o_ref[...].astype(F32)
        lane = lax.broadcasted_iota(jnp.int32, (rows, 128), 1)
        columns = jnp.zeros((rows, 128), F32)
        for h in range(heads):
            total = jnp.sum(both[:, h * HEAD_WIDTH : (h + 1) * HEAD_WIDTH], axis=1, keepdims=True)
            columns = jnp.where(lane == h, total, columns)
        delta[...] = columns.T[:8]

        def step(i, carry):
            j = own - i
            at = pl.multiple_of(j * rows, rows)
            u = at + lax.broadcasted_iota(jnp.int32, (rows, rows), 0)
            t = base + lax.broadcasted_iota(jnp.int32, (rows, rows), 1)
            seen = (u <= t) & (u >= start)
            bias[...] = jnp.where(seen, 0.0, NEGATIVE)
            for r in range(0, rows, sub):
                keys = kv_ref[pl.ds(pl.multiple_of(at + r, sub), sub), :HEAD_WIDTH]
                values = kv_ref[pl.ds(pl.multiple_of(at + r, sub), sub), HEAD_WIDTH:]
                dk = jnp.zeros((sub, HEAD_WIDTH), F32)
                dv = jnp.zeros((sub, HEAD_WIDTH), F32)
                for h in range(heads):
                    lanes = slice(h * HEAD_WIDTH, (h + 1) * HEAD_WIDTH)
                    q_h, do_h = q_ref[:, lanes], do_ref[:, lanes]
                    p = jnp.exp(nt_dot(keys, q_h) + (bias[r : r + sub, :] - lse_ref[h : h + 1, :]))
                    ds = (p * (nt_dot(values, do_h) - delta[h : h + 1, :])).astype(LOW)
                    dv = dv + nn_dot(p.astype(LOW), do_h)
                    dk = dk + nn_dot(ds, q_h)
                    dq_acc[:, lanes] = dq_acc[:, lanes] + tn_dot(ds, keys)
                dkv = jnp.concatenate([dk, dv], axis=1).astype(LOW)

                @pl.when(lax.rem(own - j, 2) == 0)
                def _():
                    keep_ref[0, j // 2, r : r + sub, :] = dkv

                @pl.when(lax.rem(own - j, 2) == 1)
                def _():
                    away_ref[0, j // 2, r : r + sub, :] = dkv
            return carry

        lax.fori_loop(0, blocks, step, 0)
        dq_ref[...] = (dq_acc[...] * 0.125).astype(LOW)

    return launch(
        body,
        out_shape=(jax.ShapeDtypeStruct((rows, q_dim), LOW),) + (jax.ShapeDtypeStruct(half, LOW),) * 2,
        grid=(1,),
        in_specs=[
            SCALARS, SCALARS, pl.BlockSpec((rows, q_dim), lambda i: (unit, 0)), whole_spec((rows, q_dim)),
            pl.BlockSpec((rows, q_dim), lambda i: (unit, 0)), pl.BlockSpec((None, length, 2 * HEAD_WIDTH), lambda i: (unit, 0, 0)),
            whole_spec((8, rows)),
        ],
        out_specs=[whole_spec((rows, q_dim)), whole_spec(half), whole_spec(half)],
        scratch_shapes=[
            pltpu.VMEM((rows, rows), F32),
            pltpu.VMEM((rows, q_dim), F32),
            pltpu.VMEM((8, rows), F32),
        ],
        us=17, name="attention_backward",
    )(place, lens, q, dog, og, kv_all, lse)


def halves(columns, first, lane):
    return jnp.where(lane < 64, columns[:, first : first + 1], columns[:, first + 1 : first + 2])


def mamba_state(unit, per_head, left, zx, right=None, first=0):
    _, pairs, _, rows = per_head.shape
    state = left.shape[1]
    rights = () if right is None else (right,)
    height = state if rights else state + 16

    def body(head_ref, left_ref, zx_ref, *rest):
        out_ref = rest[-1]
        lane = lax.broadcasted_iota(jnp.int32, (rows, 128), 1)
        turned = left_ref[...].astype(F32).T.astype(LOW)
        for i in range(pairs):
            lanes = slice(128 * i, 128 * (i + 1))
            by_col = head_ref[i].T
            if rights:
                z = zx_ref[:, 256 * i : 256 * i + 128].astype(F32)
                value = rest[0][:, first + 128 * i : first + 128 * (i + 1)].astype(F32) * z * jax.nn.sigmoid(z)
                weight = halves(by_col, 4, lane)
            else:
                value = zx_ref[:, 256 * i + 128 : 256 * (i + 1)].astype(F32)
                weight = halves(by_col, 2, lane) * halves(by_col, 6, lane)
                passing = halves(by_col[rows - 16 :], 4, lane[:16])[15:]
                high = passing.astype(LOW).astype(F32)
                row = lax.broadcasted_iota(jnp.int32, (16, 128), 0)
                out_ref[state:, lanes] = jnp.where(row == 0, high, jnp.where(row == 1, passing - high, 0.0)).astype(LOW)
            out_ref[:state, lanes] = nn_dot(turned, (value * weight).astype(LOW)).astype(LOW)

    return launch(
        body,
        grid=(1,),
        out_shape=jax.ShapeDtypeStruct((height, 128 * pairs), LOW),
        in_specs=[
            pl.BlockSpec((None, pairs, 8, rows), lambda i: (unit, 0, 0, 0)), pl.BlockSpec((rows, state), lambda i: (unit, 0)),
            pl.BlockSpec((rows, 256 * pairs), lambda i: (unit, 0)),
        ] + [whole_spec(r.shape) for r in rights],
        out_specs=whole_spec((height, 128 * pairs)),
        us=2, name="mamba_state",
    )(per_head, left, zx, *rights)


def same_document(place_ref, lens_ref, unit, rows, t_axis):
    base = place_ref[1] * rows
    shape = (1, rows) if t_axis else (rows, 1)
    start = document_start(lens_ref, unit, base + lax.broadcasted_iota(jnp.int32, shape, t_axis)) - base
    t = lax.broadcasted_iota(jnp.int32, (rows, rows), t_axis)
    u = lax.broadcasted_iota(jnp.int32, (rows, rows), 1 - t_axis)
    return (u <= t) & (u >= start)


def mamba_forward(unit, place, lens, per_head, zx, b, c, state_in, skip, into, first):
    _, pairs, _, rows = per_head.shape
    blk = min(256, rows)
    state = b.shape[1]

    def body(place_ref, lens_ref, head_ref, zx_ref, b_ref, c_ref, state_ref, skip_ref, *rest):
        g_ref, y_ref, inner, x_dt = rest[-4:]

        @pl.when(pl.program_id(0) == 0)
        def _():
            seen = same_document(place_ref, lens_ref, unit, rows, 0)
            inner[...] = jnp.where(seen, nt_dot(c_ref[...], b_ref[...]), 0.0)

        lane = lax.broadcasted_iota(jnp.int32, (rows, 128), 1)
        by_row = head_ref[...]
        by_col = by_row.T
        xs_f = zx_ref[:, 128:].astype(F32)
        x_dt[...] = (xs_f * halves(by_col, 2, lane)).astype(LOW)
        read = nn_dot(c_ref[...], state_ref[...]) * halves(by_col, 4, lane)
        for i in range(rows // blk):
            part = slice(i * blk, (i + 1) * blk)
            sums = []
            for h in range(2):
                total = None
                for j in range(i + 1):
                    other = slice(j * blk, (j + 1) * blk)
                    gap = by_col[part, h : h + 1] - by_row[h : h + 1, other]
                    kernel = jnp.exp(jnp.minimum(gap, 0.0)) * inner[part, other]
                    term = nn_dot(kernel.astype(LOW), x_dt[other, :])
                    total = term if total is None else total + term
                sums.append(total)
            y = jnp.where(lane[part] < 64, sums[0], sums[1]) + read[part]
            y_ref[part, :] = y
            z_f = zx_ref[part, :128].astype(F32)
            g_ref[part, :] = ((y + skip_ref[...] * xs_f[part]) * z_f * jax.nn.sigmoid(z_f)).astype(LOW)

    return launch(
        body,
        grid=(pairs,),
        out_shape=(jax.ShapeDtypeStruct(into.shape, LOW), jax.ShapeDtypeStruct((rows, 128 * pairs), F32)),
        in_specs=[
            SCALARS, SCALARS, pl.BlockSpec((None, None, 8, rows), lambda i: (unit, i, 0, 0)), pl.BlockSpec((rows, 256), lambda i: (unit, i)),
            pl.BlockSpec((rows, state), lambda i: (unit, 0)), pl.BlockSpec((rows, state), lambda i: (unit, 0)),
            pl.BlockSpec((None, state, 128), lambda i: (unit, 0, i)), pair_spec(1),
        ] + anywhere((into,)),
        out_specs=[pl.BlockSpec((rows, 128), lambda i: (unit, first // 128 + i)), pair_spec(rows)],
        input_output_aliases={8: 0},
        scratch_shapes=[pltpu.VMEM((rows, rows), F32), pltpu.VMEM((rows, 128), LOW)],
        us=7.5, name="mamba_forward",
    )(place, lens, per_head, zx, b, c, state_in, skip, into)


def mamba_backward(unit, place, lens, per_head, zx, y, dog, first, b, c, state_in, later, skip, aux, into):
    _, pairs, _, rows = per_head.shape
    blk = min(256, rows)
    state = b.shape[1]
    given = () if into is None else tuple(into)

    def body(place_ref, lens_ref, head_ref, zx_ref, y_ref, dg_ref, b_ref, c_ref, state_ref, later_ref, skip_ref, aux_ref, *rest):
        dzx_ref, dbc_ref, grads_ref, inner, d_inner, dy_low, x_low, db, dc, stats = rest[-10:]
        pair = pl.program_id(0)

        @pl.when(pair == 0)
        def _():
            seen = same_document(place_ref, lens_ref, unit, rows, 1)
            inner[...] = jnp.where(seen, nt_dot(b_ref[...], c_ref[...]), 0.0)
            d_inner[...] = jnp.zeros_like(d_inner)
            db[...] = jnp.zeros_like(db)
            dc[...] = jnp.zeros_like(dc)

        lane = lax.broadcasted_iota(jnp.int32, (rows, 128), 1)
        by_row = head_ref[pair]
        by_col = by_row.T
        xs_f = zx_ref[:, 128:].astype(F32)
        z_f = zx_ref[:, :128].astype(F32)
        sig = jax.nn.sigmoid(z_f)
        d_gate = dg_ref[...].astype(F32)
        d_y = d_gate * z_f * sig
        y_core = y_ref[...]
        dzx_ref[:, :128] = (d_gate * (y_core + skip_ref[...] * xs_f) * sig * (1.0 + z_f * (1.0 - sig))).astype(LOW)
        dy_low[...] = d_y.astype(LOW)
        dt = halves(by_col, 2, lane)
        x_dt = xs_f * dt
        x_low[...] = x_dt.astype(LOW)
        closing = halves(by_col, 6, lane)
        from_later = nn_dot(b_ref[...], later_ref[...]) * closing
        db[...] += nt_dot((x_dt * closing).astype(LOW), later_ref[...])
        dc[...] += nt_dot((d_y * halves(by_col, 4, lane)).astype(LOW), state_ref[...])
        count = rows // blk
        columns = jnp.zeros((rows, 128), F32)
        d_x_parts = []
        for j in range(count):
            part = slice(j * blk, (j + 1) * blk)
            sums = []
            for h in range(2):
                own = (lane[part] < 64) if h == 0 else (lane[part] >= 64)
                x_h = jnp.where(own, x_low[part, :].astype(F32), 0.0).astype(LOW)
                total = None
                for i in range(j, count):
                    other = slice(i * blk, (i + 1) * blk)
                    gap = by_row[h : h + 1, other] - by_col[part, h : h + 1]
                    decay = jnp.exp(jnp.minimum(gap, 0.0))
                    term = nn_dot((decay * inner[part, other]).astype(LOW), dy_low[other, :])
                    total = term if total is None else total + term
                    d_inner[part, other] += decay * nt_dot(x_h, dy_low[other, :])
                sums.append(total)
            d_x_parts.append(jnp.where(lane[part] < 64, sums[0], sums[1]))
        d_x = jnp.concatenate(d_x_parts, axis=0) if count > 1 else d_x_parts[0]
        d_x = d_x + from_later
        dzx_ref[:, 128:] = (d_x * dt + skip_ref[...] * d_y).astype(LOW)
        rounded_x = x_low[...].astype(F32)
        rounded_dy = dy_low[...].astype(F32)
        carried_back = jnp.sum(later_ref[...].astype(F32) * state_ref[...].astype(F32), axis=0, keepdims=True)
        row = lax.broadcasted_iota(jnp.int32, (rows, 1), 0)
        for at, value in enumerate((d_x * xs_f, rounded_dy * y_core - rounded_x * d_x, rounded_x * from_later, d_y * xs_f)):
            for h in range(2):
                own = (lane < 64) if h == 0 else (lane >= 64)
                total = jnp.sum(jnp.where(own, value, 0.0), axis=1, keepdims=True)
                if at == 2:
                    own = (lane[:1] < 64) if h == 0 else (lane[:1] >= 64)
                    passed = jnp.sum(jnp.where(own, carried_back, 0.0), axis=1, keepdims=True)
                    total = total + jnp.where(row == rows - 1, passed * by_row[4 + h : 5 + h, rows - 1 :], 0.0)
                columns = jnp.where(lane == 2 * at + h, total, columns)
        stats[pair] = columns.T[:8]

        @pl.when(pair == pairs - 1)
        def _():
            seen = same_document(place_ref, lens_ref, unit, rows, 1)
            low = jnp.where(seen, d_inner[...], 0.0).astype(LOW)
            dbc_ref[:, :state] = (db[...] + nn_dot(low, c_ref[...])).astype(LOW)
            dbc_ref[:, state : 2 * state] = (dc[...] + tn_dot(low, b_ref[...])).astype(LOW)

            def heads_of(ref, at):
                blank = jnp.zeros((16 - 2 * pairs, rows), F32)
                parts = [ref[i, 2 * at : 2 * at + 2, :] for i in range(pairs)]
                return jnp.concatenate(parts + [blank] * (2 * pairs < 16), axis=0)

            dt = heads_of(head_ref, 1)
            rate = -jnp.exp(aux_ref[:, 0:1])
            position = lax.broadcasted_iota(jnp.int32, (1, rows), 1)
            d_end = jnp.sum(heads_of(stats, 2), axis=1, keepdims=True)
            d_decay = heads_of(stats, 1) + jnp.where(position == rows - 1, d_end, 0.0)
            d_rate = lax.dot_general(
                d_decay, lower_from(rows), (((1,), (1,)), ((), ())), precision=PRECISE, preferred_element_type=F32)
            d_raw = (heads_of(stats, 0) + rate * d_rate) * (1.0 - jnp.exp(-dt))
            turned = jnp.concatenate([d_raw, jnp.zeros((112, rows), F32)], axis=0).T
            dbc_ref[:, 2 * state : 2 * state + 128] = turned.astype(LOW)
            dbc_ref[:, 2 * state + 128 :] = jnp.zeros((rows, 128), LOW)
            lanes = lax.broadcasted_iota(jnp.int32, (16, 128), 1)
            sums = jnp.zeros((16, 128), F32)
            for at, value in enumerate((d_rate * rate * dt, d_raw, heads_of(stats, 3))):
                sums = jnp.where(lanes == at, jnp.sum(value, axis=1, keepdims=True), sums)
            grads_ref[...] = sums

    total = zx.shape[0]
    return launch(
        body,
        grid=(pairs,),
        out_shape=(
            jax.ShapeDtypeStruct(zx.shape, LOW), jax.ShapeDtypeStruct((total, 2 * state + 256), LOW),
            jax.ShapeDtypeStruct((16, 128), F32),
        ),
        in_specs=[
            SCALARS, SCALARS, pl.BlockSpec((None, pairs, 8, rows), lambda i: (unit, 0, 0, 0)),
            pl.BlockSpec((rows, 256), lambda i: (unit, i)), pair_spec(rows),
            pl.BlockSpec((rows, 128), lambda i: (0, first // 128 + i)),
            pl.BlockSpec((rows, state), lambda i: (unit, 0)), pl.BlockSpec((rows, state), lambda i: (unit, 0)),
            pl.BlockSpec((None, state, 128), lambda i: (unit, 0, i)), pair_spec(state), pair_spec(1), whole_spec((16, 2)),
        ] + anywhere(given),
        out_specs=[
            pl.BlockSpec((rows, 256), lambda i: (unit, i)), pl.BlockSpec((rows, 2 * state + 256), lambda i: (unit, 0)),
            whole_spec((16, 128)),
        ],
        input_output_aliases={12: 0, 13: 1} if given else {},
        scratch_shapes=[
            pltpu.VMEM((rows, rows), F32), pltpu.VMEM((rows, rows), F32), pltpu.VMEM((rows, 128), LOW), pltpu.VMEM((rows, 128), LOW),
            pltpu.VMEM((rows, state), F32), pltpu.VMEM((rows, state), F32), pltpu.VMEM((pairs, 8, rows), F32),
        ],
        us=16.3, name="mamba_backward",
    )(place, lens, per_head, zx, y, dog, b, c, state_in, later, skip, aux, *given)


def feed_forward(unit, x, ours, theirs, gains, dy, weights, into):
    rows, model = ours.shape
    total = x.shape[0]
    hidden = weights.shape[1] // 3
    blk = min(256, hidden)
    count = hidden // blk
    given = () if into is None else tuple(into)

    def body(x_ref, ours_ref, theirs_ref, gains_ref, dy_ref, ab_ref, down_ref, *rest):
        h1_ref, n2_ref, f_ref, dab_ref, dn2_ref, dn2_acc = rest[-6:]

        @pl.when(pl.program_id(0) == 0)
        def _():
            h1 = x_ref[...].astype(F32) + (ours_ref[...].astype(F32) + theirs_ref[...].astype(F32))
            scale = lax.rsqrt(jnp.mean(h1 * h1, axis=1, keepdims=True) + EPSILON)
            h1_ref[...] = h1
            n2_ref[...] = (h1 * scale * gains_ref[1:2, :]).astype(LOW)

        ab = nn_dot(n2_ref[...], ab_ref[...])
        a, b = ab[:, :blk], ab[:, blk:]
        sig = jax.nn.sigmoid(a)
        silu = a * sig
        f = (silu * b).astype(LOW)
        f_ref[...] = f
        df = nn_dot(dy_ref[...], down_ref[...])
        dab_ref[:, :blk] = (df * b * sig * (1.0 + a * (1.0 - sig))).astype(LOW)
        dab_ref[:, blk:] = (df * silu).astype(LOW)
        dn2 = nt_dot(dab_ref[...], ab_ref[...])

        @pl.when(pl.program_id(0) == 0)
        def _():
            dn2_acc[...] = dn2

        @pl.when(pl.program_id(0) > 0)
        def _():
            dn2_acc[...] += dn2

        @pl.when(pl.program_id(0) == count - 1)
        def _():
            dn2_ref[...] = dn2_acc[...].astype(LOW)

    at_unit = pl.BlockSpec((rows, model), lambda j: (unit, 0))
    return launch(
        body,
        grid=(count,),
        out_shape=(
            jax.ShapeDtypeStruct((total, model), F32), jax.ShapeDtypeStruct((total, model), LOW),
            jax.ShapeDtypeStruct((total, hidden), LOW), jax.ShapeDtypeStruct((total, 2 * hidden), LOW),
            jax.ShapeDtypeStruct((rows, model), LOW),
        ),
        in_specs=[
            at_unit, whole_spec((rows, model)), whole_spec((rows, model)), whole_spec((8, model)), at_unit,
            pl.BlockSpec((model, 2 * blk), lambda j: (0, j)), pl.BlockSpec((model, blk), lambda j: (0, 2 * count + j)),
        ] + anywhere(given),
        out_specs=[
            at_unit, at_unit, pl.BlockSpec((rows, blk), lambda j: (unit, j)), pl.BlockSpec((rows, 2 * blk), lambda j: (unit, j)),
            whole_spec((rows, model)),
        ],
        input_output_aliases={7: 0, 8: 1, 9: 2, 10: 3} if given else {},
        scratch_shapes=[pltpu.VMEM((rows, model), F32)],
        us=14, name="feed_forward",
    )(x, ours, theirs, gains, dy, weights, weights, *given)


def feed_forward_out(f, weights):
    total, hidden = f.shape
    model = weights.shape[0]
    blk = min(512, total)

    def body(f_ref, down_ref, *rest):
        rest[-1][...] = nt_dot(f_ref[...], down_ref[...]).astype(LOW)

    return launch(
        body,
        grid=(total // blk,),
        out_shape=jax.ShapeDtypeStruct((total, model), LOW),
        in_specs=[pl.BlockSpec((blk, hidden), lambda i: (i, 0)), pl.BlockSpec((model, hidden), lambda i: (0, 2))],
        out_specs=pl.BlockSpec((blk, model), lambda i: (i, 0)),
        us=5, name="feed_forward_out",
    )(f, weights)


def norm_gradient(hidden, gain, d_normed):
    inv = lax.rsqrt(jnp.mean(hidden * hidden, axis=1, keepdims=True) + EPSILON)
    weighted = gain * d_normed
    mean = jnp.mean(weighted * hidden, axis=1, keepdims=True)
    normed = hidden * inv
    return inv * weighted - normed * (inv * inv * mean), jnp.sum(d_normed * normed, axis=0, keepdims=True)


def middle_backward(unit, h1, ours, theirs, gains, dy, third, into):
    rows, model = ours.shape
    width = third.shape[1]
    given = () if into is None else (into,)

    def body(h1_ref, ours_ref, theirs_ref, gains_ref, dy_ref, third_ref, *rest):
        dm_ref, dh_ref, dog_ref, sum_ref = rest[-4:]
        dn2 = ours_ref[...].astype(F32) + theirs_ref[...].astype(F32)
        dh, terms = norm_gradient(h1_ref[...], gains_ref[1:2, :], dn2)
        dh = dh + dy_ref[...].astype(F32)
        dh_ref[...] = dh
        dm = dh.astype(LOW)
        dm_ref[...] = dm
        dog_ref[...] = nn_dot(dm, third_ref[...]).astype(LOW)
        sum_ref[...] = jnp.broadcast_to(terms, sum_ref.shape)

    at_unit = pl.BlockSpec((rows, model), lambda i: (unit, 0))
    full = whole_spec((rows, model))
    return launch(
        body,
        grid=(1,),
        out_shape=(
            jax.ShapeDtypeStruct(h1.shape, LOW), jax.ShapeDtypeStruct((rows, model), F32),
            jax.ShapeDtypeStruct((rows, width), LOW), jax.ShapeDtypeStruct((8, model), F32),
        ),
        in_specs=[at_unit, full, full, whole_spec((8, model)), at_unit, whole_spec((model, width))] + anywhere(given),
        out_specs=[at_unit, full, whole_spec((rows, width)), whole_spec((8, model))],
        input_output_aliases={6: 0} if given else {},
        us=5.4, name="middle_backward",
    )(h1, ours, theirs, gains, dy, third, *given)


def input_backward(unit, dq, keep, got, dbc, dzx, first, second, x, into):
    rows, q_dim = dq.shape
    model = first.shape[0]
    blk = 256 if model % 256 == 0 else model
    rest_width = dbc.shape[1]
    width = q_dim + keep.shape[-1]
    rest = first.shape[1] - width
    given = () if into is None else (into,)

    def body(dq_ref, keep_ref, got_ref, dbc_ref, dzx_ref, first_ref, second_ref, x_ref, *others):
        dqkv_ref, part_ref, sum_ref, inv = others[-4:]
        j = pl.program_id(0)

        @pl.when(j == 0)
        def _():
            x = x_ref[...].astype(F32)
            scale = lax.rsqrt(jnp.mean(x * x, axis=1, keepdims=True) + EPSILON)
            inv[...] = jnp.broadcast_to(scale, inv.shape)
            dqkv_ref[:, :q_dim] = dq_ref[...]
            dqkv_ref[:, q_dim:] = (keep_ref[0, 0].astype(F32) + got_ref[0, 0].astype(F32)).astype(LOW)

        part = nt_dot(dqkv_ref[...], first_ref[:, :width]) + nt_dot(dbc_ref[:, :rest], first_ref[:, width:])
        part = part + nt_dot(dzx_ref[...], second_ref[...])
        part_ref[...] = part.astype(LOW)
        x = x_ref[:, pl.ds(pl.multiple_of(j * blk, blk), blk)].astype(F32)
        terms = jnp.sum(part * x * inv[:, :1], axis=0, keepdims=True)
        sum_ref[...] = jnp.broadcast_to(terms, sum_ref.shape)

    return launch(
        body,
        grid=(model // blk,),
        out_shape=(
            jax.ShapeDtypeStruct((x.shape[0], width), LOW), jax.ShapeDtypeStruct((rows, model), LOW), jax.ShapeDtypeStruct((8, model), F32),
        ),
        in_specs=[
            whole_spec((rows, q_dim)), whole_spec(keep.shape), whole_spec(keep.shape), pl.BlockSpec((rows, rest_width), lambda j: (unit, 0)),
            pl.BlockSpec((rows, dzx.shape[1]), lambda j: (unit, 0)), pl.BlockSpec((blk, first.shape[1]), lambda j: (j, 0)),
            pl.BlockSpec((blk, second.shape[1]), lambda j: (j, 0)), pl.BlockSpec((rows, model), lambda j: (unit, 0)),
        ] + anywhere(given),
        out_specs=[
            pl.BlockSpec((rows, width), lambda j: (unit, 0)), pl.BlockSpec((rows, blk), lambda j: (0, j)),
            pl.BlockSpec((8, blk), lambda j: (0, j)),
        ],
        input_output_aliases={8: 0} if given else {},
        scratch_shapes=[pltpu.VMEM((rows, 128), F32)],
        us=6.5, name="input_backward",
    )(dq, keep, got, dbc, dzx, first, second, x, *given)


def finish(unit, x, ours, theirs, gains, dh, into):
    rows, model = ours.shape
    given = () if into is None else (into,)

    def body(x_ref, ours_ref, theirs_ref, gains_ref, dh_ref, *rest):
        dn1 = ours_ref[...].astype(F32) + theirs_ref[...].astype(F32)
        dx, _ = norm_gradient(x_ref[...].astype(F32), gains_ref[0:1, :], dn1)
        rest[-1][...] = dx + dh_ref[...]

    at_unit = pl.BlockSpec((rows, model), lambda i: (unit, 0))
    full = whole_spec((rows, model))
    return launch(
        body,
        grid=(1,),
        out_shape=jax.ShapeDtypeStruct(x.shape, F32),
        in_specs=[at_unit, full, full, whole_spec((8, model)), full] + anywhere(given),
        out_specs=at_unit,
        input_output_aliases={5: 0} if given else {},
        us=4.2, name="finish",
    )(x, ours, theirs, gains, dh, *given)


def pack(place, parts, cols, name):
    arrays = []
    for arr, *_ in parts:
        if not any(arr is other for other in arrays):
            arrays.append(arr)
    where = [next(i for i, other in enumerate(arrays) if other is part[0]) for part in parts]
    nc = lax.axis_size("context")
    rows = arrays[0].shape[1] if parts[0][4] else arrays[0].shape[0]
    filled = max(part[1] + part[2] for part in parts)

    def body(place_ref, *refs):
        out_ref, own_ref = refs[-2:]
        if filled < cols:
            start = filled - filled % 128
            out_ref[:, start:] = jnp.zeros((rows, cols - start), LOW)
        for n, (_, at, width, first, turned) in zip(where, parts):
            if turned:
                out_ref[:, at : at + width] = refs[n][...].T
            else:
                out_ref[:, at : at + width] = refs[n][:, first : first + width]
        own_ref[...] = out_ref[pl.ds(pl.multiple_of(place_ref[1] * (rows // nc), rows // nc), rows // nc), :]

    return launch(
        body, out_shape=(jax.ShapeDtypeStruct((rows, cols), LOW), jax.ShapeDtypeStruct((rows // nc, cols), LOW)),
        in_specs=[SCALARS] + [whole_spec(arr.shape) for arr in arrays],
        out_specs=[whole_spec((rows, cols)), whole_spec((rows // nc, cols))], name=name, us=2,
    )(place, *arrays)


def emit(place, held, got, outs, name):
    half, part, cols = held.shape
    nc = 2 * half
    rows = nc * part
    offsets = [reverse_bits(m) for m in range(nc)][:half]
    widths = [sum(width for _, width in pieces) for pieces, _ in outs]

    def body(place_ref, held_ref, got_ref, *refs):
        whole = refs[-1]
        ci = place_ref[1]
        for m, off in enumerate(offsets):
            for ref, bit in ((held_ref, 0), (got_ref, 1)):
                at = pl.multiple_of(lax.bitwise_xor(ci, off ^ bit) * part, part)
                whole[pl.ds(at, part), :] = ref[m].astype(F32)
        for ref, (pieces, turned) in zip(refs, outs):
            to = 0
            for first, width in pieces:
                if turned:
                    ref[to : to + width, :] = whole[:, first : first + width].T
                else:
                    ref[:, to : to + width] = whole[:, first : first + width]
                to += width

    shapes = [(width, rows) if turned else (rows, width) for width, (_, turned) in zip(widths, outs)]
    return launch(
        body, out_shape=tuple(jax.ShapeDtypeStruct(shape, F32) for shape in shapes),
        in_specs=[SCALARS, whole_spec(held.shape), whole_spec(held.shape)], out_specs=[whole_spec(shape) for shape in shapes],
        scratch_shapes=[pltpu.VMEM((rows, cols), F32)], name=name, us=3,
    )(place, held, got)


def close_forward(h1, ours, theirs):
    total, model = h1.shape
    blk = min(256, total)

    def body(h1_ref, ours_ref, theirs_ref, out_ref):
        out_ref[...] = (h1_ref[...] + (ours_ref[...].astype(F32) + theirs_ref[...].astype(F32))).astype(LOW)

    spec = pl.BlockSpec((blk, model), lambda i: (i, 0))
    return launch(
        body, grid=(total // blk,), out_shape=jax.ShapeDtypeStruct((total, model), LOW), in_specs=[spec] * 3, out_specs=spec,
        name="close_forward", us=4,
    )(h1, ours, theirs)


def project_mixer(n1, second):
    tokens, model = n1.shape
    cols = second.shape[1]
    blk = column_block(cols)

    def body(n1_ref, second_ref, out_ref):
        out_ref[...] = nn_dot(n1_ref[...], second_ref[...]).astype(LOW)

    return launch(
        body, grid=(cols // blk,), out_shape=jax.ShapeDtypeStruct((tokens, cols), LOW),
        in_specs=[whole_spec((tokens, model)), pl.BlockSpec((model, blk), lambda j: (0, j))],
        out_specs=pl.BlockSpec((tokens, blk), lambda j: (0, j)), name="project_mixer", us=5,
    )(n1, second)


def mixer_out(unit, og, third, rows):
    width = og.shape[1]
    model = third.shape[0]
    blk = column_block(model)

    def body(og_ref, third_ref, out_ref):
        out_ref[...] = nt_dot(og_ref[...], third_ref[...]).astype(LOW)

    return launch(
        body, grid=(model // blk,), out_shape=jax.ShapeDtypeStruct((rows, model), LOW),
        in_specs=[pl.BlockSpec((rows, width), lambda j: (unit, 0)), pl.BlockSpec((blk, width), lambda j: (j, 0))],
        out_specs=pl.BlockSpec((rows, blk), lambda j: (0, j)), name="mixer_out", us=2,
    )(og, third)


def turns(first, second, width):
    count = first.shape[-1] // width
    parts = [arr[..., width * i : width * (i + 1)] for i in range(count) for arr in (first, second)]
    return jnp.concatenate(parts, axis=-1)


def unturned(mixed, width, which):
    count = mixed.shape[-1] // (2 * width)
    return jnp.concatenate([mixed[..., width * (2 * i + which) : width * (2 * i + which + 1)] for i in range(count)], axis=-1)


def per_device(
    tokens, cotangent, doc_lengths, mixer_gain, w_query, key_matrix, value_matrix, mamba_gate_weight,
    mamba_input_weight, w_bproj, w_cproj, w_dt, a_log, dt_bias, d_skip, w_attn_out, w_mixer_out,
    ffn_gain, w_gate, w_up, w_down,
):
    CHAIN.clear()
    micro_count, seq_count, block_len, model_dim = tokens.shape
    rows_here = mixer_gain.shape[0]
    heads = w_dt.shape[1]
    ssm_dim = mamba_gate_weight.shape[1]
    head_dim = ssm_dim // heads
    q_dim = w_query.shape[1]
    kv_dim = key_matrix.shape[1]
    state_dim = w_bproj.shape[1]
    ff_dim = w_gate.shape[1]
    ff_blk = min(256, ff_dim)
    ci = lax.axis_index("context")
    nc = lax.axis_size("context")
    full_len = nc * block_len
    units = micro_count * seq_count
    pairs = heads // 2
    tokens_here = units * block_len
    at_b = q_dim + 2 * kv_dim
    at_c = at_b + state_dim
    at_dt = at_c + state_dim
    at_gain = at_dt + heads
    first_width = at_gain + 2 + -(at_gain + 2) % 128

    place = jnp.stack([lax.axis_index("fsdp"), ci]).astype(jnp.int32)
    at_k, at_v = q_dim, q_dim + kv_dim
    two = 2 * head_dim
    first, own_first = pack(
        place,
        [(w_query, 0, q_dim, 0, False), (key_matrix, at_k, kv_dim, 0, False), (value_matrix, at_v, kv_dim, 0, False),
         (w_bproj, at_b, state_dim, 0, False), (w_cproj, at_c, state_dim, 0, False), (w_dt, at_dt, heads, 0, False),
         (jnp.stack([mixer_gain, ffn_gain], axis=1), at_gain, 2, 0, False)],
        first_width, "pack_first")
    near_first = send_near(own_first)
    second, own_second = pack(
        place,
        [(arr, (2 * i + n) * two, two, i * two, False)
         for i in range(pairs) for n, arr in enumerate((mamba_gate_weight, mamba_input_weight))],
        2 * ssm_dim, "pack_second")
    third, own_third = pack(
        place, [(w_attn_out, 0, q_dim, 0, True), (w_mixer_out, q_dim, ssm_dim, 0, True)], q_dim + ssm_dim, "pack_third")
    fourth, own_fourth = pack(
        place,
        [(arr, (2 * i + n) * ff_blk, ff_blk, i * ff_blk, False) for i in range(ff_dim // ff_blk) for n, arr in enumerate((w_gate, w_up))]
        + [(w_down, 2 * ff_dim, ff_dim, 0, True)],
        3 * ff_dim, "pack_fourth")
    lens = doc_lengths.reshape(units, -1)
    aux = jnp.pad(jnp.stack([a_log, dt_bias], axis=1), ((0, 16 - heads), (0, 0)))
    skip_row = jnp.repeat(d_skip, head_dim)[None]
    tokens = tokens.reshape(tokens_here, model_dim)
    cotangent = cotangent.reshape(tokens_here, model_dim)
    width = q_dim + ssm_dim

    def placed(shard, mine, other):
        return place_rows(place, shard.reshape(nc, -1, shard.shape[1]), mine, other)

    held_first = join(near_first, True)
    wait_for(held_first)
    near_second = send_near(own_second)
    held_first = spread_far(held_first)
    core_first = swap_context(held_first, 1)
    first = placed(first, held_first, core_first)
    wait_for(*near_second)
    n1, q, kv, b, c, per_head, gains = project(place, lens, tokens, first, aux, q_dim, kv_dim, state_dim, pairs)
    kv = kv.reshape(1, units, block_len, 2 * kv_dim)
    kv_far = [swap_context(kv, bit) for bit in far_bits()[:1]]
    held_second = join(near_second, True)
    near_third = send_near(own_third)
    kv_held = join([kv, *kv_far], False)
    for bit in far_bits()[1:]:
        kv_held = join([kv_held, swap_context(kv_held, bit)], False)
    kv_all = place_blocks(place, kv_held, swap_context(kv_held, 1))
    wait_for(*near_third)
    og, lse = None, [None] * units
    og, lse[0] = attention_forward(0, place, lens, q, kv_all, og, width)
    near_fourth = send_near(own_fourth)
    held_second = spread_far(held_second)
    held_third = join(near_third, True)
    second = placed(second, held_second, swap_context(held_second, 1))
    zx = project_mixer(n1, second)
    span = join([mamba_state(u, per_head, b, zx) for u in range(units)], True)[None]
    span_far = [swap_context(span, bit) for bit in far_bits()[:1]]
    held_fourth = join(near_fourth, True)
    for u in range(1, units):
        og, lse[u] = attention_forward(u, place, lens, q, kv_all, og, width)
    span = join([span, *span_far], False)
    for bit in far_bits()[1:]:
        span = join([span, swap_context(span, bit)], False)
    spans = (span, swap_context(span, 1))
    held_third = spread_far(held_third)
    core_third = swap_context(held_third, 1)
    state = chain_states(place, spans, state_dim)
    third = placed(third, held_third, core_third)
    og, y_u = mamba_forward(0, place, lens, per_head, zx, b, c, state, skip_row, og, q_dim)
    y, ours = [y_u], [mixer_out(0, og, third, block_len)]
    theirs = [swap_tensor(ours[0])]
    held_fourth = spread_far(held_fourth)
    core_fourth = swap_context(held_fourth, 1)
    for u in range(1, units):
        og, y_u = mamba_forward(u, place, lens, per_head, zx, b, c, state, skip_row, og, q_dim)
        y.append(y_u)
        ours.append(mixer_out(u, og, third, block_len))
        theirs.append(swap_tensor(ours[u]))
    fourth = placed(fourth, held_fourth, core_fourth)

    stacked, dn2, dn2_theirs = None, [], []
    for u in range(units):
        *stacked, dn2_u = feed_forward(u, tokens, ours[u], theirs[u], gains, cotangent, fourth, stacked)
        dn2.append(dn2_u)
        dn2_theirs.append(swap_tensor(dn2_u))
    h1, n2, f, dab = stacked
    wide = 3 * ff_dim
    away, keep_fourth = outer(place, n2, dab, None, 0, wide)
    wait_for(dn2_theirs[0])
    away, keep_fourth = outer(place, cotangent, f, (away, keep_fourth), 2 * ff_dim, wide)
    got_fourth = swap_context(away, 1)

    dm, dh, dog, d_span, local = None, [], [], [], []
    g_gain_two = 0.0
    d_second, dq, dkv, head_grads = None, [None] * units, [None] * units, 0.0
    bits = context_bits()[1:]

    def open_backward(u, dm):
        dm, dh_u, dog_u, terms = middle_backward(u, h1, dn2[u], dn2_theirs[u], gains, cotangent, third, dm)
        dh.append(dh_u)
        dog.append(dog_u)
        local.append(mamba_state(u, per_head, c, zx, dog_u, q_dim)[None, None])
        return dm, terms[0]

    def attend_back(u):
        dq[u], away, keep = attention_backward(u, place, lens, q, dog[u], og, kv_all, lse[u])
        return keep, swap_context(away, 1)

    def close_states(u):
        held = spread_far(local[u])
        return held, swap_context(held, 1)

    def to_owners(keep, got):
        own, *away = split_fsdp(place, keep, got)
        return [own] + [from_next(arr, "fsdp", k + 1) for k, arr in enumerate(away)]

    def share(total):
        held = spread_far(total[None])
        return held, swap_context(held, 1)

    for u in range(units - 1):
        dm, terms = open_backward(u, dm)
        g_gain_two = g_gain_two + terms
        kept = attend_back(u)
        pair = close_states(u)
        if u == 0:
            keep_fourth, got_fourth = reduce_far(place, keep_fourth, got_fourth, bits)
        dkv[u] = reduce_far(place, *kept, bits)
        d_span.append(chain_states(place, spans, state_dim, pair, u)[0])
    dm, terms = open_backward(units - 1, dm)
    g_gain_two = g_gain_two + terms
    ff = feed_forward_out(f, fourth)
    ff_theirs = swap_tensor(ff)
    wide = q_dim + ssm_dim
    away, keep_third = outer(place, dm, og, None, 0, wide)
    got_third = swap_context(away, 1)
    for u in range(units):
        if u == units - 1:
            pair = close_states(u)
            keep_third, got_third = reduce_far(place, keep_third, got_third, bits)
            parts_fourth = to_owners(keep_fourth, got_fourth)
            d_span.append(chain_states(place, spans, state_dim, pair, u)[0])
        *d_second, grads_u = mamba_backward(
            u, place, lens, per_head, zx, y[u], dog[u], q_dim, b, c, state, d_span[u], skip_row, aux, d_second)
        head_grads = head_grads + grads_u
    dzx, dbc = d_second
    at_rest = 2 * ssm_dim
    wide = at_rest + dbc.shape[1]
    pair = outer(place, n1, dzx, None, 0, wide)
    wait_for(*parts_fourth)
    away, keep_second = outer(place, n1, dbc, pair, at_rest, wide)
    got_second = swap_context(away, 1)
    parts_third = to_owners(keep_third, got_third)
    parts, parts_theirs, g_gain_one, dqkv = [None] * units, [None] * units, 0.0, None

    def close_backward(u, dqkv):
        dqkv, parts[u], terms = input_backward(u, dq[u], *dkv[u], dbc, dzx, first, second, tokens, dqkv)
        parts_theirs[u] = swap_tensor(parts[u])
        return dqkv, terms[0]

    for u in range(units - 1):
        dqkv, terms = close_backward(u, dqkv)
        g_gain_one = g_gain_one + terms
    g_fourth = sum_parts(parts_fourth)
    keep_second, got_second = reduce_far(place, keep_second, got_second, bits)
    kept = attend_back(units - 1)
    head_grads = all_sum(head_grads[:heads, :3])
    dkv[units - 1] = reduce_far(place, *kept, bits)
    g_third = sum_parts(parts_third)
    layer_out = close_forward(h1, ff, ff_theirs)
    dqkv, terms = close_backward(units - 1, dqkv)
    g_gain_one = g_gain_one + terms
    g_gains = jnp.pad(jnp.stack([g_gain_one, g_gain_two], axis=1).astype(LOW), ((0, 0), (0, 126)))
    wide = at_b + 128
    away, keep_first = outer(place, n1, dqkv, None, 0, wide)
    g_gains = g_gains.reshape((lax.axis_size("fsdp"), nc // 2, 2, -1, 128))
    mine = ci % 2
    away = away.at[..., at_b:].set(lax.dynamic_index_in_dim(g_gains, 1 - mine, 2, keepdims=False))
    keep_first = keep_first.at[..., at_b:].set(lax.dynamic_index_in_dim(g_gains, mine, 2, keepdims=False))
    got_first = swap_context(away, 1)
    parts_second = to_owners(keep_second, got_second)
    keep_first, got_first = reduce_far(place, keep_first, got_first, bits)
    fourth_pair = share(g_fourth)
    third_pair = share(g_third)
    parts_first = to_owners(keep_first, got_first)
    input_grads = None
    for u in range(units - 1):
        input_grads = finish(u, tokens, parts[u], parts_theirs[u], gains, dh[u], input_grads)

    def columns(first, width, turned=False):
        return [(first, width)], turned

    def in_turns(which, width, total):
        return [(width * (2 * i + which), width) for i in range(total // width)], False

    g_gate, g_up, g_down = emit(
        place, *fourth_pair,
        [in_turns(0, ff_blk, ff_dim), in_turns(1, ff_blk, ff_dim), columns(2 * ff_dim, ff_dim, True)], "emit_fourth")
    g_attn, g_mixer = emit(place, *third_pair, [columns(0, q_dim, True), columns(q_dim, ssm_dim, True)], "emit_third")
    g_second = sum_parts(parts_second, (at_rest, at_rest + 2 * state_dim))
    g_first = sum_parts(parts_first)
    lane = jnp.arange(128)[None]
    g_gains = g_first[:, at_b:]
    g_gains = jnp.where(lane == 0, (g_gains.astype(F32) + swap_tensor(g_gains).astype(F32)).astype(LOW), g_gains)
    g_first = jnp.concatenate([g_first[:, :at_b], g_gains], axis=1)
    u = units - 1
    input_grads = finish(u, tokens, parts[u], parts_theirs[u], gains, dh[u], input_grads)
    g_z, g_x, g_b, g_c, g_dt = emit(
        place, *share(g_second),
        [in_turns(0, two, ssm_dim), in_turns(1, two, ssm_dim), columns(at_rest, state_dim),
         columns(at_rest + state_dim, state_dim), columns(at_rest + 2 * state_dim, heads)], "emit_second")
    g_q, g_k, g_v, g_gains = emit(
        place, *share(g_first),
        [columns(0, q_dim), columns(at_k, kv_dim), columns(at_v, kv_dim), columns(at_b, 128)], "emit_first")
    shape = (micro_count, seq_count, block_len, model_dim)
    return (
        layer_out.reshape(shape), input_grads.reshape(shape), g_gains[:, 0], g_q, g_k, g_v, g_z, g_x, g_b, g_c, g_dt,
        head_grads[:, 0], head_grads[:, 1], head_grads[:, 2], g_attn, g_mixer, g_gains[:, 1], g_gate, g_up, g_down,
    )


def solution(mesh):
    rows, cols = P("fsdp", "tensor"), P("tensor", "fsdp")
    acts = P(None, "fsdp", "context", None)
    return jax.shard_map(
        per_device,
        mesh=mesh,
        in_specs=(
            acts, acts, P(None, "fsdp", None), P("fsdp"), rows, rows, rows, rows, rows, P("fsdp", None),
            P("fsdp", None), rows, P("tensor"), P("tensor"), P("tensor"), cols, cols, P("fsdp"), rows, rows, cols,
        ),
        out_specs=(
            acts, acts, P("fsdp"), rows, rows, rows, rows, rows, P("fsdp", None), P("fsdp", None), rows,
            P("tensor"), P("tensor"), P("tensor"), cols, cols, P("fsdp"), rows, rows, cols,
        ),
        check_vma=False,
    )
```

```python
import jax
import jax.numpy as jnp
from jax import lax
from jax.experimental import pallas as pl
from jax.experimental.pallas import tpu as pltpu
from jax.sharding import PartitionSpec as P

HEAD_WIDTH = 64
EPSILON = 1e-06
LOW = jnp.bfloat16
F32 = jnp.float32
NEGATIVE = -1e30
PRECISE = lax.Precision.HIGHEST


def swap_context(x, bit):
    size = lax.axis_size("context")
    return lax.ppermute(x, "context", [(i, i ^ bit) for i in range(size)])


def from_next(x, axis, step=1):
    size = lax.axis_size(axis)
    return lax.ppermute(x, axis, [((i + step) % size, i) for i in range(size)])


def swap_tensor(x):
    size = lax.axis_size("tensor")
    return lax.ppermute(x, "tensor", [(i, (i + 1) % size) for i in range(size)])


def context_bits():
    size = lax.axis_size("context")
    return [1 << k for k in range(size.bit_length() - 1)]


def reverse_bits(index):
    bits = context_bits()
    return sum(((index // low) % 2) * high for low, high in zip(bits, reversed(bits)))


CHAIN = []
SCALE = 0.4e9


def anywhere(arrays):
    return [pl.BlockSpec(memory_space=pl.ANY)] * len(arrays)


def whole_spec(shape):
    return pl.BlockSpec(shape, lambda i: (0,) * len(shape))


def pair_spec(rows):
    return pl.BlockSpec((rows, 128), lambda i: (0, i))


SCALARS = pl.BlockSpec(memory_space=pltpu.SMEM)


def wait_for(*arrays):
    CHAIN.extend(arrays)


def launch(body, *, out_shape, in_specs, out_specs, name, us, grid=(1,), scratch_shapes=(), input_output_aliases=None):
    single = not isinstance(out_shape, tuple)
    outs = (out_shape,) if single else out_shape
    specs = [out_specs] if single else list(out_specs)

    def call(*args):
        waits = tuple(CHAIN)
        n_in, n_out = len(args), len(outs)
        at = n_in + len(waits)

        def run(*refs):
            body(*refs[:n_in], *refs[at : at + n_out], *refs[at + n_out + 1 :])

        made = pl.pallas_call(
            run,
            grid=grid,
            out_shape=outs + (jax.ShapeDtypeStruct((8, 128), F32),),
            in_specs=list(in_specs) + anywhere(waits),
            out_specs=specs + anywhere((0,)),
            scratch_shapes=list(scratch_shapes),
            input_output_aliases=input_output_aliases or {},
            compiler_params=pltpu.CompilerParams(vmem_limit_bytes=(60 if name.startswith("pack") else 18 if name in ("feed_forward", "outer") else 10) * 2**20),
            cost_estimate=pl.CostEstimate(flops=int(us * SCALE), bytes_accessed=1, transcendentals=0),
            name=name,
        )(*args, *waits)
        CHAIN[:] = made[-1:]
        return made[0] if single else made[:-1]

    return call


def column_block(cols):
    return next(blk for blk in (512, 256, 128) if cols % blk == 0)


def join(parts, axis_new, splits=1):
    if axis_new:
        parts = [part[None] for part in parts]
    counts = [part.shape[0] for part in parts]
    shape = parts[0].shape[1:]
    cols = shape[-1]
    blk = column_block(cols)

    def spec(count):
        return pl.BlockSpec((count, *shape[:-1], blk), lambda j: (0,) * len(shape) + (j,))

    def body(*refs):
        outs = refs[len(counts) :]
        width = blk // len(outs)
        at = 0
        for ref, count in zip(refs, counts):
            for n, out in enumerate(outs):
                out[at : at + count] = ref[..., n * width : (n + 1) * width]
            at += count

    if splits > 1:
        blk = cols
        out = (sum(counts), *shape[:-1], cols // splits)
        return launch(
            body, out_shape=(jax.ShapeDtypeStruct(out, parts[0].dtype),) * splits, in_specs=[spec(count) for count in counts],
            out_specs=[whole_spec(out)] * splits, name="join", us=3,
        )(*parts)
    return launch(
        body, grid=(cols // blk,), out_shape=jax.ShapeDtypeStruct((sum(counts), *shape), parts[0].dtype),
        in_specs=[spec(count) for count in counts], out_specs=spec(sum(counts)), name="join", us=2,
    )(*parts)


def send_near(own, ring=False):
    got = []
    for k in range(1, lax.axis_size("fsdp")):
        got.append(from_next(got[-1] if ring and got else own, "fsdp", 1 if ring else k))
    return got


def far_bits():
    return list(reversed(context_bits()[1:]))


def spread_far(held, splits=1):
    for bit in far_bits():
        held = join([held, swap_context(held, bit)], False, splits if bit == far_bits()[-1] else 1)
    return held


def place_rows(place, shard, mine, other):
    nc, part, cols = shard.shape
    nf = lax.axis_size("fsdp")
    offsets = [reverse_bits(m) for m in range(nc)][: nc // 2]
    pieces = len(mine)
    blk = column_block(cols // pieces)
    steps = cols // pieces // blk

    def body(place_ref, shard_ref, *refs):
        out_ref = refs[-1]
        fi, ci = place_ref[0], place_ref[1]
        out_ref[fi] = shard_ref[...]

        def fill(mine_ref, other_ref):
            for k in range(1, nf):
                z = lax.rem(fi + k, nf)
                for m, off in enumerate(offsets):
                    at = m * (nf - 1) + k - 1
                    out_ref[z, lax.bitwise_xor(ci, off)] = mine_ref[at]
                    out_ref[z, lax.bitwise_xor(ci, off ^ 1)] = other_ref[at]

        for n in range(pieces):
            pl.when(pl.program_id(0) // steps == n)(lambda n=n: fill(refs[n], refs[pieces + n]))

    def columns(*leading):
        return pl.BlockSpec((*leading, blk), lambda j: (0,) * len(leading) + (j,))

    def piece(n):
        return pl.BlockSpec((count, part, blk), lambda j: (0, 0, jnp.clip(j - n * steps, 0, steps - 1)))

    count = mine[0].shape[0]
    full = launch(
        body,
        grid=(cols // blk,),
        out_shape=jax.ShapeDtypeStruct((nf, nc, part, cols), shard.dtype),
        in_specs=[SCALARS, columns(nc, part)] + [piece(n) for n in range(pieces)] * 2,
        out_specs=columns(nf, nc, part),
        name="place_rows",
        us=cols / 600,
    )(place, shard, *mine, *other)
    return full.reshape(nf * nc * part, cols)


def place_blocks(place, mine, other):
    half, units, rows, cols = mine.shape
    nc = 2 * half
    offsets = [reverse_bits(m) for m in range(nc)][:half]

    def body(place_ref, mine_ref, other_ref, out_ref):
        ci = place_ref[1]
        for u in range(units):
            for m, off in enumerate(offsets):
                for ref, bit in ((mine_ref, 0), (other_ref, 1)):
                    at = pl.multiple_of(lax.bitwise_xor(ci, off ^ bit) * rows, rows)
                    out_ref[u, pl.ds(at, rows), :] = ref[m, u]

    return launch(
        body,
        out_shape=jax.ShapeDtypeStruct((units, nc * rows, cols), mine.dtype),
        in_specs=[SCALARS, whole_spec(mine.shape), whole_spec(other.shape)],
        out_specs=whole_spec((units, nc * rows, cols)),
        name="place_blocks",
        us=1,
    )(place, mine, other)


def at_offset(ref_pair, ci, k, nc):
    off = lax.bitwise_xor(ci, k)
    entry, weight, rest = 0, nc // 2, off
    half = lax.div(off, 2)
    width = nc // 2
    index, bit = 0, width // 2
    low = 1
    while bit:
        index = index + lax.rem(lax.div(half, low), 2) * bit
        bit, low = bit // 2, low * 2
    same = lax.rem(off, 2) == 0
    mine, other = ref_pair
    return index, same, mine, other


def chain_states(place, spans, state_dim, local=None, unit=None):
    half, units, height, width = spans[0].shape
    nc = 2 * half
    blk = column_block(width)
    count = units if local is None else 1
    extra = () if local is None else tuple(local)

    def body(place_ref, *refs):
        ci = place_ref[1]
        out_ref = refs[-1]
        for n in range(count):
            u = n if local is None else unit
            total = jnp.zeros((state_dim, blk), F32)
            for k in range(nc - 1) if local is None else range(nc - 1, 0, -1):
                index, same, mine, other = at_offset(refs[:2], ci, k, nc)
                passing = jnp.where(same, mine[index, u, state_dim:].astype(F32), other[index, u, state_dim:].astype(F32))
                if local is None:
                    term = jnp.where(same, mine[index, u, :state_dim].astype(F32), other[index, u, :state_dim].astype(F32))
                    active = k < ci
                else:
                    term = jnp.where(same, refs[2][index, 0].astype(F32), refs[3][index, 0].astype(F32))
                    active = k > ci
                new = (passing[0:1] + passing[1:2]) * total + term
                total = jnp.where(active, new, total)
            out_ref[n] = total.astype(LOW)

    def columns(shape):
        return pl.BlockSpec((*shape[:-1], blk), lambda j: (0,) * (len(shape) - 1) + (j,))

    out = (count, state_dim, width)
    return launch(
        body,
        grid=(width // blk,),
        out_shape=jax.ShapeDtypeStruct(out, LOW),
        in_specs=[SCALARS] + [columns(arr.shape) for arr in (*spans, *extra)],
        out_specs=columns(out),
        name="chain_states",
        us=1.2,
    )(place, *spans, *extra)


def outer(place, left, right, into, at, width, last=None):
    nf, nc = lax.axis_size("fsdp"), lax.axis_size("context")
    tokens, model = left.shape
    cols = right.shape[1]
    part = model // (nf * nc)
    blk = next(b for b in (512, 256, 128) if cols % b == 0 and at % b == 0)
    given = () if into is None else tuple(into)
    lasts = () if last is None else (last,)

    def body(place_ref, left_ref, right_ref, *rest):
        away_ref, keep_ref, turned, made = rest[-4:]

        @pl.when(pl.program_id(0) == 0)
        def _():
            turned[...] = left_ref[...].T

        made[...] = nn_dot(turned[...], right_ref[...])
        if lasts:

            @pl.when(pl.program_id(0) == cols // blk - 1)
            def _():
                for top in range(0, model, part):
                    made[top : top + 8, blk - 128 :] = rest[len(given)][...]

        mine = lax.rem(place_ref[1], 2)
        for z in range(nf):
            for x in range(nc // 2):
                first = (z * nc + 2 * x) * part
                keep_ref[z, x] = made[pl.ds(pl.multiple_of(first + mine * part, part), part), :].astype(LOW)
                away_ref[z, x] = made[pl.ds(pl.multiple_of(first + (1 - mine) * part, part), part), :].astype(LOW)

    shape = jax.ShapeDtypeStruct((nf, nc // 2, part, width), LOW)
    spec = pl.BlockSpec((nf, nc // 2, part, blk), lambda j: (0, 0, 0, at // blk + j))
    return launch(
        body,
        grid=(cols // blk,),
        out_shape=(shape, shape),
        in_specs=[SCALARS, whole_spec((tokens, model)), pl.BlockSpec((tokens, blk), lambda j: (0, j))]
        + anywhere(given) + [whole_spec((8, 128)) for _ in lasts],
        out_specs=[spec, spec],
        input_output_aliases={3: 0, 4: 1} if given else {},
        scratch_shapes=[pltpu.VMEM((model, tokens), LOW), pltpu.VMEM((model, blk), F32)],
        name="outer",
        us=cols / 230,
    )(place, left, right, *given, *lasts)


def split_sum(place, keep, got, bit):
    n, left, rows, cols = keep.shape
    blk = column_block(cols)

    def body(place_ref, keep_ref, got_ref, away_ref, stay_ref):
        mine = lax.rem(lax.div(place_ref[1], bit), 2)
        for z in range(n):
            for j in range(left // 2):
                for ref, b in ((stay_ref, mine), (away_ref, 1 - mine)):
                    i = 2 * j + b
                    ref[z, j] = (keep_ref[z, i].astype(F32) + got_ref[z, i].astype(F32)).astype(LOW)

    def spec(count):
        return pl.BlockSpec((n, count, rows, blk), lambda j: (0, 0, 0, j))

    shape = jax.ShapeDtypeStruct((n, left // 2, rows, cols), LOW)
    return launch(
        body, grid=(cols // blk,), out_shape=(shape, shape), in_specs=[SCALARS, spec(left), spec(left)],
        out_specs=[spec(left // 2)] * 2, name="split_sum", us=cols / 900,
    )(place, keep, got)


def split_fsdp(place, keep, got):
    nf, _, part, cols = keep.shape
    blk = column_block(cols)

    def body(place_ref, keep_ref, got_ref, *outs):
        for k in range(nf):
            z = lax.rem(place_ref[0] + (nf - k), nf)
            outs[k][...] = (keep_ref[z, 0].astype(F32) + got_ref[z, 0].astype(F32)).astype(LOW)

    spec = pl.BlockSpec((nf, 1, part, blk), lambda j: (0, 0, 0, j))
    return launch(
        body, grid=(cols // blk,), out_shape=(jax.ShapeDtypeStruct((part, cols), LOW),) * nf, in_specs=[SCALARS, spec, spec],
        out_specs=[pl.BlockSpec((part, blk), lambda j: (0, j))] * nf, name="split_fsdp", us=cols / 1200,
    )(place, keep, got)


def ring_step(got, own):
    part, cols = own.shape
    blk = column_block(cols)

    def body(got_ref, own_ref, out_ref):
        out_ref[...] = (got_ref[...].astype(F32) + own_ref[...].astype(F32)).astype(LOW)

    spec = pl.BlockSpec((part, blk), lambda j: (0, j))
    return launch(
        body, grid=(cols // blk,), out_shape=jax.ShapeDtypeStruct((part, cols), LOW), in_specs=[spec, spec], out_specs=spec,
        name="ring_step", us=1,
    )(got, own)


def share_columns(total, first, last):
    mid = total[:, first:last]
    mid = (mid.astype(F32) + swap_tensor(mid).astype(F32)).astype(LOW)
    return jnp.concatenate([total[:, :first], mid, total[:, last:]], axis=1)


def sum_parts(parts, shared=(), ordered=None):
    cols = parts[0].shape[1]
    blk = column_block(cols)
    given = () if ordered is None else (ordered,)
    nf = len(parts)

    def body(*refs):
        some = refs[len(given) : -1]
        total = some[0][...].astype(F32)
        for ref in some[1:]:
            total = total + ref[...].astype(F32)
        refs[-1][...] = total.astype(LOW)
        if given:

            @pl.when(pl.program_id(0) == cols // blk - 1)
            def _():
                total = None
                for z in range(nf):
                    k = lax.rem(z + nf - refs[0][0], nf)
                    value = some[0][:, blk - 128 :].astype(F32)
                    for n in range(1, nf):
                        value = jnp.where(k == n, some[n][:, blk - 128 :].astype(F32), value)
                    total = value if total is None else total + value
                refs[-1][:, blk - 128 :] = total.astype(LOW)

    spec = pl.BlockSpec((parts[0].shape[0], blk), lambda j: (0, j))
    total = launch(
        body, grid=(cols // blk,), out_shape=jax.ShapeDtypeStruct(parts[0].shape, LOW),
        in_specs=[SCALARS] * len(given) + [spec] * nf, out_specs=spec, name="sum_parts", us=1.3,
    )(*given, *parts)
    if shared:
        mid = total[:, shared[0] : shared[1]]
        mid = (mid.astype(F32) + swap_tensor(mid).astype(F32)).astype(LOW)
        total = jnp.concatenate([total[:, : shared[0]], mid, total[:, shared[1] :]], axis=1)
    return total


def share_rows(total):
    held = total[None]
    for bit in reversed(context_bits()):
        held = jnp.concatenate([held, swap_context(held, bit)])
    ci = lax.axis_index("context")
    order = [reverse_bits(k) ^ reverse_bits(ci) for k in range(lax.axis_size("context"))]
    rows = jnp.stack([lax.dynamic_index_in_dim(held, m, 0, keepdims=False) for m in order])
    return rows.astype(F32).reshape(-1, total.shape[1])


def reduce_far(place, keep, got, bits):
    for bit in bits:
        away, keep = split_sum(place, keep, got, bit)
        got = swap_context(away, bit)
    return keep, got


def nt_dot(left, right):
    return lax.dot_general(left, right, (((1,), (1,)), ((), ())), preferred_element_type=F32)


def tn_dot(left, right):
    return lax.dot_general(left, right, (((0,), (0,)), ((), ())), preferred_element_type=F32)


def nn_dot(left, right):
    return jnp.dot(left, right, preferred_element_type=F32)


def document_start(lens_ref, unit, position):
    start, end = jnp.zeros_like(position), 0
    for d in range(lens_ref.shape[1]):
        end = end + lens_ref[unit, d]
        start = jnp.where(position >= end, end, start)
    return start


def lower_from(rows):
    u = lax.broadcasted_iota(jnp.int32, (rows, rows), 0)
    t = lax.broadcasted_iota(jnp.int32, (rows, rows), 1)
    return jnp.where(u <= t, 1.0, 0.0)


def project(place, lens, tokens, first, aux, q_dim, kv_dim, state, pairs):
    units = lens.shape[0]
    total, model = tokens.shape
    rows = total // units
    width = first.shape[1]
    at_b = q_dim + 2 * kv_dim
    at_dt = at_b + 2 * state

    def body(place_ref, lens_ref, x_ref, first_ref, aux_ref, n1_ref, q_ref, kv_ref, b_ref, c_ref, head_ref, gains_ref):
        unit = pl.program_id(0)

        @pl.when(unit == 0)
        def _():
            gains_ref[...] = first_ref[:, at_dt:].astype(F32).T[2 * pairs : 2 * pairs + 8]

        x = x_ref[...].astype(F32)
        scale = lax.rsqrt(jnp.mean(x * x, axis=1, keepdims=True) + EPSILON)
        n1_ref[...] = (x * scale * gains_ref[0:1, :]).astype(LOW)
        made = nn_dot(n1_ref[...], first_ref[...])
        q_ref[...] = (made[:, :q_dim].astype(LOW).astype(F32) * 0.125).astype(LOW)
        kv_ref[...] = made[:, q_dim:at_b].astype(LOW)
        b_ref[...] = made[:, at_b : at_b + state].astype(LOW)
        c_ref[...] = made[:, at_b + state : at_dt].astype(LOW)
        raw = made[:, at_dt:].T[:16] + aux_ref[:, 1:2]
        dt = jnp.maximum(raw, 0.0) + jnp.log1p(jnp.exp(-jnp.abs(raw)))
        decay = jnp.dot(-jnp.exp(aux_ref[:, 0:1]) * dt, lower_from(rows), precision=PRECISE, preferred_element_type=F32)
        base = place_ref[1] * rows
        position = base + lax.broadcasted_iota(jnp.int32, (1, rows), 1)
        carried = document_start(lens_ref, unit, position) < base
        closing = position >= document_start(lens_ref, unit, base + rows - 1)
        entering = jnp.where(carried, jnp.exp(decay), 0.0)
        leaving = jnp.where(closing, jnp.exp(decay[:, rows - 1 :] - decay), 0.0)
        for i in range(pairs):
            for at, value in enumerate((decay, dt, entering, leaving)):
                head_ref[i, 2 * at : 2 * at + 2, :] = value[2 * i : 2 * i + 2]

    def of_unit(cols):
        return pl.BlockSpec((rows, cols), lambda u: (u, 0))

    def made_as(cols):
        return jax.ShapeDtypeStruct((total, cols), LOW)

    return launch(
        body,
        grid=(units,),
        out_shape=(
            made_as(model), made_as(q_dim), made_as(2 * kv_dim), made_as(state), made_as(state),
            jax.ShapeDtypeStruct((units, pairs, 8, rows), F32), jax.ShapeDtypeStruct((8, model), F32),
        ),
        in_specs=[SCALARS, SCALARS, of_unit(model), whole_spec((model, width)), whole_spec((16, 2))],
        out_specs=[
            of_unit(model), of_unit(q_dim), of_unit(2 * kv_dim), of_unit(state), of_unit(state),
            pl.BlockSpec((None, pairs, 8, rows), lambda u: (u, 0, 0, 0)), whole_spec((8, model)),
        ],
        us=6.5, name="project",
    )(place, lens, tokens, first, aux)


def attention_forward(unit, place, lens, q, kv_all, into, width):
    units, length, _ = kv_all.shape
    rows, q_dim = q.shape[0] // units, q.shape[1]
    heads = q_dim // HEAD_WIDTH
    given = () if into is None else (into,)

    def body(place_ref, lens_ref, q_ref, kv_ref, *rest):
        o_ref, lse_ref, bias, top, low, acc = rest[-6:]
        top[...] = jnp.full_like(top, NEGATIVE)
        low[...] = jnp.zeros_like(low)
        acc[...] = jnp.zeros_like(acc)
        own = place_ref[1]
        base = own * rows
        start = document_start(lens_ref, unit, base + lax.broadcasted_iota(jnp.int32, (1, rows), 1))
        blocks = own - document_start(lens_ref, unit, base) // rows + 1

        def step(i, carry):
            j = own - i
            at = pl.multiple_of(j * rows, rows)
            keys = kv_ref[pl.ds(at, rows), :HEAD_WIDTH]
            turned = kv_ref[pl.ds(at, rows), :].astype(F32).T[HEAD_WIDTH:].astype(LOW)
            u = at + lax.broadcasted_iota(jnp.int32, (rows, rows), 0)
            t = base + lax.broadcasted_iota(jnp.int32, (rows, rows), 1)
            seen = (u <= t) & (u >= start)
            bias[...] = jnp.where(seen, 0.0, NEGATIVE)
            for h in range(heads):
                lanes = slice(h * HEAD_WIDTH, (h + 1) * HEAD_WIDTH)
                s = nt_dot(keys, q_ref[:, lanes]) + bias[...]
                before = top[h : h + 1, :]
                now = jnp.maximum(before, jnp.max(s, axis=0, keepdims=True))
                p = jnp.exp(s - now)
                scale = jnp.exp(before - now)
                top[h : h + 1, :] = now
                low[h : h + 1, :] = low[h : h + 1, :] * scale + jnp.sum(p, axis=0, keepdims=True)
                acc[lanes, :] = acc[lanes, :] * scale + nn_dot(turned, p.astype(LOW))
            return carry

        lax.fori_loop(0, blocks, step, 0)
        for h in range(heads):
            lanes = slice(h * HEAD_WIDTH, (h + 1) * HEAD_WIDTH)
            acc[lanes, :] = acc[lanes, :] / low[h : h + 1, :]
        o_ref[...] = acc[...].T.astype(LOW)
        lse_ref[...] = top[...] + jnp.log(low[...])

    return launch(
        body,
        grid=(1,),
        out_shape=(jax.ShapeDtypeStruct((units * rows, width), LOW), jax.ShapeDtypeStruct((8, rows), F32)),
        in_specs=[
            SCALARS, SCALARS, pl.BlockSpec((rows, q_dim), lambda i: (unit, 0)),
            pl.BlockSpec((None, length, 2 * HEAD_WIDTH), lambda i: (unit, 0, 0)),
        ] + anywhere(given),
        out_specs=[pl.BlockSpec((rows, q_dim), lambda i: (unit, 0)), whole_spec((8, rows))],
        input_output_aliases={4: 0} if given else {},
        scratch_shapes=[
            pltpu.VMEM((rows, rows), F32),
            pltpu.VMEM((8, rows), F32),
            pltpu.VMEM((8, rows), F32),
            pltpu.VMEM((q_dim, rows), F32),
        ],
        us=10.5, name="attention_forward",
    )(place, lens, q, kv_all, *given)


def attention_backward(unit, place, lens, q, dog, og, kv_all, lse):
    units, length, _ = kv_all.shape
    rows, q_dim = q.shape[0] // units, q.shape[1]
    heads = q_dim // HEAD_WIDTH
    half = (1, length // rows // 2, rows, 2 * HEAD_WIDTH)
    sub = min(256, rows)

    def body(place_ref, lens_ref, q_ref, do_ref, o_ref, kv_ref, lse_ref, *rest):
        dq_ref, away_ref, keep_ref, bias, dq_acc, delta = rest[-6:]
        own = place_ref[1]
        base = own * rows
        start = document_start(lens_ref, unit, base + lax.broadcasted_iota(jnp.int32, (1, rows), 1))
        blocks = own - document_start(lens_ref, unit, base) // rows + 1
        dq_acc[...] = jnp.zeros_like(dq_acc)
        away_ref[...] = jnp.zeros_like(away_ref)
        keep_ref[...] = jnp.zeros_like(keep_ref)
        both = do_ref[...].astype(F32) * o_ref[...].astype(F32)
        lane = lax.broadcasted_iota(jnp.int32, (rows, 128), 1)
        columns = jnp.zeros((rows, 128), F32)
        for h in range(heads):
            total = jnp.sum(both[:, h * HEAD_WIDTH : (h + 1) * HEAD_WIDTH], axis=1, keepdims=True)
            columns = jnp.where(lane == h, total, columns)
        delta[...] = columns.T[:8]

        def step(i, carry):
            j = own - i
            at = pl.multiple_of(j * rows, rows)
            u = at + lax.broadcasted_iota(jnp.int32, (rows, rows), 0)
            t = base + lax.broadcasted_iota(jnp.int32, (rows, rows), 1)
            seen = (u <= t) & (u >= start)
            bias[...] = jnp.where(seen, 0.0, NEGATIVE)
            for r in range(0, rows, sub):
                keys = kv_ref[pl.ds(pl.multiple_of(at + r, sub), sub), :HEAD_WIDTH]
                values = kv_ref[pl.ds(pl.multiple_of(at + r, sub), sub), HEAD_WIDTH:]
                dk = jnp.zeros((sub, HEAD_WIDTH), F32)
                dv = jnp.zeros((sub, HEAD_WIDTH), F32)
                for h in range(heads):
                    lanes = slice(h * HEAD_WIDTH, (h + 1) * HEAD_WIDTH)
                    q_h, do_h = q_ref[:, lanes], do_ref[:, lanes]
                    p = jnp.exp(nt_dot(keys, q_h) + (bias[r : r + sub, :] - lse_ref[h : h + 1, :]))
                    ds = (p * (nt_dot(values, do_h) - delta[h : h + 1, :])).astype(LOW)
                    dv = dv + nn_dot(p.astype(LOW), do_h)
                    dk = dk + nn_dot(ds, q_h)
                    dq_acc[:, lanes] = dq_acc[:, lanes] + tn_dot(ds, keys)
                dkv = jnp.concatenate([dk, dv], axis=1).astype(LOW)

                @pl.when(lax.rem(own - j, 2) == 0)
                def _():
                    keep_ref[0, j // 2, r : r + sub, :] = dkv

                @pl.when(lax.rem(own - j, 2) == 1)
                def _():
                    away_ref[0, j // 2, r : r + sub, :] = dkv
            return carry

        lax.fori_loop(0, blocks, step, 0)
        dq_ref[...] = (dq_acc[...] * 0.125).astype(LOW)

    return launch(
        body,
        out_shape=(jax.ShapeDtypeStruct((rows, q_dim), LOW),) + (jax.ShapeDtypeStruct(half, LOW),) * 2,
        grid=(1,),
        in_specs=[
            SCALARS, SCALARS, pl.BlockSpec((rows, q_dim), lambda i: (unit, 0)), whole_spec((rows, q_dim)),
            pl.BlockSpec((rows, q_dim), lambda i: (unit, 0)), pl.BlockSpec((None, length, 2 * HEAD_WIDTH), lambda i: (unit, 0, 0)),
            whole_spec((8, rows)),
        ],
        out_specs=[whole_spec((rows, q_dim)), whole_spec(half), whole_spec(half)],
        scratch_shapes=[
            pltpu.VMEM((rows, rows), F32),
            pltpu.VMEM((rows, q_dim), F32),
            pltpu.VMEM((8, rows), F32),
        ],
        us=17, name="attention_backward",
    )(place, lens, q, dog, og, kv_all, lse)


def halves(columns, first, lane):
    return jnp.where(lane < 64, columns[:, first : first + 1], columns[:, first + 1 : first + 2])


def mamba_state(unit, per_head, left, zx, right=None, first=0):
    _, pairs, _, rows = per_head.shape
    state = left.shape[1]
    rights = () if right is None else (right,)
    height = state if rights else state + 16

    def body(head_ref, left_ref, zx_ref, *rest):
        out_ref = rest[-1]
        lane = lax.broadcasted_iota(jnp.int32, (rows, 128), 1)
        turned = left_ref[...].astype(F32).T.astype(LOW)
        for i in range(pairs):
            lanes = slice(128 * i, 128 * (i + 1))
            by_col = head_ref[i].T
            if rights:
                z = zx_ref[:, 256 * i : 256 * i + 128].astype(F32)
                value = rest[0][:, first + 128 * i : first + 128 * (i + 1)].astype(F32) * z * jax.nn.sigmoid(z)
                weight = halves(by_col, 4, lane)
            else:
                value = zx_ref[:, 256 * i + 128 : 256 * (i + 1)].astype(F32)
                weight = halves(by_col, 2, lane) * halves(by_col, 6, lane)
                passing = halves(by_col[rows - 16 :], 4, lane[:16])[15:]
                high = passing.astype(LOW).astype(F32)
                row = lax.broadcasted_iota(jnp.int32, (16, 128), 0)
                out_ref[state:, lanes] = jnp.where(row == 0, high, jnp.where(row == 1, passing - high, 0.0)).astype(LOW)
            out_ref[:state, lanes] = nn_dot(turned, (value * weight).astype(LOW)).astype(LOW)

    return launch(
        body,
        grid=(1,),
        out_shape=jax.ShapeDtypeStruct((height, 128 * pairs), LOW),
        in_specs=[
            pl.BlockSpec((None, pairs, 8, rows), lambda i: (unit, 0, 0, 0)), pl.BlockSpec((rows, state), lambda i: (unit, 0)),
            pl.BlockSpec((rows, 256 * pairs), lambda i: (unit, 0)),
        ] + [whole_spec(r.shape) for r in rights],
        out_specs=whole_spec((height, 128 * pairs)),
        us=2, name="mamba_state",
    )(per_head, left, zx, *rights)


def same_document(place_ref, lens_ref, unit, rows, t_axis):
    base = place_ref[1] * rows
    shape = (1, rows) if t_axis else (rows, 1)
    start = document_start(lens_ref, unit, base + lax.broadcasted_iota(jnp.int32, shape, t_axis)) - base
    t = lax.broadcasted_iota(jnp.int32, (rows, rows), t_axis)
    u = lax.broadcasted_iota(jnp.int32, (rows, rows), 1 - t_axis)
    return (u <= t) & (u >= start)


def mamba_forward(unit, place, lens, per_head, zx, b, c, state_in, skip, into, first):
    _, pairs, _, rows = per_head.shape
    blk = min(256, rows)
    state = b.shape[1]

    def body(place_ref, lens_ref, head_ref, zx_ref, b_ref, c_ref, state_ref, skip_ref, *rest):
        g_ref, y_ref, inner, x_dt = rest[-4:]

        @pl.when(pl.program_id(0) == 0)
        def _():
            seen = same_document(place_ref, lens_ref, unit, rows, 0)
            inner[...] = jnp.where(seen, nt_dot(c_ref[...], b_ref[...]), 0.0)

        lane = lax.broadcasted_iota(jnp.int32, (rows, 128), 1)
        by_row = head_ref[...]
        by_col = by_row.T
        xs_f = zx_ref[:, 128:].astype(F32)
        x_dt[...] = (xs_f * halves(by_col, 2, lane)).astype(LOW)
        read = nn_dot(c_ref[...], state_ref[...]) * halves(by_col, 4, lane)
        for i in range(rows // blk):
            part = slice(i * blk, (i + 1) * blk)
            sums = []
            for h in range(2):
                total = None
                for j in range(i + 1):
                    other = slice(j * blk, (j + 1) * blk)
                    gap = by_col[part, h : h + 1] - by_row[h : h + 1, other]
                    kernel = jnp.exp(jnp.minimum(gap, 0.0)) * inner[part, other]
                    term = nn_dot(kernel.astype(LOW), x_dt[other, :])
                    total = term if total is None else total + term
                sums.append(total)
            y = jnp.where(lane[part] < 64, sums[0], sums[1]) + read[part]
            y_ref[part, :] = y
            z_f = zx_ref[part, :128].astype(F32)
            g_ref[part, :] = ((y + skip_ref[...] * xs_f[part]) * z_f * jax.nn.sigmoid(z_f)).astype(LOW)

    return launch(
        body,
        grid=(pairs,),
        out_shape=(jax.ShapeDtypeStruct(into.shape, LOW), jax.ShapeDtypeStruct((rows, 128 * pairs), F32)),
        in_specs=[
            SCALARS, SCALARS, pl.BlockSpec((None, None, 8, rows), lambda i: (unit, i, 0, 0)), pl.BlockSpec((rows, 256), lambda i: (unit, i)),
            pl.BlockSpec((rows, state), lambda i: (unit, 0)), pl.BlockSpec((rows, state), lambda i: (unit, 0)),
            pl.BlockSpec((None, state, 128), lambda i: (unit, 0, i)), pair_spec(1),
        ] + anywhere((into,)),
        out_specs=[pl.BlockSpec((rows, 128), lambda i: (unit, first // 128 + i)), pair_spec(rows)],
        input_output_aliases={8: 0},
        scratch_shapes=[pltpu.VMEM((rows, rows), F32), pltpu.VMEM((rows, 128), LOW)],
        us=7.5, name="mamba_forward",
    )(place, lens, per_head, zx, b, c, state_in, skip, into)


def mamba_backward(unit, place, lens, per_head, zx, y, dog, first, b, c, state_in, later, skip, aux, into):
    _, pairs, _, rows = per_head.shape
    blk = min(256, rows)
    state = b.shape[1]
    given = () if into is None else tuple(into)

    def body(place_ref, lens_ref, head_ref, zx_ref, y_ref, dg_ref, b_ref, c_ref, state_ref, later_ref, skip_ref, aux_ref, *rest):
        dzx_ref, dbc_ref, grads_ref, inner, d_inner, dy_low, x_low, db, dc, stats = rest[-10:]
        pair = pl.program_id(0)

        @pl.when(pair == 0)
        def _():
            seen = same_document(place_ref, lens_ref, unit, rows, 1)
            inner[...] = jnp.where(seen, nt_dot(b_ref[...], c_ref[...]), 0.0)
            d_inner[...] = jnp.zeros_like(d_inner)
            db[...] = jnp.zeros_like(db)
            dc[...] = jnp.zeros_like(dc)

        lane = lax.broadcasted_iota(jnp.int32, (rows, 128), 1)
        by_row = head_ref[pair]
        by_col = by_row.T
        xs_f = zx_ref[:, 128:].astype(F32)
        z_f = zx_ref[:, :128].astype(F32)
        sig = jax.nn.sigmoid(z_f)
        d_gate = dg_ref[...].astype(F32)
        d_y = d_gate * z_f * sig
        y_core = y_ref[...]
        dzx_ref[:, :128] = (d_gate * (y_core + skip_ref[...] * xs_f) * sig * (1.0 + z_f * (1.0 - sig))).astype(LOW)
        dy_low[...] = d_y.astype(LOW)
        dt = halves(by_col, 2, lane)
        x_dt = xs_f * dt
        x_low[...] = x_dt.astype(LOW)
        closing = halves(by_col, 6, lane)
        from_later = nn_dot(b_ref[...], later_ref[...]) * closing
        db[...] += nt_dot((x_dt * closing).astype(LOW), later_ref[...])
        dc[...] += nt_dot((d_y * halves(by_col, 4, lane)).astype(LOW), state_ref[...])
        count = rows // blk
        columns = jnp.zeros((rows, 128), F32)
        d_x_parts = []
        for j in range(count):
            part = slice(j * blk, (j + 1) * blk)
            sums = []
            for h in range(2):
                own = (lane[part] < 64) if h == 0 else (lane[part] >= 64)
                x_h = jnp.where(own, x_low[part, :].astype(F32), 0.0).astype(LOW)
                total = None
                for i in range(j, count):
                    other = slice(i * blk, (i + 1) * blk)
                    gap = by_row[h : h + 1, other] - by_col[part, h : h + 1]
                    decay = jnp.exp(jnp.minimum(gap, 0.0))
                    term = nn_dot((decay * inner[part, other]).astype(LOW), dy_low[other, :])
                    total = term if total is None else total + term
                    d_inner[part, other] += decay * nt_dot(x_h, dy_low[other, :])
                sums.append(total)
            d_x_parts.append(jnp.where(lane[part] < 64, sums[0], sums[1]))
        d_x = jnp.concatenate(d_x_parts, axis=0) if count > 1 else d_x_parts[0]
        d_x = d_x + from_later
        dzx_ref[:, 128:] = (d_x * dt + skip_ref[...] * d_y).astype(LOW)
        rounded_x = x_low[...].astype(F32)
        rounded_dy = dy_low[...].astype(F32)
        carried_back = jnp.sum(later_ref[...].astype(F32) * state_ref[...].astype(F32), axis=0, keepdims=True)
        row = lax.broadcasted_iota(jnp.int32, (rows, 1), 0)
        for at, value in enumerate((d_x * xs_f, rounded_dy * y_core - rounded_x * d_x, rounded_x * from_later, d_y * xs_f)):
            for h in range(2):
                own = (lane < 64) if h == 0 else (lane >= 64)
                total = jnp.sum(jnp.where(own, value, 0.0), axis=1, keepdims=True)
                if at == 2:
                    own = (lane[:1] < 64) if h == 0 else (lane[:1] >= 64)
                    passed = jnp.sum(jnp.where(own, carried_back, 0.0), axis=1, keepdims=True)
                    total = total + jnp.where(row == rows - 1, passed * by_row[4 + h : 5 + h, rows - 1 :], 0.0)
                columns = jnp.where(lane == 2 * at + h, total, columns)
        stats[pair] = columns.T[:8]

        @pl.when(pair == pairs - 1)
        def _():
            seen = same_document(place_ref, lens_ref, unit, rows, 1)
            low = jnp.where(seen, d_inner[...], 0.0).astype(LOW)
            dbc_ref[:, :state] = (db[...] + nn_dot(low, c_ref[...])).astype(LOW)
            dbc_ref[:, state : 2 * state] = (dc[...] + tn_dot(low, b_ref[...])).astype(LOW)

            def heads_of(ref, at):
                blank = jnp.zeros((16 - 2 * pairs, rows), F32)
                parts = [ref[i, 2 * at : 2 * at + 2, :] for i in range(pairs)]
                return jnp.concatenate(parts + [blank] * (2 * pairs < 16), axis=0)

            dt = heads_of(head_ref, 1)
            rate = -jnp.exp(aux_ref[:, 0:1])
            position = lax.broadcasted_iota(jnp.int32, (1, rows), 1)
            d_end = jnp.sum(heads_of(stats, 2), axis=1, keepdims=True)
            d_decay = heads_of(stats, 1) + jnp.where(position == rows - 1, d_end, 0.0)
            d_rate = lax.dot_general(
                d_decay, lower_from(rows), (((1,), (1,)), ((), ())), precision=PRECISE, preferred_element_type=F32)
            d_raw = (heads_of(stats, 0) + rate * d_rate) * (1.0 - jnp.exp(-dt))
            turned = jnp.concatenate([d_raw, jnp.zeros((112, rows), F32)], axis=0).T
            dbc_ref[:, 2 * state : 2 * state + 128] = turned.astype(LOW)
            dbc_ref[:, 2 * state + 128 :] = jnp.zeros((rows, 128), LOW)
            lanes = lax.broadcasted_iota(jnp.int32, (16, 128), 1)
            sums = jnp.zeros((16, 128), F32)
            for at, value in enumerate((d_rate * rate * dt, d_raw, heads_of(stats, 3))):
                sums = jnp.where(lanes == at, jnp.sum(value, axis=1, keepdims=True), sums)
            grads_ref[...] = sums

    total = zx.shape[0]
    return launch(
        body,
        grid=(pairs,),
        out_shape=(
            jax.ShapeDtypeStruct(zx.shape, LOW), jax.ShapeDtypeStruct((total, 2 * state + 256), LOW),
            jax.ShapeDtypeStruct((16, 128), F32),
        ),
        in_specs=[
            SCALARS, SCALARS, pl.BlockSpec((None, pairs, 8, rows), lambda i: (unit, 0, 0, 0)),
            pl.BlockSpec((rows, 256), lambda i: (unit, i)), pair_spec(rows),
            pl.BlockSpec((rows, 128), lambda i: (0, first // 128 + i)),
            pl.BlockSpec((rows, state), lambda i: (unit, 0)), pl.BlockSpec((rows, state), lambda i: (unit, 0)),
            pl.BlockSpec((None, state, 128), lambda i: (unit, 0, i)), pair_spec(state), pair_spec(1), whole_spec((16, 2)),
        ] + anywhere(given),
        out_specs=[
            pl.BlockSpec((rows, 256), lambda i: (unit, i)), pl.BlockSpec((rows, 2 * state + 256), lambda i: (unit, 0)),
            whole_spec((16, 128)),
        ],
        input_output_aliases={12: 0, 13: 1} if given else {},
        scratch_shapes=[
            pltpu.VMEM((rows, rows), F32), pltpu.VMEM((rows, rows), F32), pltpu.VMEM((rows, 128), LOW), pltpu.VMEM((rows, 128), LOW),
            pltpu.VMEM((rows, state), F32), pltpu.VMEM((rows, state), F32), pltpu.VMEM((pairs, 8, rows), F32),
        ],
        us=16.3, name="mamba_backward",
    )(place, lens, per_head, zx, y, dog, b, c, state_in, later, skip, aux, *given)


def feed_forward(unit, x, ours, theirs, gains, dy, weights, into):
    rows, model = ours.shape
    total = x.shape[0]
    hidden = weights.shape[1] // 3
    blk = min(256, hidden)
    count = hidden // blk
    given = () if into is None else tuple(into)

    def body(x_ref, ours_ref, theirs_ref, gains_ref, dy_ref, ab_ref, down_ref, *rest):
        h1_ref, n2_ref, f_ref, dab_ref, dn2_ref, dn2_acc = rest[-6:]

        @pl.when(pl.program_id(0) == 0)
        def _():
            h1 = x_ref[...].astype(F32) + (ours_ref[...].astype(F32) + theirs_ref[...].astype(F32))
            scale = lax.rsqrt(jnp.mean(h1 * h1, axis=1, keepdims=True) + EPSILON)
            h1_ref[...] = h1
            n2_ref[...] = (h1 * scale * gains_ref[1:2, :]).astype(LOW)

        ab = nn_dot(n2_ref[...], ab_ref[...])
        a, b = ab[:, :blk], ab[:, blk:]
        sig = jax.nn.sigmoid(a)
        silu = a * sig
        f = (silu * b).astype(LOW)
        f_ref[...] = f
        df = nn_dot(dy_ref[...], down_ref[...])
        dab_ref[:, :blk] = (df * b * sig * (1.0 + a * (1.0 - sig))).astype(LOW)
        dab_ref[:, blk:] = (df * silu).astype(LOW)
        dn2 = nt_dot(dab_ref[...], ab_ref[...])

        @pl.when(pl.program_id(0) == 0)
        def _():
            dn2_acc[...] = dn2

        @pl.when(pl.program_id(0) > 0)
        def _():
            dn2_acc[...] += dn2

        @pl.when(pl.program_id(0) == count - 1)
        def _():
            dn2_ref[...] = dn2_acc[...].astype(LOW)

    at_unit = pl.BlockSpec((rows, model), lambda j: (unit, 0))
    return launch(
        body,
        grid=(count,),
        out_shape=(
            jax.ShapeDtypeStruct((total, model), F32), jax.ShapeDtypeStruct((total, model), LOW),
            jax.ShapeDtypeStruct((total, hidden), LOW), jax.ShapeDtypeStruct((total, 2 * hidden), LOW),
            jax.ShapeDtypeStruct((rows, model), LOW),
        ),
        in_specs=[
            at_unit, whole_spec((rows, model)), whole_spec((rows, model)), whole_spec((8, model)), at_unit,
            pl.BlockSpec((model, 2 * blk), lambda j: (0, j)), pl.BlockSpec((model, blk), lambda j: (0, 2 * count + j)),
        ] + anywhere(given),
        out_specs=[
            at_unit, at_unit, pl.BlockSpec((rows, blk), lambda j: (unit, j)), pl.BlockSpec((rows, 2 * blk), lambda j: (unit, j)),
            whole_spec((rows, model)),
        ],
        input_output_aliases={7: 0, 8: 1, 9: 2, 10: 3} if given else {},
        scratch_shapes=[pltpu.VMEM((rows, model), F32)],
        us=14, name="feed_forward",
    )(x, ours, theirs, gains, dy, weights, weights, *given)


def feed_forward_out(f, weights):
    total, hidden = f.shape
    model = weights.shape[0]
    blk = min(512, total)

    def body(f_ref, down_ref, *rest):
        rest[-1][...] = nt_dot(f_ref[...], down_ref[...]).astype(LOW)

    return launch(
        body,
        grid=(total // blk,),
        out_shape=jax.ShapeDtypeStruct((total, model), LOW),
        in_specs=[pl.BlockSpec((blk, hidden), lambda i: (i, 0)), pl.BlockSpec((model, hidden), lambda i: (0, 2))],
        out_specs=pl.BlockSpec((blk, model), lambda i: (i, 0)),
        us=5, name="feed_forward_out",
    )(f, weights)


def norm_gradient(hidden, gain, d_normed):
    inv = lax.rsqrt(jnp.mean(hidden * hidden, axis=1, keepdims=True) + EPSILON)
    weighted = gain * d_normed
    mean = jnp.mean(weighted * hidden, axis=1, keepdims=True)
    normed = hidden * inv
    return inv * weighted - normed * (inv * inv * mean), jnp.sum(d_normed * normed, axis=0, keepdims=True)


def middle_backward(unit, h1, ours, theirs, gains, dy, third, into):
    rows, model = ours.shape
    width = third.shape[1]
    given = () if into is None else (into,)

    def body(h1_ref, ours_ref, theirs_ref, gains_ref, dy_ref, third_ref, *rest):
        dm_ref, dh_ref, dog_ref, sum_ref = rest[-4:]
        dn2 = ours_ref[...].astype(F32) + theirs_ref[...].astype(F32)
        dh, terms = norm_gradient(h1_ref[...], gains_ref[1:2, :], dn2)
        dh = dh + dy_ref[...].astype(F32)
        dh_ref[...] = dh
        dm = dh.astype(LOW)
        dm_ref[...] = dm
        dog_ref[...] = nn_dot(dm, third_ref[...]).astype(LOW)
        sum_ref[...] = jnp.broadcast_to(terms, sum_ref.shape)

    at_unit = pl.BlockSpec((rows, model), lambda i: (unit, 0))
    full = whole_spec((rows, model))
    return launch(
        body,
        grid=(1,),
        out_shape=(
            jax.ShapeDtypeStruct(h1.shape, LOW), jax.ShapeDtypeStruct((rows, model), F32),
            jax.ShapeDtypeStruct((rows, width), LOW), jax.ShapeDtypeStruct((8, model), F32),
        ),
        in_specs=[at_unit, full, full, whole_spec((8, model)), at_unit, whole_spec((model, width))] + anywhere(given),
        out_specs=[at_unit, full, whole_spec((rows, width)), whole_spec((8, model))],
        input_output_aliases={6: 0} if given else {},
        us=5.4, name="middle_backward",
    )(h1, ours, theirs, gains, dy, third, *given)


def input_backward(unit, dq, keep, got, dbc, dzx, first, second, x, into):
    rows, q_dim = dq.shape
    model = first.shape[0]
    blk = 256 if model % 256 == 0 else model
    rest_width = dbc.shape[1]
    width = q_dim + keep.shape[-1]
    rest = first.shape[1] - width
    given = () if into is None else (into,)

    def body(dq_ref, keep_ref, got_ref, dbc_ref, dzx_ref, first_ref, second_ref, x_ref, *others):
        dqkv_ref, part_ref, sum_ref, inv = others[-4:]
        j = pl.program_id(0)

        @pl.when(j == 0)
        def _():
            x = x_ref[...].astype(F32)
            scale = lax.rsqrt(jnp.mean(x * x, axis=1, keepdims=True) + EPSILON)
            inv[...] = jnp.broadcast_to(scale, inv.shape)
            dqkv_ref[:, :q_dim] = dq_ref[...]
            dqkv_ref[:, q_dim:] = (keep_ref[0, 0].astype(F32) + got_ref[0, 0].astype(F32)).astype(LOW)

        part = nt_dot(dqkv_ref[...], first_ref[:, :width]) + nt_dot(dbc_ref[:, :rest], first_ref[:, width:])
        part = part + nt_dot(dzx_ref[...], second_ref[...])
        part_ref[...] = part.astype(LOW)
        x = x_ref[:, pl.ds(pl.multiple_of(j * blk, blk), blk)].astype(F32)
        terms = jnp.sum(part * x * inv[:, :1], axis=0, keepdims=True)
        sum_ref[...] = jnp.broadcast_to(terms, sum_ref.shape)

    return launch(
        body,
        grid=(model // blk,),
        out_shape=(
            jax.ShapeDtypeStruct((x.shape[0], width), LOW), jax.ShapeDtypeStruct((rows, model), LOW), jax.ShapeDtypeStruct((8, model), F32),
        ),
        in_specs=[
            whole_spec((rows, q_dim)), whole_spec(keep.shape), whole_spec(keep.shape), pl.BlockSpec((rows, rest_width), lambda j: (unit, 0)),
            pl.BlockSpec((rows, dzx.shape[1]), lambda j: (unit, 0)), pl.BlockSpec((blk, first.shape[1]), lambda j: (j, 0)),
            pl.BlockSpec((blk, second.shape[1]), lambda j: (j, 0)), pl.BlockSpec((rows, model), lambda j: (unit, 0)),
        ] + anywhere(given),
        out_specs=[
            pl.BlockSpec((rows, width), lambda j: (unit, 0)), pl.BlockSpec((rows, blk), lambda j: (0, j)),
            pl.BlockSpec((8, blk), lambda j: (0, j)),
        ],
        input_output_aliases={8: 0} if given else {},
        scratch_shapes=[pltpu.VMEM((rows, 128), F32)],
        us=6.5, name="input_backward",
    )(dq, keep, got, dbc, dzx, first, second, x, *given)


def finish(unit, x, ours, theirs, gains, dh, into):
    rows, model = ours.shape
    given = () if into is None else (into,)

    def body(x_ref, ours_ref, theirs_ref, gains_ref, dh_ref, *rest):
        dn1 = ours_ref[...].astype(F32) + theirs_ref[...].astype(F32)
        dx, _ = norm_gradient(x_ref[...].astype(F32), gains_ref[0:1, :], dn1)
        rest[-1][...] = dx + dh_ref[...]

    at_unit = pl.BlockSpec((rows, model), lambda i: (unit, 0))
    full = whole_spec((rows, model))
    return launch(
        body,
        grid=(1,),
        out_shape=jax.ShapeDtypeStruct(x.shape, F32),
        in_specs=[at_unit, full, full, whole_spec((8, model)), full] + anywhere(given),
        out_specs=at_unit,
        input_output_aliases={5: 0} if given else {},
        us=4.2, name="finish",
    )(x, ours, theirs, gains, dh, *given)


def pack(place, parts, cols, name):
    arrays = []
    for arr, *_ in parts:
        if not any(arr is other for other in arrays):
            arrays.append(arr)
    where = [next(i for i, other in enumerate(arrays) if other is part[0]) for part in parts]
    nc = lax.axis_size("context")
    rows = arrays[0].shape[1] if parts[0][4] else arrays[0].shape[0]
    filled = max(part[1] + part[2] for part in parts)

    def body(place_ref, *refs):
        out_ref, own_ref = refs[-2:]
        if filled < cols:
            start = filled - filled % 128
            out_ref[:, start:] = jnp.zeros((rows, cols - start), LOW)
        for n, (_, at, width, first, turned) in zip(where, parts):
            if turned:
                out_ref[:, at : at + width] = refs[n][...].astype(F32).T.astype(LOW)
            else:
                out_ref[:, at : at + width] = refs[n][:, first : first + width]
        own_ref[...] = out_ref[pl.ds(pl.multiple_of(place_ref[1] * (rows // nc), rows // nc), rows // nc), :]

    return launch(
        body, out_shape=(jax.ShapeDtypeStruct((rows, cols), LOW), jax.ShapeDtypeStruct((rows // nc, cols), LOW)),
        in_specs=[SCALARS] + [whole_spec(arr.shape) for arr in arrays],
        out_specs=[whole_spec((rows, cols)), whole_spec((rows // nc, cols))], name=name, us=2,
    )(place, *arrays)


def emit(place, held, got, outs, name):
    half, part, _ = held.shape
    low = min(first for pieces, _ in outs for first, _ in pieces)
    low -= low % 128
    cols = max(first + width for pieces, _ in outs for first, width in pieces) - low
    cols += -cols % 128
    nc = 2 * half
    rows = nc * part
    offsets = [reverse_bits(m) for m in range(nc)][:half]
    widths = [sum(width for _, width in pieces) for pieces, _ in outs]

    def body(place_ref, held_ref, got_ref, *refs):
        whole = refs[-1]
        ci = place_ref[1]
        for m, off in enumerate(offsets):
            for ref, bit in ((held_ref, 0), (got_ref, 1)):
                at = pl.multiple_of(lax.bitwise_xor(ci, off ^ bit) * part, part)
                whole[pl.ds(at, part), :] = ref[m, :, low : low + cols].astype(F32)
        for ref, (pieces, turned) in zip(refs, outs):
            to = 0
            for first, width in pieces:
                if turned:
                    ref[to : to + width, :] = whole[:, first - low : first - low + width].T
                else:
                    ref[:, to : to + width] = whole[:, first - low : first - low + width]
                to += width

    shapes = [(width, rows) if turned else (rows, width) for width, (_, turned) in zip(widths, outs)]
    return launch(
        body, out_shape=tuple(jax.ShapeDtypeStruct(shape, F32) for shape in shapes),
        in_specs=[SCALARS, whole_spec(held.shape), whole_spec(held.shape)], out_specs=[whole_spec(shape) for shape in shapes],
        scratch_shapes=[pltpu.VMEM((rows, cols), F32)], name=name, us=3,
    )(place, held, got)


def close_forward(h1, ours, theirs):
    total, model = h1.shape
    blk = min(256, total)

    def body(h1_ref, ours_ref, theirs_ref, out_ref):
        out_ref[...] = (h1_ref[...] + (ours_ref[...].astype(F32) + theirs_ref[...].astype(F32))).astype(LOW)

    spec = pl.BlockSpec((blk, model), lambda i: (i, 0))
    return launch(
        body, grid=(total // blk,), out_shape=jax.ShapeDtypeStruct((total, model), LOW), in_specs=[spec] * 3, out_specs=spec,
        name="close_forward", us=4,
    )(h1, ours, theirs)


def project_mixer(n1, second):
    tokens, model = n1.shape
    cols = second.shape[1]
    blk = column_block(cols)

    def body(n1_ref, second_ref, out_ref):
        out_ref[...] = nn_dot(n1_ref[...], second_ref[...]).astype(LOW)

    return launch(
        body, grid=(cols // blk,), out_shape=jax.ShapeDtypeStruct((tokens, cols), LOW),
        in_specs=[whole_spec((tokens, model)), pl.BlockSpec((model, blk), lambda j: (0, j))],
        out_specs=pl.BlockSpec((tokens, blk), lambda j: (0, j)), name="project_mixer", us=5,
    )(n1, second)


def mixer_out(unit, og, third, rows):
    width = og.shape[1]
    model = third.shape[0]
    blk = column_block(model)

    def body(og_ref, third_ref, out_ref):
        out_ref[...] = nt_dot(og_ref[...], third_ref[...]).astype(LOW)

    return launch(
        body, grid=(model // blk,), out_shape=jax.ShapeDtypeStruct((rows, model), LOW),
        in_specs=[pl.BlockSpec((rows, width), lambda j: (unit, 0)), pl.BlockSpec((blk, width), lambda j: (j, 0))],
        out_specs=pl.BlockSpec((rows, blk), lambda j: (0, j)), name="mixer_out", us=2,
    )(og, third)


def turns(first, second, width):
    count = first.shape[-1] // width
    parts = [arr[..., width * i : width * (i + 1)] for i in range(count) for arr in (first, second)]
    return jnp.concatenate(parts, axis=-1)


def unturned(mixed, width, which):
    count = mixed.shape[-1] // (2 * width)
    return jnp.concatenate([mixed[..., width * (2 * i + which) : width * (2 * i + which + 1)] for i in range(count)], axis=-1)


def per_device(
    tokens, cotangent, doc_lengths, mixer_gain, w_query, key_matrix, value_matrix, mamba_gate_weight,
    mamba_input_weight, w_bproj, w_cproj, w_dt, a_log, dt_bias, d_skip, w_attn_out, w_mixer_out,
    ffn_gain, w_gate, w_up, w_down,
):
    CHAIN.clear()
    micro_count, seq_count, block_len, model_dim = tokens.shape
    rows_here = mixer_gain.shape[0]
    heads = w_dt.shape[1]
    ssm_dim = mamba_gate_weight.shape[1]
    head_dim = ssm_dim // heads
    q_dim = w_query.shape[1]
    kv_dim = key_matrix.shape[1]
    state_dim = w_bproj.shape[1]
    ff_dim = w_gate.shape[1]
    ff_blk = min(256, ff_dim)
    ci = lax.axis_index("context")
    nc = lax.axis_size("context")
    full_len = nc * block_len
    units = micro_count * seq_count
    pairs = heads // 2
    tokens_here = units * block_len
    at_b = q_dim + 2 * kv_dim
    at_c = at_b + state_dim
    at_dt = at_c + state_dim
    at_gain = at_dt + heads
    first_width = at_gain + 2 + -(at_gain + 2) % 128

    place = jnp.stack([lax.axis_index("fsdp"), ci]).astype(jnp.int32)
    at_k, at_v = q_dim, q_dim + kv_dim
    two = 2 * head_dim
    first, own_first = pack(
        place,
        [(w_query, 0, q_dim, 0, False), (key_matrix.T, at_k, kv_dim, 0, True), (value_matrix.T, at_v, kv_dim, 0, True),
         (w_bproj, at_b, state_dim, 0, False), (w_cproj, at_c, state_dim, 0, False), (w_dt.T, at_dt, heads, 0, True),
         (jnp.stack([mixer_gain, ffn_gain]), at_gain, 2, 0, True)],
        first_width, "pack_first")
    near_first = send_near(own_first)
    second, own_second = pack(
        place,
        [(arr, (2 * i + n) * two, two, i * two, False)
         for i in range(pairs) for n, arr in enumerate((mamba_gate_weight, mamba_input_weight))],
        2 * ssm_dim, "pack_second")
    third, own_third = pack(
        place, [(w_attn_out, 0, q_dim, 0, True), (w_mixer_out, q_dim, ssm_dim, 0, True)], q_dim + ssm_dim, "pack_third")
    fourth, own_fourth = pack(
        place,
        [(arr, (2 * i + n) * ff_blk, ff_blk, i * ff_blk, False) for i in range(ff_dim // ff_blk) for n, arr in enumerate((w_gate, w_up))]
        + [(w_down, 2 * ff_dim, ff_dim, 0, True)],
        3 * ff_dim, "pack_fourth")
    lens = doc_lengths.reshape(units, -1)
    aux = jnp.pad(jnp.stack([a_log, dt_bias], axis=1), ((0, 16 - heads), (0, 0)))
    skip_row = jnp.repeat(d_skip, head_dim)[None]
    tokens = tokens.reshape(tokens_here, model_dim)
    cotangent = cotangent.reshape(tokens_here, model_dim)
    width = q_dim + ssm_dim

    def placed(shard, mine, other):
        return place_rows(place, shard.reshape(nc, -1, shard.shape[1]), [mine], [other])

    held_first = join(near_first, True)
    near_second = send_near(own_second)
    wait_for(*near_second)
    held_first = spread_far(held_first)
    core_first = swap_context(held_first, 1)
    held_second = join(near_second, True)
    first = placed(first, held_first, core_first)
    n1, q, kv, b, c, per_head, gains = project(place, lens, tokens, first, aux, q_dim, kv_dim, state_dim, pairs)
    kv = kv.reshape(1, units, block_len, 2 * kv_dim)
    kv_far = [swap_context(kv, bit) for bit in far_bits()[:1]]
    near_third = send_near(own_third)
    near_fourth = send_near(own_fourth, True)
    wait_for(*near_third)
    kv_held = join([kv, *kv_far], False)
    for bit in far_bits()[1:]:
        kv_held = join([kv_held, swap_context(kv_held, bit)], False)
    kv_core = swap_context(kv_held, 1)
    held_second = spread_far(held_second)
    core_second = swap_context(held_second, 1)
    kv_all = place_blocks(place, kv_held, kv_core)
    held_third = join(near_third, True)
    wait_for(near_fourth[0])
    second = placed(second, held_second, core_second)
    zx = project_mixer(n1, second)
    span = join([mamba_state(u, per_head, b, zx) for u in range(units)], True)[None]
    span_far = [swap_context(span, bit) for bit in far_bits()[:1]]
    og, lse = None, [None] * units
    wait_for(*near_fourth[1:2])
    og, lse[0] = attention_forward(0, place, lens, q, kv_all, og, width)
    span = join([span, *span_far], False)
    for bit in far_bits()[1:]:
        span = join([span, swap_context(span, bit)], False)
    spans = (span, swap_context(span, 1))
    wait_for(*near_fourth[2:])
    held_third = spread_far(held_third)
    core_third = swap_context(held_third, 1)
    held_fourth = join(near_fourth, True)
    state = chain_states(place, spans, state_dim)
    third = placed(third, held_third, core_third)
    og, y_u = mamba_forward(0, place, lens, per_head, zx, b, c, state, skip_row, og, q_dim)
    y, ours = [y_u], [mixer_out(0, og, third, block_len)]
    theirs = [swap_tensor(ours[0])]
    for u in range(1, units):
        og, lse[u] = attention_forward(u, place, lens, q, kv_all, og, width)
        og, y_u = mamba_forward(u, place, lens, per_head, zx, b, c, state, skip_row, og, q_dim)
        y.append(y_u)
        ours.append(mixer_out(u, og, third, block_len))
        theirs.append(swap_tensor(ours[u]))
    held_fourth = spread_far(held_fourth, 3)
    fourth = place_rows(
        place, fourth.reshape(nc, -1, fourth.shape[1]), held_fourth, [swap_context(arr, 1) for arr in held_fourth])

    stacked, dn2, dn2_theirs = None, [], []
    for u in range(units):
        *stacked, dn2_u = feed_forward(u, tokens, ours[u], theirs[u], gains, cotangent, fourth, stacked)
        dn2.append(dn2_u)
        dn2_theirs.append(swap_tensor(dn2_u))
    h1, n2, f, dab = stacked
    wide = 3 * ff_dim
    away, keep_fourth = outer(place, n2, dab, None, 0, wide)
    wait_for(dn2_theirs[0])
    away, keep_fourth = outer(place, cotangent, f, (away, keep_fourth), 2 * ff_dim, wide)
    got_fourth = swap_context(away, 1)

    dm, dh, dog, d_span, local = None, [], [], [], []
    g_gain_two = 0.0
    d_second, dq, dkv, head_grads = None, [None] * units, [None] * units, 0.0
    bits = context_bits()[1:]

    def open_backward(u, dm):
        dm, dh_u, dog_u, terms = middle_backward(u, h1, dn2[u], dn2_theirs[u], gains, cotangent, third, dm)
        dh.append(dh_u)
        dog.append(dog_u)
        local.append(mamba_state(u, per_head, c, zx, dog_u, q_dim)[None, None])
        return dm, terms[0]

    def attend_back(u):
        dq[u], away, keep = attention_backward(u, place, lens, q, dog[u], og, kv_all, lse[u])
        return keep, swap_context(away, 1)

    def close_states(u):
        held = spread_far(local[u])
        return held, swap_context(held, 1)

    def to_owners(keep, got):
        own, *away = split_fsdp(place, keep, got)
        return [own] + [from_next(arr, "fsdp", k + 1) for k, arr in enumerate(away)]

    def share(total):
        held = spread_far(total[None])
        return held, swap_context(held, 1)

    for u in range(units - 1):
        dm, terms = open_backward(u, dm)
        g_gain_two = g_gain_two + terms
        kept = attend_back(u)
        pair = close_states(u)
        if u == 0:
            keep_fourth, got_fourth = reduce_far(place, keep_fourth, got_fourth, bits)
        dkv[u] = reduce_far(place, *kept, bits)
        d_span.append(chain_states(place, spans, state_dim, pair, u)[0])
    dm, terms = open_backward(units - 1, dm)
    g_gain_two = g_gain_two + terms
    ff = feed_forward_out(f, fourth)
    ff_theirs = swap_tensor(ff)
    at_zx = q_dim + ssm_dim
    at_rest = at_zx + 2 * ssm_dim
    wide = wide_second = at_rest + 2 * state_dim + 256
    pair_second = outer(place, dm, og, None, 0, wide)
    for u in range(units):
        if u == units - 1:
            pair = close_states(u)
            parts_fourth = to_owners(keep_fourth, got_fourth)
            d_span.append(chain_states(place, spans, state_dim, pair, u)[0])
        *d_second, grads_u = mamba_backward(
            u, place, lens, per_head, zx, y[u], dog[u], q_dim, b, c, state, d_span[u], skip_row, aux, d_second)
        head_grads = head_grads + grads_u
    dzx, dbc = d_second
    pair_second = outer(place, n1, dzx, pair_second, at_zx, wide)
    away, keep_second = outer(place, n1, dbc, pair_second, at_rest, wide)
    got_second = swap_context(away, 1)
    parts, parts_theirs, g_gain_one, dqkv = [None] * units, [None] * units, 0.0, None

    def close_backward(u, dqkv):
        dqkv, parts[u], terms = input_backward(u, dq[u], *dkv[u], dbc, dzx, first, second, tokens, dqkv)
        parts_theirs[u] = swap_tensor(parts[u])
        return dqkv, terms[0]

    for u in range(units - 1):
        dqkv, terms = close_backward(u, dqkv)
        g_gain_one = g_gain_one + terms
    keep_second, got_second = reduce_far(place, keep_second, got_second, bits)
    kept = attend_back(units - 1)
    g_fourth = sum_parts(parts_fourth)
    dkv[units - 1] = reduce_far(place, *kept, bits)
    own_second, *below = split_fsdp(place, keep_second, got_second)
    chunks = below[::-1]
    ring = from_next(chunks[0], "fsdp")
    layer_out = close_forward(h1, ff, ff_theirs)
    fourth_held = spread_far(g_fourth[None])
    fourth_core = swap_context(fourth_held, 1)
    nf = lax.axis_size("fsdp")
    for k in range(1, nf - 2):
        ring = from_next(ring_step(ring, chunks[k]), "fsdp")
    dqkv, terms = close_backward(units - 1, dqkv)
    g_gain_one = g_gain_one + terms
    nf = lax.axis_size("fsdp")
    part = model_dim // (nf * nc)
    head_grads = jnp.tile(jnp.pad(head_grads[:16, :3], ((0, part - 16), (0, 0))), (nf * nc, 1))
    g_gains = jnp.concatenate([jnp.stack([g_gain_one, g_gain_two], axis=1), head_grads], axis=1).astype(LOW)
    g_gains = jnp.pad(g_gains, ((0, 0), (0, 123)))
    wide = at_b + 128
    away, keep_first = outer(place, n1, dqkv, None, 0, wide)
    g_gains = g_gains.reshape((nf, nc // 2, 2, -1, 128))
    mine = ci % 2
    away = away.at[..., at_b:].set(lax.dynamic_index_in_dim(g_gains, 1 - mine, 2, keepdims=False))
    keep_first = keep_first.at[..., at_b:].set(lax.dynamic_index_in_dim(g_gains, mine, 2, keepdims=False))
    got_first = swap_context(away, 1)
    if nf > 2:
        ring = from_next(ring_step(ring, chunks[nf - 2]), "fsdp")
    input_grads = None
    for u in range(units - 1):
        input_grads = finish(u, tokens, parts[u], parts_theirs[u], gains, dh[u], input_grads)
    keep_first, got_first = reduce_far(place, keep_first, got_first, bits)

    def columns(first, width, turned=False):
        return [(first, width)], turned

    def in_turns(which, width, total, first=0):
        return [(first + width * (2 * i + which), width) for i in range(total // width)], False

    g_gate, g_up, g_down = emit(
        place, fourth_held, fourth_core,
        [in_turns(0, ff_blk, ff_dim), in_turns(1, ff_blk, ff_dim), columns(2 * ff_dim, ff_dim, True)], "emit_fourth")
    parts_first = to_owners(keep_first, got_first)
    g_second = share_columns(ring_step(ring, own_second), at_rest, at_rest + 2 * state_dim)
    u = units - 1
    input_grads = finish(u, tokens, parts[u], parts_theirs[u], gains, dh[u], input_grads)
    g_first = share_columns(sum_parts(parts_first, (), place), at_b, at_b + 1)
    last_held = spread_far(jnp.concatenate([g_second, g_first], axis=1)[None])
    last_core = swap_context(last_held, 1)
    at_last = wide_second
    outs = [
        columns(0, q_dim, True), columns(q_dim, ssm_dim, True), in_turns(0, two, ssm_dim, at_zx), in_turns(1, two, ssm_dim, at_zx),
        columns(at_rest, state_dim), columns(at_rest + state_dim, state_dim), columns(at_rest + 2 * state_dim, heads, True)]
    g_attn, g_mixer, g_z, g_x, g_b, g_c, g_dt = emit(place, last_held, last_core, outs, "emit_second")
    g_q, g_k, g_v, g_gains = emit(
        place, last_held, last_core,
        [columns(at_last, q_dim), columns(at_last + at_k, kv_dim, True), columns(at_last + at_v, kv_dim, True),
         columns(at_last + at_b, 16, True)], "emit_first")
    head_grads = g_gains[2:5]
    shape = (micro_count, seq_count, block_len, model_dim)
    return (
        layer_out.reshape(shape), input_grads.reshape(shape), g_gains[0], g_q, g_k.T, g_v.T, g_z, g_x, g_b, g_c, g_dt.T,
        head_grads[0, :heads], head_grads[1, :heads], head_grads[2, :heads], g_attn, g_mixer, g_gains[1], g_gate, g_up, g_down,
    )


def solution(mesh):
    rows, cols = P("fsdp", "tensor"), P("tensor", "fsdp")
    acts = P(None, "fsdp", "context", None)
    return jax.shard_map(
        per_device,
        mesh=mesh,
        in_specs=(
            acts, acts, P(None, "fsdp", None), P("fsdp"), rows, rows, rows, rows, rows, P("fsdp", None),
            P("fsdp", None), rows, P("tensor"), P("tensor"), P("tensor"), cols, cols, P("fsdp"), rows, rows, cols,
        ),
        out_specs=(
            acts, acts, P("fsdp"), rows, rows, rows, rows, rows, P("fsdp", None), P("fsdp", None), rows,
            P("tensor"), P("tensor"), P("tensor"), cols, cols, P("fsdp"), rows, rows, cols,
        ),
        check_vma=False,
    )
```

```python
import jax
import jax.numpy as jnp
from jax import lax
from jax.experimental import pallas as pl
from jax.experimental.pallas import tpu as pltpu
from jax.sharding import PartitionSpec as P

HEAD_WIDTH = 64
EPSILON = 1e-06
LOW = jnp.bfloat16
F32 = jnp.float32
NEGATIVE = -1e30
PRECISE = lax.Precision.HIGHEST


def swap_context(x, bit):
    size = lax.axis_size("context")
    return lax.ppermute(x, "context", [(i, i ^ bit) for i in range(size)])


def from_next(x, axis, step=1):
    size = lax.axis_size(axis)
    return lax.ppermute(x, axis, [((i + step) % size, i) for i in range(size)])


def swap_tensor(x):
    size = lax.axis_size("tensor")
    return lax.ppermute(x, "tensor", [(i, (i + 1) % size) for i in range(size)])


def context_bits():
    size = lax.axis_size("context")
    return [1 << k for k in range(size.bit_length() - 1)]


def reverse_bits(index):
    bits = context_bits()
    return sum(((index // low) % 2) * high for low, high in zip(bits, reversed(bits)))


CHAIN = []
SCALE = 0.4e9


def anywhere(arrays):
    return [pl.BlockSpec(memory_space=pl.ANY)] * len(arrays)


def whole_spec(shape):
    return pl.BlockSpec(shape, lambda i: (0,) * len(shape))


def pair_spec(rows):
    return pl.BlockSpec((rows, 128), lambda i: (0, i))


SCALARS = pl.BlockSpec(memory_space=pltpu.SMEM)


def wait_for(*arrays):
    CHAIN.extend(arrays)


def launch(body, *, out_shape, in_specs, out_specs, name, us, grid=(1,), scratch_shapes=(), input_output_aliases=None):
    single = not isinstance(out_shape, tuple)
    outs = (out_shape,) if single else out_shape
    specs = [out_specs] if single else list(out_specs)

    def call(*args):
        waits = tuple(CHAIN)
        n_in, n_out = len(args), len(outs)
        at = n_in + len(waits)

        def run(*refs):
            body(*refs[:n_in], *refs[at : at + n_out], *refs[at + n_out + 1 :])

        made = pl.pallas_call(
            run,
            grid=grid,
            out_shape=outs + (jax.ShapeDtypeStruct((8, 128), F32),),
            in_specs=list(in_specs) + anywhere(waits),
            out_specs=specs + anywhere((0,)),
            scratch_shapes=list(scratch_shapes),
            input_output_aliases=input_output_aliases or {},
            compiler_params=pltpu.CompilerParams(vmem_limit_bytes=(60 if name.startswith("pack") else 18 if name in ("feed_forward", "outer") else 10) * 2**20),
            cost_estimate=pl.CostEstimate(flops=int(us * SCALE), bytes_accessed=1, transcendentals=0),
            name=name,
        )(*args, *waits)
        CHAIN[:] = made[-1:]
        return made[0] if single else made[:-1]

    return call


def column_block(cols):
    return next(blk for blk in (512, 256, 128) if cols % blk == 0)


def join(parts, axis_new, splits=1):
    if axis_new:
        parts = [part[None] for part in parts]
    counts = [part.shape[0] for part in parts]
    shape = parts[0].shape[1:]
    cols = shape[-1]
    blk = column_block(cols)

    def spec(count):
        return pl.BlockSpec((count, *shape[:-1], blk), lambda j: (0,) * len(shape) + (j,))

    def body(*refs):
        outs = refs[len(counts) :]
        width = blk // len(outs)
        at = 0
        for ref, count in zip(refs, counts):
            for n, out in enumerate(outs):
                out[at : at + count] = ref[..., n * width : (n + 1) * width]
            at += count

    if splits > 1:
        blk = cols
        out = (sum(counts), *shape[:-1], cols // splits)
        return launch(
            body, out_shape=(jax.ShapeDtypeStruct(out, parts[0].dtype),) * splits, in_specs=[spec(count) for count in counts],
            out_specs=[whole_spec(out)] * splits, name="join", us=3,
        )(*parts)
    return launch(
        body, grid=(cols // blk,), out_shape=jax.ShapeDtypeStruct((sum(counts), *shape), parts[0].dtype),
        in_specs=[spec(count) for count in counts], out_specs=spec(sum(counts)), name="join", us=2,
    )(*parts)


def send_near(own, ring=False):
    got = []
    for k in range(1, lax.axis_size("fsdp")):
        got.append(from_next(got[-1] if ring and got else own, "fsdp", 1 if ring else k))
    return got


def far_bits():
    return list(reversed(context_bits()[1:]))


def spread_far(held, splits=1):
    for bit in far_bits():
        held = join([held, swap_context(held, bit)], False, splits if bit == far_bits()[-1] else 1)
    return held


def place_rows(place, shard, mine, other):
    nc, part, cols = shard.shape
    nf = lax.axis_size("fsdp")
    offsets = [reverse_bits(m) for m in range(nc)][: nc // 2]
    pieces = len(mine)
    blk = column_block(cols // pieces)
    steps = cols // pieces // blk

    def body(place_ref, shard_ref, *refs):
        out_ref = refs[-1]
        fi, ci = place_ref[0], place_ref[1]
        out_ref[fi] = shard_ref[...]

        def fill(mine_ref, other_ref):
            for k in range(1, nf):
                z = lax.rem(fi + k, nf)
                for m, off in enumerate(offsets):
                    at = m * (nf - 1) + k - 1
                    out_ref[z, lax.bitwise_xor(ci, off)] = mine_ref[at]
                    out_ref[z, lax.bitwise_xor(ci, off ^ 1)] = other_ref[at]

        for n in range(pieces):
            pl.when(pl.program_id(0) // steps == n)(lambda n=n: fill(refs[n], refs[pieces + n]))

    def columns(*leading):
        return pl.BlockSpec((*leading, blk), lambda j: (0,) * len(leading) + (j,))

    def piece(n):
        return pl.BlockSpec((count, part, blk), lambda j: (0, 0, jnp.clip(j - n * steps, 0, steps - 1)))

    count = mine[0].shape[0]
    full = launch(
        body,
        grid=(cols // blk,),
        out_shape=jax.ShapeDtypeStruct((nf, nc, part, cols), shard.dtype),
        in_specs=[SCALARS, columns(nc, part)] + [piece(n) for n in range(pieces)] * 2,
        out_specs=columns(nf, nc, part),
        name="place_rows",
        us=cols / 600,
    )(place, shard, *mine, *other)
    return full.reshape(nf * nc * part, cols)


def place_blocks(place, mine, other):
    half, units, rows, cols = mine.shape
    nc = 2 * half
    offsets = [reverse_bits(m) for m in range(nc)][:half]

    def body(place_ref, mine_ref, other_ref, out_ref):
        ci = place_ref[1]
        for u in range(units):
            for m, off in enumerate(offsets):
                for ref, bit in ((mine_ref, 0), (other_ref, 1)):
                    at = pl.multiple_of(lax.bitwise_xor(ci, off ^ bit) * rows, rows)
                    out_ref[u, pl.ds(at, rows), :] = ref[m, u]

    return launch(
        body,
        out_shape=jax.ShapeDtypeStruct((units, nc * rows, cols), mine.dtype),
        in_specs=[SCALARS, whole_spec(mine.shape), whole_spec(other.shape)],
        out_specs=whole_spec((units, nc * rows, cols)),
        name="place_blocks",
        us=1,
    )(place, mine, other)


def at_offset(ref_pair, ci, k, nc):
    off = lax.bitwise_xor(ci, k)
    entry, weight, rest = 0, nc // 2, off
    half = lax.div(off, 2)
    width = nc // 2
    index, bit = 0, width // 2
    low = 1
    while bit:
        index = index + lax.rem(lax.div(half, low), 2) * bit
        bit, low = bit // 2, low * 2
    same = lax.rem(off, 2) == 0
    mine, other = ref_pair
    return index, same, mine, other


def chain_states(place, spans, state_dim, local=None, unit=None):
    half, units, height, width = spans[0].shape
    nc = 2 * half
    blk = column_block(width)
    count = units if local is None else 1
    extra = () if local is None else tuple(local)

    def body(place_ref, *refs):
        ci = place_ref[1]
        out_ref = refs[-1]
        for n in range(count):
            u = n if local is None else unit
            total = jnp.zeros((state_dim, blk), F32)
            for k in range(nc - 1) if local is None else range(nc - 1, 0, -1):
                index, same, mine, other = at_offset(refs[:2], ci, k, nc)
                passing = jnp.where(same, mine[index, u, state_dim:].astype(F32), other[index, u, state_dim:].astype(F32))
                if local is None:
                    term = jnp.where(same, mine[index, u, :state_dim].astype(F32), other[index, u, :state_dim].astype(F32))
                    active = k < ci
                else:
                    term = jnp.where(same, refs[2][index, 0].astype(F32), refs[3][index, 0].astype(F32))
                    active = k > ci
                new = (passing[0:1] + passing[1:2]) * total + term
                total = jnp.where(active, new, total)
            out_ref[n] = total.astype(LOW)

    def columns(shape):
        return pl.BlockSpec((*shape[:-1], blk), lambda j: (0,) * (len(shape) - 1) + (j,))

    out = (count, state_dim, width)
    return launch(
        body,
        grid=(width // blk,),
        out_shape=jax.ShapeDtypeStruct(out, LOW),
        in_specs=[SCALARS] + [columns(arr.shape) for arr in (*spans, *extra)],
        out_specs=columns(out),
        name="chain_states",
        us=1.2,
    )(place, *spans, *extra)


def outer(place, left, right, into, at, width, last=None):
    nf, nc = lax.axis_size("fsdp"), lax.axis_size("context")
    tokens, model = left.shape
    cols = right.shape[1]
    part = model // (nf * nc)
    blk = next(b for b in (512, 256, 128) if cols % b == 0 and at % b == 0)
    given = () if into is None else tuple(into)
    lasts = () if last is None else (last,)

    def body(place_ref, left_ref, right_ref, *rest):
        away_ref, keep_ref, turned, made = rest[-4:]

        @pl.when(pl.program_id(0) == 0)
        def _():
            turned[...] = left_ref[...].T

        made[...] = nn_dot(turned[...], right_ref[...])
        if lasts:

            @pl.when(pl.program_id(0) == cols // blk - 1)
            def _():
                for top in range(0, model, part):
                    made[top : top + 8, blk - 128 :] = rest[len(given)][...]

        mine = lax.rem(place_ref[1], 2)
        for z in range(nf):
            for x in range(nc // 2):
                first = (z * nc + 2 * x) * part
                keep_ref[z, x] = made[pl.ds(pl.multiple_of(first + mine * part, part), part), :].astype(LOW)
                away_ref[z, x] = made[pl.ds(pl.multiple_of(first + (1 - mine) * part, part), part), :].astype(LOW)

    shape = jax.ShapeDtypeStruct((nf, nc // 2, part, width), LOW)
    spec = pl.BlockSpec((nf, nc // 2, part, blk), lambda j: (0, 0, 0, at // blk + j))
    return launch(
        body,
        grid=(cols // blk,),
        out_shape=(shape, shape),
        in_specs=[SCALARS, whole_spec((tokens, model)), pl.BlockSpec((tokens, blk), lambda j: (0, j))]
        + anywhere(given) + [whole_spec((8, 128)) for _ in lasts],
        out_specs=[spec, spec],
        input_output_aliases={3: 0, 4: 1} if given else {},
        scratch_shapes=[pltpu.VMEM((model, tokens), LOW), pltpu.VMEM((model, blk), F32)],
        name="outer",
        us=cols / 230,
    )(place, left, right, *given, *lasts)


def split_sum(place, keep, got, bit):
    n, left, rows, cols = keep.shape
    blk = column_block(cols)

    def body(place_ref, keep_ref, got_ref, away_ref, stay_ref):
        mine = lax.rem(lax.div(place_ref[1], bit), 2)
        for z in range(n):
            for j in range(left // 2):
                for ref, b in ((stay_ref, mine), (away_ref, 1 - mine)):
                    i = 2 * j + b
                    ref[z, j] = (keep_ref[z, i].astype(F32) + got_ref[z, i].astype(F32)).astype(LOW)

    def spec(count):
        return pl.BlockSpec((n, count, rows, blk), lambda j: (0, 0, 0, j))

    shape = jax.ShapeDtypeStruct((n, left // 2, rows, cols), LOW)
    return launch(
        body, grid=(cols // blk,), out_shape=(shape, shape), in_specs=[SCALARS, spec(left), spec(left)],
        out_specs=[spec(left // 2)] * 2, name="split_sum", us=cols / 900,
    )(place, keep, got)


def split_fsdp(place, keep, got):
    nf, _, part, cols = keep.shape
    blk = column_block(cols)

    def body(place_ref, keep_ref, got_ref, *outs):
        for k in range(nf):
            z = lax.rem(place_ref[0] + (nf - k), nf)
            outs[k][...] = (keep_ref[z, 0].astype(F32) + got_ref[z, 0].astype(F32)).astype(LOW)

    spec = pl.BlockSpec((nf, 1, part, blk), lambda j: (0, 0, 0, j))
    return launch(
        body, grid=(cols // blk,), out_shape=(jax.ShapeDtypeStruct((part, cols), LOW),) * nf, in_specs=[SCALARS, spec, spec],
        out_specs=[pl.BlockSpec((part, blk), lambda j: (0, j))] * nf, name="split_fsdp", us=cols / 1200,
    )(place, keep, got)


def ring_step(got, own):
    part, cols = own.shape
    blk = column_block(cols)

    def body(got_ref, own_ref, out_ref):
        out_ref[...] = (got_ref[...].astype(F32) + own_ref[...].astype(F32)).astype(LOW)

    spec = pl.BlockSpec((part, blk), lambda j: (0, j))
    return launch(
        body, grid=(cols // blk,), out_shape=jax.ShapeDtypeStruct((part, cols), LOW), in_specs=[spec, spec], out_specs=spec,
        name="ring_step", us=1,
    )(got, own)


def share_columns(total, first, last):
    mid = total[:, first:last]
    mid = (mid.astype(F32) + swap_tensor(mid).astype(F32)).astype(LOW)
    return jnp.concatenate([total[:, :first], mid, total[:, last:]], axis=1)


def sum_parts(parts, shared=(), ordered=None):
    cols = parts[0].shape[1]
    blk = column_block(cols)
    given = () if ordered is None else (ordered,)
    nf = len(parts)

    def body(*refs):
        some = refs[len(given) : -1]
        total = some[0][...].astype(F32)
        for ref in some[1:]:
            total = total + ref[...].astype(F32)
        refs[-1][...] = total.astype(LOW)
        if given:

            @pl.when(pl.program_id(0) == cols // blk - 1)
            def _():
                total = None
                for z in range(nf):
                    k = lax.rem(z + nf - refs[0][0], nf)
                    value = some[0][:, blk - 128 :].astype(F32)
                    for n in range(1, nf):
                        value = jnp.where(k == n, some[n][:, blk - 128 :].astype(F32), value)
                    total = value if total is None else total + value
                refs[-1][:, blk - 128 :] = total.astype(LOW)

    spec = pl.BlockSpec((parts[0].shape[0], blk), lambda j: (0, j))
    total = launch(
        body, grid=(cols // blk,), out_shape=jax.ShapeDtypeStruct(parts[0].shape, LOW),
        in_specs=[SCALARS] * len(given) + [spec] * nf, out_specs=spec, name="sum_parts", us=1.3,
    )(*given, *parts)
    if shared:
        mid = total[:, shared[0] : shared[1]]
        mid = (mid.astype(F32) + swap_tensor(mid).astype(F32)).astype(LOW)
        total = jnp.concatenate([total[:, : shared[0]], mid, total[:, shared[1] :]], axis=1)
    return total


def share_rows(total):
    held = total[None]
    for bit in reversed(context_bits()):
        held = jnp.concatenate([held, swap_context(held, bit)])
    ci = lax.axis_index("context")
    order = [reverse_bits(k) ^ reverse_bits(ci) for k in range(lax.axis_size("context"))]
    rows = jnp.stack([lax.dynamic_index_in_dim(held, m, 0, keepdims=False) for m in order])
    return rows.astype(F32).reshape(-1, total.shape[1])


def reduce_far(place, keep, got, bits):
    for bit in bits:
        away, keep = split_sum(place, keep, got, bit)
        got = swap_context(away, bit)
    return keep, got


def nt_dot(left, right):
    return lax.dot_general(left, right, (((1,), (1,)), ((), ())), preferred_element_type=F32)


def tn_dot(left, right):
    return lax.dot_general(left, right, (((0,), (0,)), ((), ())), preferred_element_type=F32)


def nn_dot(left, right):
    return jnp.dot(left, right, preferred_element_type=F32)


def document_start(lens_ref, unit, position):
    start, end = jnp.zeros_like(position), 0
    for d in range(lens_ref.shape[1]):
        end = end + lens_ref[unit, d]
        start = jnp.where(position >= end, end, start)
    return start


def lower_from(rows):
    u = lax.broadcasted_iota(jnp.int32, (rows, rows), 0)
    t = lax.broadcasted_iota(jnp.int32, (rows, rows), 1)
    return jnp.where(u <= t, 1.0, 0.0)


def project(place, lens, tokens, first, aux, q_dim, kv_dim, state, pairs):
    units = lens.shape[0]
    total, model = tokens.shape
    rows = total // units
    width = first.shape[1]
    at_b = q_dim + 2 * kv_dim
    at_dt = at_b + 2 * state

    def body(place_ref, lens_ref, x_ref, first_ref, aux_ref, n1_ref, q_ref, kv_ref, b_ref, c_ref, head_ref, gains_ref):
        unit = pl.program_id(0)

        @pl.when(unit == 0)
        def _():
            gains_ref[...] = first_ref[:, at_dt:].astype(F32).T[2 * pairs : 2 * pairs + 8]

        x = x_ref[...].astype(F32)
        scale = lax.rsqrt(jnp.mean(x * x, axis=1, keepdims=True) + EPSILON)
        n1_ref[...] = (x * scale * gains_ref[0:1, :]).astype(LOW)
        made = nn_dot(n1_ref[...], first_ref[...])
        q_ref[...] = (made[:, :q_dim].astype(LOW).astype(F32) * 0.125).astype(LOW)
        kv_ref[...] = made[:, q_dim:at_b].astype(LOW)
        b_ref[...] = made[:, at_b : at_b + state].astype(LOW)
        c_ref[...] = made[:, at_b + state : at_dt].astype(LOW)
        raw = made[:, at_dt:].T[:16] + aux_ref[:, 1:2]
        dt = jnp.maximum(raw, 0.0) + jnp.log1p(jnp.exp(-jnp.abs(raw)))
        decay = jnp.dot(-jnp.exp(aux_ref[:, 0:1]) * dt, lower_from(rows), precision=PRECISE, preferred_element_type=F32)
        base = place_ref[1] * rows
        position = base + lax.broadcasted_iota(jnp.int32, (1, rows), 1)
        carried = document_start(lens_ref, unit, position) < base
        closing = position >= document_start(lens_ref, unit, base + rows - 1)
        entering = jnp.where(carried, jnp.exp(decay), 0.0)
        leaving = jnp.where(closing, jnp.exp(decay[:, rows - 1 :] - decay), 0.0)
        for i in range(pairs):
            for at, value in enumerate((decay, dt, entering, leaving)):
                head_ref[i, 2 * at : 2 * at + 2, :] = value[2 * i : 2 * i + 2]

    def of_unit(cols):
        return pl.BlockSpec((rows, cols), lambda u: (u, 0))

    def made_as(cols):
        return jax.ShapeDtypeStruct((total, cols), LOW)

    return launch(
        body,
        grid=(units,),
        out_shape=(
            made_as(model), made_as(q_dim), made_as(2 * kv_dim), made_as(state), made_as(state),
            jax.ShapeDtypeStruct((units, pairs, 8, rows), F32), jax.ShapeDtypeStruct((8, model), F32),
        ),
        in_specs=[SCALARS, SCALARS, of_unit(model), whole_spec((model, width)), whole_spec((16, 2))],
        out_specs=[
            of_unit(model), of_unit(q_dim), of_unit(2 * kv_dim), of_unit(state), of_unit(state),
            pl.BlockSpec((None, pairs, 8, rows), lambda u: (u, 0, 0, 0)), whole_spec((8, model)),
        ],
        us=6.5, name="project",
    )(place, lens, tokens, first, aux)


def attention_forward(unit, place, lens, q, kv_all, into, width):
    units, length, _ = kv_all.shape
    rows, q_dim = q.shape[0] // units, q.shape[1]
    heads = q_dim // HEAD_WIDTH
    given = () if into is None else (into,)

    def body(place_ref, lens_ref, q_ref, kv_ref, *rest):
        o_ref, lse_ref, bias, top, low, acc = rest[-6:]
        top[...] = jnp.full_like(top, NEGATIVE)
        low[...] = jnp.zeros_like(low)
        acc[...] = jnp.zeros_like(acc)
        own = place_ref[1]
        base = own * rows
        start = document_start(lens_ref, unit, base + lax.broadcasted_iota(jnp.int32, (1, rows), 1))
        blocks = own - document_start(lens_ref, unit, base) // rows + 1

        def step(i, carry):
            j = own - i
            at = pl.multiple_of(j * rows, rows)
            keys = kv_ref[pl.ds(at, rows), :HEAD_WIDTH]
            turned = kv_ref[pl.ds(at, rows), :].astype(F32).T[HEAD_WIDTH:].astype(LOW)
            u = at + lax.broadcasted_iota(jnp.int32, (rows, rows), 0)
            t = base + lax.broadcasted_iota(jnp.int32, (rows, rows), 1)
            seen = (u <= t) & (u >= start)
            bias[...] = jnp.where(seen, 0.0, NEGATIVE)
            for h in range(heads):
                lanes = slice(h * HEAD_WIDTH, (h + 1) * HEAD_WIDTH)
                s = nt_dot(keys, q_ref[:, lanes]) + bias[...]
                before = top[h : h + 1, :]
                now = jnp.maximum(before, jnp.max(s, axis=0, keepdims=True))
                p = jnp.exp(s - now)
                scale = jnp.exp(before - now)
                top[h : h + 1, :] = now
                low[h : h + 1, :] = low[h : h + 1, :] * scale + jnp.sum(p, axis=0, keepdims=True)
                acc[lanes, :] = acc[lanes, :] * scale + nn_dot(turned, p.astype(LOW))
            return carry

        lax.fori_loop(0, blocks, step, 0)
        for h in range(heads):
            lanes = slice(h * HEAD_WIDTH, (h + 1) * HEAD_WIDTH)
            acc[lanes, :] = acc[lanes, :] / low[h : h + 1, :]
        o_ref[...] = acc[...].T.astype(LOW)
        lse_ref[...] = top[...] + jnp.log(low[...])

    return launch(
        body,
        grid=(1,),
        out_shape=(jax.ShapeDtypeStruct((units * rows, width), LOW), jax.ShapeDtypeStruct((8, rows), F32)),
        in_specs=[
            SCALARS, SCALARS, pl.BlockSpec((rows, q_dim), lambda i: (unit, 0)),
            pl.BlockSpec((None, length, 2 * HEAD_WIDTH), lambda i: (unit, 0, 0)),
        ] + anywhere(given),
        out_specs=[pl.BlockSpec((rows, q_dim), lambda i: (unit, 0)), whole_spec((8, rows))],
        input_output_aliases={4: 0} if given else {},
        scratch_shapes=[
            pltpu.VMEM((rows, rows), F32),
            pltpu.VMEM((8, rows), F32),
            pltpu.VMEM((8, rows), F32),
            pltpu.VMEM((q_dim, rows), F32),
        ],
        us=10.5, name="attention_forward",
    )(place, lens, q, kv_all, *given)


def attention_backward(unit, place, lens, q, dog, og, kv_all, lse):
    units, length, _ = kv_all.shape
    rows, q_dim = q.shape[0] // units, q.shape[1]
    heads = q_dim // HEAD_WIDTH
    half = (1, length // rows // 2, rows, 2 * HEAD_WIDTH)
    sub = min(256, rows)

    def body(place_ref, lens_ref, q_ref, do_ref, o_ref, kv_ref, lse_ref, *rest):
        dq_ref, away_ref, keep_ref, bias, dq_acc, delta = rest[-6:]
        own = place_ref[1]
        base = own * rows
        start = document_start(lens_ref, unit, base + lax.broadcasted_iota(jnp.int32, (1, rows), 1))
        blocks = own - document_start(lens_ref, unit, base) // rows + 1
        dq_acc[...] = jnp.zeros_like(dq_acc)
        away_ref[...] = jnp.zeros_like(away_ref)
        keep_ref[...] = jnp.zeros_like(keep_ref)
        both = do_ref[...].astype(F32) * o_ref[...].astype(F32)
        lane = lax.broadcasted_iota(jnp.int32, (rows, 128), 1)
        columns = jnp.zeros((rows, 128), F32)
        for h in range(heads):
            total = jnp.sum(both[:, h * HEAD_WIDTH : (h + 1) * HEAD_WIDTH], axis=1, keepdims=True)
            columns = jnp.where(lane == h, total, columns)
        delta[...] = columns.T[:8]

        def step(i, carry):
            j = own - i
            at = pl.multiple_of(j * rows, rows)
            u = at + lax.broadcasted_iota(jnp.int32, (rows, rows), 0)
            t = base + lax.broadcasted_iota(jnp.int32, (rows, rows), 1)
            seen = (u <= t) & (u >= start)
            bias[...] = jnp.where(seen, 0.0, NEGATIVE)
            for r in range(0, rows, sub):
                keys = kv_ref[pl.ds(pl.multiple_of(at + r, sub), sub), :HEAD_WIDTH]
                values = kv_ref[pl.ds(pl.multiple_of(at + r, sub), sub), HEAD_WIDTH:]
                dk = jnp.zeros((sub, HEAD_WIDTH), F32)
                dv = jnp.zeros((sub, HEAD_WIDTH), F32)
                for h in range(heads):
                    lanes = slice(h * HEAD_WIDTH, (h + 1) * HEAD_WIDTH)
                    q_h, do_h = q_ref[:, lanes], do_ref[:, lanes]
                    p = jnp.exp(nt_dot(keys, q_h) + (bias[r : r + sub, :] - lse_ref[h : h + 1, :]))
                    ds = (p * (nt_dot(values, do_h) - delta[h : h + 1, :])).astype(LOW)
                    dv = dv + nn_dot(p.astype(LOW), do_h)
                    dk = dk + nn_dot(ds, q_h)
                    dq_acc[:, lanes] = dq_acc[:, lanes] + tn_dot(ds, keys)
                dkv = jnp.concatenate([dk, dv], axis=1).astype(LOW)

                @pl.when(lax.rem(own - j, 2) == 0)
                def _():
                    keep_ref[0, j // 2, r : r + sub, :] = dkv

                @pl.when(lax.rem(own - j, 2) == 1)
                def _():
                    away_ref[0, j // 2, r : r + sub, :] = dkv
            return carry

        lax.fori_loop(0, blocks, step, 0)
        dq_ref[...] = (dq_acc[...] * 0.125).astype(LOW)

    return launch(
        body,
        out_shape=(jax.ShapeDtypeStruct((rows, q_dim), LOW),) + (jax.ShapeDtypeStruct(half, LOW),) * 2,
        grid=(1,),
        in_specs=[
            SCALARS, SCALARS, pl.BlockSpec((rows, q_dim), lambda i: (unit, 0)), whole_spec((rows, q_dim)),
            pl.BlockSpec((rows, q_dim), lambda i: (unit, 0)), pl.BlockSpec((None, length, 2 * HEAD_WIDTH), lambda i: (unit, 0, 0)),
            whole_spec((8, rows)),
        ],
        out_specs=[whole_spec((rows, q_dim)), whole_spec(half), whole_spec(half)],
        scratch_shapes=[
            pltpu.VMEM((rows, rows), F32),
            pltpu.VMEM((rows, q_dim), F32),
            pltpu.VMEM((8, rows), F32),
        ],
        us=17, name="attention_backward",
    )(place, lens, q, dog, og, kv_all, lse)


def halves(columns, first, lane):
    return jnp.where(lane < 64, columns[:, first : first + 1], columns[:, first + 1 : first + 2])


def mamba_state(unit, per_head, left, zx, right=None, first=0):
    _, pairs, _, rows = per_head.shape
    state = left.shape[1]
    rights = () if right is None else (right,)
    height = state if rights else state + 16

    def body(head_ref, left_ref, zx_ref, *rest):
        out_ref = rest[-1]
        lane = lax.broadcasted_iota(jnp.int32, (rows, 128), 1)
        turned = left_ref[...].astype(F32).T.astype(LOW)
        for i in range(pairs):
            lanes = slice(128 * i, 128 * (i + 1))
            by_col = head_ref[i].T
            if rights:
                z = zx_ref[:, 256 * i : 256 * i + 128].astype(F32)
                value = rest[0][:, first + 128 * i : first + 128 * (i + 1)].astype(F32) * z * jax.nn.sigmoid(z)
                weight = halves(by_col, 4, lane)
            else:
                value = zx_ref[:, 256 * i + 128 : 256 * (i + 1)].astype(F32)
                weight = halves(by_col, 2, lane) * halves(by_col, 6, lane)
                passing = halves(by_col[rows - 16 :], 4, lane[:16])[15:]
                high = passing.astype(LOW).astype(F32)
                row = lax.broadcasted_iota(jnp.int32, (16, 128), 0)
                out_ref[state:, lanes] = jnp.where(row == 0, high, jnp.where(row == 1, passing - high, 0.0)).astype(LOW)
            out_ref[:state, lanes] = nn_dot(turned, (value * weight).astype(LOW)).astype(LOW)

    return launch(
        body,
        grid=(1,),
        out_shape=jax.ShapeDtypeStruct((height, 128 * pairs), LOW),
        in_specs=[
            pl.BlockSpec((None, pairs, 8, rows), lambda i: (unit, 0, 0, 0)), pl.BlockSpec((rows, state), lambda i: (unit, 0)),
            pl.BlockSpec((rows, 256 * pairs), lambda i: (unit, 0)),
        ] + [whole_spec(r.shape) for r in rights],
        out_specs=whole_spec((height, 128 * pairs)),
        us=2, name="mamba_state",
    )(per_head, left, zx, *rights)


def same_document(place_ref, lens_ref, unit, rows, t_axis):
    base = place_ref[1] * rows
    shape = (1, rows) if t_axis else (rows, 1)
    start = document_start(lens_ref, unit, base + lax.broadcasted_iota(jnp.int32, shape, t_axis)) - base
    t = lax.broadcasted_iota(jnp.int32, (rows, rows), t_axis)
    u = lax.broadcasted_iota(jnp.int32, (rows, rows), 1 - t_axis)
    return (u <= t) & (u >= start)


def mamba_forward(unit, place, lens, per_head, zx, b, c, state_in, skip, into, first):
    _, pairs, _, rows = per_head.shape
    blk = min(256, rows)
    state = b.shape[1]

    def body(place_ref, lens_ref, head_ref, zx_ref, b_ref, c_ref, state_ref, skip_ref, *rest):
        g_ref, y_ref, inner, x_dt = rest[-4:]

        @pl.when(pl.program_id(0) == 0)
        def _():
            seen = same_document(place_ref, lens_ref, unit, rows, 0)
            inner[...] = jnp.where(seen, nt_dot(c_ref[...], b_ref[...]), 0.0)

        lane = lax.broadcasted_iota(jnp.int32, (rows, 128), 1)
        by_row = head_ref[...]
        by_col = by_row.T
        xs_f = zx_ref[:, 128:].astype(F32)
        x_dt[...] = (xs_f * halves(by_col, 2, lane)).astype(LOW)
        read = nn_dot(c_ref[...], state_ref[...]) * halves(by_col, 4, lane)
        for i in range(rows // blk):
            part = slice(i * blk, (i + 1) * blk)
            sums = []
            for h in range(2):
                total = None
                for j in range(i + 1):
                    other = slice(j * blk, (j + 1) * blk)
                    gap = by_col[part, h : h + 1] - by_row[h : h + 1, other]
                    kernel = jnp.exp(jnp.minimum(gap, 0.0)) * inner[part, other]
                    term = nn_dot(kernel.astype(LOW), x_dt[other, :])
                    total = term if total is None else total + term
                sums.append(total)
            y = jnp.where(lane[part] < 64, sums[0], sums[1]) + read[part]
            y_ref[part, :] = y
            z_f = zx_ref[part, :128].astype(F32)
            g_ref[part, :] = ((y + skip_ref[...] * xs_f[part]) * z_f * jax.nn.sigmoid(z_f)).astype(LOW)

    return launch(
        body,
        grid=(pairs,),
        out_shape=(jax.ShapeDtypeStruct(into.shape, LOW), jax.ShapeDtypeStruct((rows, 128 * pairs), F32)),
        in_specs=[
            SCALARS, SCALARS, pl.BlockSpec((None, None, 8, rows), lambda i: (unit, i, 0, 0)), pl.BlockSpec((rows, 256), lambda i: (unit, i)),
            pl.BlockSpec((rows, state), lambda i: (unit, 0)), pl.BlockSpec((rows, state), lambda i: (unit, 0)),
            pl.BlockSpec((None, state, 128), lambda i: (unit, 0, i)), pair_spec(1),
        ] + anywhere((into,)),
        out_specs=[pl.BlockSpec((rows, 128), lambda i: (unit, first // 128 + i)), pair_spec(rows)],
        input_output_aliases={8: 0},
        scratch_shapes=[pltpu.VMEM((rows, rows), F32), pltpu.VMEM((rows, 128), LOW)],
        us=7.5, name="mamba_forward",
    )(place, lens, per_head, zx, b, c, state_in, skip, into)


def mamba_backward(unit, place, lens, per_head, zx, y, dog, first, b, c, state_in, later, skip, aux, into):
    _, pairs, _, rows = per_head.shape
    blk = min(256, rows)
    state = b.shape[1]
    given = () if into is None else tuple(into)

    def body(place_ref, lens_ref, head_ref, zx_ref, y_ref, dg_ref, b_ref, c_ref, state_ref, later_ref, skip_ref, aux_ref, *rest):
        dzx_ref, dbc_ref, grads_ref, inner, d_inner, dy_low, x_low, db, dc, stats = rest[-10:]
        pair = pl.program_id(0)

        @pl.when(pair == 0)
        def _():
            seen = same_document(place_ref, lens_ref, unit, rows, 1)
            inner[...] = jnp.where(seen, nt_dot(b_ref[...], c_ref[...]), 0.0)
            d_inner[...] = jnp.zeros_like(d_inner)
            db[...] = jnp.zeros_like(db)
            dc[...] = jnp.zeros_like(dc)

        lane = lax.broadcasted_iota(jnp.int32, (rows, 128), 1)
        by_row = head_ref[pair]
        by_col = by_row.T
        xs_f = zx_ref[:, 128:].astype(F32)
        z_f = zx_ref[:, :128].astype(F32)
        sig = jax.nn.sigmoid(z_f)
        d_gate = dg_ref[...].astype(F32)
        d_y = d_gate * z_f * sig
        y_core = y_ref[...]
        dzx_ref[:, :128] = (d_gate * (y_core + skip_ref[...] * xs_f) * sig * (1.0 + z_f * (1.0 - sig))).astype(LOW)
        dy_low[...] = d_y.astype(LOW)
        dt = halves(by_col, 2, lane)
        x_dt = xs_f * dt
        x_low[...] = x_dt.astype(LOW)
        closing = halves(by_col, 6, lane)
        from_later = nn_dot(b_ref[...], later_ref[...]) * closing
        db[...] += nt_dot((x_dt * closing).astype(LOW), later_ref[...])
        dc[...] += nt_dot((d_y * halves(by_col, 4, lane)).astype(LOW), state_ref[...])
        count = rows // blk
        columns = jnp.zeros((rows, 128), F32)
        d_x_parts = []
        for j in range(count):
            part = slice(j * blk, (j + 1) * blk)
            sums = []
            for h in range(2):
                own = (lane[part] < 64) if h == 0 else (lane[part] >= 64)
                x_h = jnp.where(own, x_low[part, :].astype(F32), 0.0).astype(LOW)
                total = None
                for i in range(j, count):
                    other = slice(i * blk, (i + 1) * blk)
                    gap = by_row[h : h + 1, other] - by_col[part, h : h + 1]
                    decay = jnp.exp(jnp.minimum(gap, 0.0))
                    term = nn_dot((decay * inner[part, other]).astype(LOW), dy_low[other, :])
                    total = term if total is None else total + term
                    d_inner[part, other] += decay * nt_dot(x_h, dy_low[other, :])
                sums.append(total)
            d_x_parts.append(jnp.where(lane[part] < 64, sums[0], sums[1]))
        d_x = jnp.concatenate(d_x_parts, axis=0) if count > 1 else d_x_parts[0]
        d_x = d_x + from_later
        dzx_ref[:, 128:] = (d_x * dt + skip_ref[...] * d_y).astype(LOW)
        rounded_x = x_low[...].astype(F32)
        rounded_dy = dy_low[...].astype(F32)
        carried_back = jnp.sum(later_ref[...].astype(F32) * state_ref[...].astype(F32), axis=0, keepdims=True)
        row = lax.broadcasted_iota(jnp.int32, (rows, 1), 0)
        for at, value in enumerate((d_x * xs_f, rounded_dy * y_core - rounded_x * d_x, rounded_x * from_later, d_y * xs_f)):
            for h in range(2):
                own = (lane < 64) if h == 0 else (lane >= 64)
                total = jnp.sum(jnp.where(own, value, 0.0), axis=1, keepdims=True)
                if at == 2:
                    own = (lane[:1] < 64) if h == 0 else (lane[:1] >= 64)
                    passed = jnp.sum(jnp.where(own, carried_back, 0.0), axis=1, keepdims=True)
                    total = total + jnp.where(row == rows - 1, passed * by_row[4 + h : 5 + h, rows - 1 :], 0.0)
                columns = jnp.where(lane == 2 * at + h, total, columns)
        stats[pair] = columns.T[:8]

        @pl.when(pair == pairs - 1)
        def _():
            seen = same_document(place_ref, lens_ref, unit, rows, 1)
            low = jnp.where(seen, d_inner[...], 0.0).astype(LOW)
            dbc_ref[:, :state] = (db[...] + nn_dot(low, c_ref[...])).astype(LOW)
            dbc_ref[:, state : 2 * state] = (dc[...] + tn_dot(low, b_ref[...])).astype(LOW)

            def heads_of(ref, at):
                blank = jnp.zeros((16 - 2 * pairs, rows), F32)
                parts = [ref[i, 2 * at : 2 * at + 2, :] for i in range(pairs)]
                return jnp.concatenate(parts + [blank] * (2 * pairs < 16), axis=0)

            dt = heads_of(head_ref, 1)
            rate = -jnp.exp(aux_ref[:, 0:1])
            position = lax.broadcasted_iota(jnp.int32, (1, rows), 1)
            d_end = jnp.sum(heads_of(stats, 2), axis=1, keepdims=True)
            d_decay = heads_of(stats, 1) + jnp.where(position == rows - 1, d_end, 0.0)
            d_rate = lax.dot_general(
                d_decay, lower_from(rows), (((1,), (1,)), ((), ())), precision=PRECISE, preferred_element_type=F32)
            d_raw = (heads_of(stats, 0) + rate * d_rate) * (1.0 - jnp.exp(-dt))
            turned = jnp.concatenate([d_raw, jnp.zeros((112, rows), F32)], axis=0).T
            dbc_ref[:, 2 * state : 2 * state + 128] = turned.astype(LOW)
            dbc_ref[:, 2 * state + 128 :] = jnp.zeros((rows, 128), LOW)
            lanes = lax.broadcasted_iota(jnp.int32, (16, 128), 1)
            sums = jnp.zeros((16, 128), F32)
            for at, value in enumerate((d_rate * rate * dt, d_raw, heads_of(stats, 3))):
                sums = jnp.where(lanes == at, jnp.sum(value, axis=1, keepdims=True), sums)
            grads_ref[...] = sums

    total = zx.shape[0]
    return launch(
        body,
        grid=(pairs,),
        out_shape=(
            jax.ShapeDtypeStruct(zx.shape, LOW), jax.ShapeDtypeStruct((total, 2 * state + 256), LOW),
            jax.ShapeDtypeStruct((16, 128), F32),
        ),
        in_specs=[
            SCALARS, SCALARS, pl.BlockSpec((None, pairs, 8, rows), lambda i: (unit, 0, 0, 0)),
            pl.BlockSpec((rows, 256), lambda i: (unit, i)), pair_spec(rows),
            pl.BlockSpec((rows, 128), lambda i: (0, first // 128 + i)),
            pl.BlockSpec((rows, state), lambda i: (unit, 0)), pl.BlockSpec((rows, state), lambda i: (unit, 0)),
            pl.BlockSpec((None, state, 128), lambda i: (unit, 0, i)), pair_spec(state), pair_spec(1), whole_spec((16, 2)),
        ] + anywhere(given),
        out_specs=[
            pl.BlockSpec((rows, 256), lambda i: (unit, i)), pl.BlockSpec((rows, 2 * state + 256), lambda i: (unit, 0)),
            whole_spec((16, 128)),
        ],
        input_output_aliases={12: 0, 13: 1} if given else {},
        scratch_shapes=[
            pltpu.VMEM((rows, rows), F32), pltpu.VMEM((rows, rows), F32), pltpu.VMEM((rows, 128), LOW), pltpu.VMEM((rows, 128), LOW),
            pltpu.VMEM((rows, state), F32), pltpu.VMEM((rows, state), F32), pltpu.VMEM((pairs, 8, rows), F32),
        ],
        us=16.3, name="mamba_backward",
    )(place, lens, per_head, zx, y, dog, b, c, state_in, later, skip, aux, *given)


def feed_forward(unit, x, ours, theirs, gains, dy, weights, into):
    rows, model = ours.shape
    total = x.shape[0]
    hidden = weights.shape[1] // 3
    blk = min(256, hidden)
    count = hidden // blk
    given = () if into is None else tuple(into)

    def body(x_ref, ours_ref, theirs_ref, gains_ref, dy_ref, ab_ref, down_ref, *rest):
        h1_ref, n2_ref, f_ref, dab_ref, dn2_ref, dn2_acc = rest[-6:]

        @pl.when(pl.program_id(0) == 0)
        def _():
            h1 = x_ref[...].astype(F32) + (ours_ref[...].astype(F32) + theirs_ref[...].astype(F32))
            scale = lax.rsqrt(jnp.mean(h1 * h1, axis=1, keepdims=True) + EPSILON)
            h1_ref[...] = h1
            n2_ref[...] = (h1 * scale * gains_ref[1:2, :]).astype(LOW)

        ab = nn_dot(n2_ref[...], ab_ref[...])
        a, b = ab[:, :blk], ab[:, blk:]
        sig = jax.nn.sigmoid(a)
        silu = a * sig
        f = (silu * b).astype(LOW)
        f_ref[...] = f
        df = nn_dot(dy_ref[...], down_ref[...])
        dab_ref[:, :blk] = (df * b * sig * (1.0 + a * (1.0 - sig))).astype(LOW)
        dab_ref[:, blk:] = (df * silu).astype(LOW)
        dn2 = nt_dot(dab_ref[...], ab_ref[...])

        @pl.when(pl.program_id(0) == 0)
        def _():
            dn2_acc[...] = dn2

        @pl.when(pl.program_id(0) > 0)
        def _():
            dn2_acc[...] += dn2

        @pl.when(pl.program_id(0) == count - 1)
        def _():
            dn2_ref[...] = dn2_acc[...].astype(LOW)

    at_unit = pl.BlockSpec((rows, model), lambda j: (unit, 0))
    return launch(
        body,
        grid=(count,),
        out_shape=(
            jax.ShapeDtypeStruct((total, model), F32), jax.ShapeDtypeStruct((total, model), LOW),
            jax.ShapeDtypeStruct((total, hidden), LOW), jax.ShapeDtypeStruct((total, 2 * hidden), LOW),
            jax.ShapeDtypeStruct((rows, model), LOW),
        ),
        in_specs=[
            at_unit, whole_spec((rows, model)), whole_spec((rows, model)), whole_spec((8, model)), at_unit,
            pl.BlockSpec((model, 2 * blk), lambda j: (0, j)), pl.BlockSpec((model, blk), lambda j: (0, 2 * count + j)),
        ] + anywhere(given),
        out_specs=[
            at_unit, at_unit, pl.BlockSpec((rows, blk), lambda j: (unit, j)), pl.BlockSpec((rows, 2 * blk), lambda j: (unit, j)),
            whole_spec((rows, model)),
        ],
        input_output_aliases={7: 0, 8: 1, 9: 2, 10: 3} if given else {},
        scratch_shapes=[pltpu.VMEM((rows, model), F32)],
        us=14, name="feed_forward",
    )(x, ours, theirs, gains, dy, weights, weights, *given)


def feed_forward_out(f, weights):
    total, hidden = f.shape
    model = weights.shape[0]
    blk = min(512, total)

    def body(f_ref, down_ref, *rest):
        rest[-1][...] = nt_dot(f_ref[...], down_ref[...]).astype(LOW)

    return launch(
        body,
        grid=(total // blk,),
        out_shape=jax.ShapeDtypeStruct((total, model), LOW),
        in_specs=[pl.BlockSpec((blk, hidden), lambda i: (i, 0)), pl.BlockSpec((model, hidden), lambda i: (0, 2))],
        out_specs=pl.BlockSpec((blk, model), lambda i: (i, 0)),
        us=5, name="feed_forward_out",
    )(f, weights)


def norm_gradient(hidden, gain, d_normed):
    inv = lax.rsqrt(jnp.mean(hidden * hidden, axis=1, keepdims=True) + EPSILON)
    weighted = gain * d_normed
    mean = jnp.mean(weighted * hidden, axis=1, keepdims=True)
    normed = hidden * inv
    return inv * weighted - normed * (inv * inv * mean), jnp.sum(d_normed * normed, axis=0, keepdims=True)


def middle_backward(unit, h1, ours, theirs, gains, dy, third, into):
    rows, model = ours.shape
    width = third.shape[1]
    given = () if into is None else (into,)

    def body(h1_ref, ours_ref, theirs_ref, gains_ref, dy_ref, third_ref, *rest):
        dm_ref, dh_ref, dog_ref, sum_ref = rest[-4:]
        dn2 = ours_ref[...].astype(F32) + theirs_ref[...].astype(F32)
        dh, terms = norm_gradient(h1_ref[...], gains_ref[1:2, :], dn2)
        dh = dh + dy_ref[...].astype(F32)
        dh_ref[...] = dh
        dm = dh.astype(LOW)
        dm_ref[...] = dm
        dog_ref[...] = nn_dot(dm, third_ref[...]).astype(LOW)
        sum_ref[...] = jnp.broadcast_to(terms, sum_ref.shape)

    at_unit = pl.BlockSpec((rows, model), lambda i: (unit, 0))
    full = whole_spec((rows, model))
    return launch(
        body,
        grid=(1,),
        out_shape=(
            jax.ShapeDtypeStruct(h1.shape, LOW), jax.ShapeDtypeStruct((rows, model), F32),
            jax.ShapeDtypeStruct((rows, width), LOW), jax.ShapeDtypeStruct((8, model), F32),
        ),
        in_specs=[at_unit, full, full, whole_spec((8, model)), at_unit, whole_spec((model, width))] + anywhere(given),
        out_specs=[at_unit, full, whole_spec((rows, width)), whole_spec((8, model))],
        input_output_aliases={6: 0} if given else {},
        us=5.4, name="middle_backward",
    )(h1, ours, theirs, gains, dy, third, *given)


def input_backward(unit, dq, keep, got, dbc, dzx, first, second, x, into):
    rows, q_dim = dq.shape
    model = first.shape[0]
    blk = 256 if model % 256 == 0 else model
    rest_width = dbc.shape[1]
    width = q_dim + keep.shape[-1]
    rest = first.shape[1] - width
    given = () if into is None else (into,)

    def body(dq_ref, keep_ref, got_ref, dbc_ref, dzx_ref, first_ref, second_ref, x_ref, *others):
        dqkv_ref, part_ref, sum_ref, inv = others[-4:]
        j = pl.program_id(0)

        @pl.when(j == 0)
        def _():
            x = x_ref[...].astype(F32)
            scale = lax.rsqrt(jnp.mean(x * x, axis=1, keepdims=True) + EPSILON)
            inv[...] = jnp.broadcast_to(scale, inv.shape)
            dqkv_ref[:, :q_dim] = dq_ref[...]
            dqkv_ref[:, q_dim:] = (keep_ref[0, 0].astype(F32) + got_ref[0, 0].astype(F32)).astype(LOW)

        part = nt_dot(dqkv_ref[...], first_ref[:, :width]) + nt_dot(dbc_ref[:, :rest], first_ref[:, width:])
        part = part + nt_dot(dzx_ref[...], second_ref[...])
        part_ref[...] = part.astype(LOW)
        x = x_ref[:, pl.ds(pl.multiple_of(j * blk, blk), blk)].astype(F32)
        terms = jnp.sum(part * x * inv[:, :1], axis=0, keepdims=True)
        sum_ref[...] = jnp.broadcast_to(terms, sum_ref.shape)

    return launch(
        body,
        grid=(model // blk,),
        out_shape=(
            jax.ShapeDtypeStruct((x.shape[0], width), LOW), jax.ShapeDtypeStruct((rows, model), LOW), jax.ShapeDtypeStruct((8, model), F32),
        ),
        in_specs=[
            whole_spec((rows, q_dim)), whole_spec(keep.shape), whole_spec(keep.shape), pl.BlockSpec((rows, rest_width), lambda j: (unit, 0)),
            pl.BlockSpec((rows, dzx.shape[1]), lambda j: (unit, 0)), pl.BlockSpec((blk, first.shape[1]), lambda j: (j, 0)),
            pl.BlockSpec((blk, second.shape[1]), lambda j: (j, 0)), pl.BlockSpec((rows, model), lambda j: (unit, 0)),
        ] + anywhere(given),
        out_specs=[
            pl.BlockSpec((rows, width), lambda j: (unit, 0)), pl.BlockSpec((rows, blk), lambda j: (0, j)),
            pl.BlockSpec((8, blk), lambda j: (0, j)),
        ],
        input_output_aliases={8: 0} if given else {},
        scratch_shapes=[pltpu.VMEM((rows, 128), F32)],
        us=6.5, name="input_backward",
    )(dq, keep, got, dbc, dzx, first, second, x, *given)


def finish(unit, x, ours, theirs, gains, dh, into):
    rows, model = ours.shape
    given = () if into is None else (into,)

    def body(x_ref, ours_ref, theirs_ref, gains_ref, dh_ref, *rest):
        dn1 = ours_ref[...].astype(F32) + theirs_ref[...].astype(F32)
        dx, _ = norm_gradient(x_ref[...].astype(F32), gains_ref[0:1, :], dn1)
        rest[-1][...] = dx + dh_ref[...]

    at_unit = pl.BlockSpec((rows, model), lambda i: (unit, 0))
    full = whole_spec((rows, model))
    return launch(
        body,
        grid=(1,),
        out_shape=jax.ShapeDtypeStruct(x.shape, F32),
        in_specs=[at_unit, full, full, whole_spec((8, model)), full] + anywhere(given),
        out_specs=at_unit,
        input_output_aliases={5: 0} if given else {},
        us=4.2, name="finish",
    )(x, ours, theirs, gains, dh, *given)


def pack(place, parts, cols, name):
    arrays = []
    for arr, *_ in parts:
        if not any(arr is other for other in arrays):
            arrays.append(arr)
    where = [next(i for i, other in enumerate(arrays) if other is part[0]) for part in parts]
    nc = lax.axis_size("context")
    rows = arrays[0].shape[1] if parts[0][4] else arrays[0].shape[0]
    filled = max(part[1] + part[2] for part in parts)

    def body(place_ref, *refs):
        out_ref, own_ref = refs[-2:]
        if filled < cols:
            start = filled - filled % 128
            out_ref[:, start:] = jnp.zeros((rows, cols - start), LOW)
        for n, (_, at, width, first, turned) in zip(where, parts):
            if turned:
                out_ref[:, at : at + width] = refs[n][...].astype(F32).T.astype(LOW)
            else:
                out_ref[:, at : at + width] = refs[n][:, first : first + width]
        own_ref[...] = out_ref[pl.ds(pl.multiple_of(place_ref[1] * (rows // nc), rows // nc), rows // nc), :]

    return launch(
        body, out_shape=(jax.ShapeDtypeStruct((rows, cols), LOW), jax.ShapeDtypeStruct((rows // nc, cols), LOW)),
        in_specs=[SCALARS] + [whole_spec(arr.shape) for arr in arrays],
        out_specs=[whole_spec((rows, cols)), whole_spec((rows // nc, cols))], name=name, us=2,
    )(place, *arrays)


def emit(place, held, got, outs, name):
    half, part, _ = held.shape
    low = min(first for pieces, _ in outs for first, _ in pieces)
    low -= low % 128
    cols = max(first + width for pieces, _ in outs for first, width in pieces) - low
    cols += -cols % 128
    nc = 2 * half
    rows = nc * part
    offsets = [reverse_bits(m) for m in range(nc)][:half]
    widths = [sum(width for _, width in pieces) for pieces, _ in outs]

    def body(place_ref, held_ref, got_ref, *refs):
        whole = refs[-1]
        ci = place_ref[1]
        for m, off in enumerate(offsets):
            for ref, bit in ((held_ref, 0), (got_ref, 1)):
                at = pl.multiple_of(lax.bitwise_xor(ci, off ^ bit) * part, part)
                whole[pl.ds(at, part), :] = ref[m, :, low : low + cols].astype(F32)
        for ref, (pieces, turned) in zip(refs, outs):
            to = 0
            for first, width in pieces:
                if turned:
                    ref[to : to + width, :] = whole[:, first - low : first - low + width].T
                else:
                    ref[:, to : to + width] = whole[:, first - low : first - low + width]
                to += width

    shapes = [(width, rows) if turned else (rows, width) for width, (_, turned) in zip(widths, outs)]
    return launch(
        body, out_shape=tuple(jax.ShapeDtypeStruct(shape, F32) for shape in shapes),
        in_specs=[SCALARS, whole_spec(held.shape), whole_spec(held.shape)], out_specs=[whole_spec(shape) for shape in shapes],
        scratch_shapes=[pltpu.VMEM((rows, cols), F32)], name=name, us=3,
    )(place, held, got)


def close_forward(h1, ours, theirs):
    total, model = h1.shape
    blk = min(256, total)

    def body(h1_ref, ours_ref, theirs_ref, out_ref):
        out_ref[...] = (h1_ref[...] + (ours_ref[...].astype(F32) + theirs_ref[...].astype(F32))).astype(LOW)

    spec = pl.BlockSpec((blk, model), lambda i: (i, 0))
    return launch(
        body, grid=(total // blk,), out_shape=jax.ShapeDtypeStruct((total, model), LOW), in_specs=[spec] * 3, out_specs=spec,
        name="close_forward", us=4,
    )(h1, ours, theirs)


def project_mixer(n1, second):
    tokens, model = n1.shape
    cols = second.shape[1]
    blk = column_block(cols)

    def body(n1_ref, second_ref, out_ref):
        out_ref[...] = nn_dot(n1_ref[...], second_ref[...]).astype(LOW)

    return launch(
        body, grid=(cols // blk,), out_shape=jax.ShapeDtypeStruct((tokens, cols), LOW),
        in_specs=[whole_spec((tokens, model)), pl.BlockSpec((model, blk), lambda j: (0, j))],
        out_specs=pl.BlockSpec((tokens, blk), lambda j: (0, j)), name="project_mixer", us=5,
    )(n1, second)


def mixer_out(unit, og, third, rows):
    width = og.shape[1]
    model = third.shape[0]
    blk = column_block(model)

    def body(og_ref, third_ref, out_ref):
        out_ref[...] = nt_dot(og_ref[...], third_ref[...]).astype(LOW)

    return launch(
        body, grid=(model // blk,), out_shape=jax.ShapeDtypeStruct((rows, model), LOW),
        in_specs=[pl.BlockSpec((rows, width), lambda j: (unit, 0)), pl.BlockSpec((blk, width), lambda j: (j, 0))],
        out_specs=pl.BlockSpec((rows, blk), lambda j: (0, j)), name="mixer_out", us=2,
    )(og, third)


def turns(first, second, width):
    count = first.shape[-1] // width
    parts = [arr[..., width * i : width * (i + 1)] for i in range(count) for arr in (first, second)]
    return jnp.concatenate(parts, axis=-1)


def unturned(mixed, width, which):
    count = mixed.shape[-1] // (2 * width)
    return jnp.concatenate([mixed[..., width * (2 * i + which) : width * (2 * i + which + 1)] for i in range(count)], axis=-1)


def per_device(
    tokens, cotangent, doc_lengths, mixer_gain, w_query, key_matrix, value_matrix, mamba_gate_weight,
    mamba_input_weight, w_bproj, w_cproj, w_dt, a_log, dt_bias, d_skip, w_attn_out, w_mixer_out,
    ffn_gain, w_gate, w_up, w_down,
):
    CHAIN.clear()
    micro_count, seq_count, block_len, model_dim = tokens.shape
    rows_here = mixer_gain.shape[0]
    heads = w_dt.shape[1]
    ssm_dim = mamba_gate_weight.shape[1]
    head_dim = ssm_dim // heads
    q_dim = w_query.shape[1]
    kv_dim = key_matrix.shape[1]
    state_dim = w_bproj.shape[1]
    ff_dim = w_gate.shape[1]
    ff_blk = min(256, ff_dim)
    ci = lax.axis_index("context")
    nc = lax.axis_size("context")
    full_len = nc * block_len
    units = micro_count * seq_count
    pairs = heads // 2
    tokens_here = units * block_len
    at_b = q_dim + 2 * kv_dim
    at_c = at_b + state_dim
    at_dt = at_c + state_dim
    at_gain = at_dt + heads
    first_width = at_gain + 2 + -(at_gain + 2) % 128

    place = jnp.stack([lax.axis_index("fsdp"), ci]).astype(jnp.int32)
    at_k, at_v = q_dim, q_dim + kv_dim
    two = 2 * head_dim
    first, own_first = pack(
        place,
        [(w_query, 0, q_dim, 0, False), (key_matrix.T, at_k, kv_dim, 0, True), (value_matrix.T, at_v, kv_dim, 0, True),
         (w_bproj, at_b, state_dim, 0, False), (w_cproj, at_c, state_dim, 0, False), (w_dt.T, at_dt, heads, 0, True),
         (jnp.stack([mixer_gain, ffn_gain]), at_gain, 2, 0, True)],
        first_width, "pack_first")
    near_first = send_near(own_first)
    second, own_second = pack(
        place,
        [(arr, (2 * i + n) * two, two, i * two, False)
         for i in range(pairs) for n, arr in enumerate((mamba_gate_weight, mamba_input_weight))],
        2 * ssm_dim, "pack_second")
    third, own_third = pack(
        place, [(w_attn_out, 0, q_dim, 0, True), (w_mixer_out, q_dim, ssm_dim, 0, True)], q_dim + ssm_dim, "pack_third")
    fourth, own_fourth = pack(
        place,
        [(arr, (2 * i + n) * ff_blk, ff_blk, i * ff_blk, False) for i in range(ff_dim // ff_blk) for n, arr in enumerate((w_gate, w_up))]
        + [(w_down, 2 * ff_dim, ff_dim, 0, True)],
        3 * ff_dim, "pack_fourth")
    lens = doc_lengths.reshape(units, -1)
    aux = jnp.pad(jnp.stack([a_log, dt_bias], axis=1), ((0, 16 - heads), (0, 0)))
    skip_row = jnp.repeat(d_skip, head_dim)[None]
    tokens = tokens.reshape(tokens_here, model_dim)
    cotangent = cotangent.reshape(tokens_here, model_dim)
    width = q_dim + ssm_dim

    def placed(shard, mine, other):
        return place_rows(place, shard.reshape(nc, -1, shard.shape[1]), [mine], [other])

    held_first = join(near_first, True)
    near_second = send_near(own_second)
    wait_for(*near_second)
    held_first = spread_far(held_first)
    core_first = swap_context(held_first, 1)
    held_second = join(near_second, True)
    first = placed(first, held_first, core_first)
    n1, q, kv, b, c, per_head, gains = project(place, lens, tokens, first, aux, q_dim, kv_dim, state_dim, pairs)
    kv = kv.reshape(1, units, block_len, 2 * kv_dim)
    kv_far = [swap_context(kv, bit) for bit in far_bits()[:1]]
    near_third = send_near(own_third)
    near_fourth = send_near(own_fourth, True)
    wait_for(*near_third)
    kv_held = join([kv, *kv_far], False)
    for bit in far_bits()[1:]:
        kv_held = join([kv_held, swap_context(kv_held, bit)], False)
    kv_core = swap_context(kv_held, 1)
    held_second = spread_far(held_second)
    core_second = swap_context(held_second, 1)
    kv_all = place_blocks(place, kv_held, kv_core)
    held_third = join(near_third, True)
    wait_for(near_fourth[0])
    second = placed(second, held_second, core_second)
    zx = project_mixer(n1, second)
    span = join([mamba_state(u, per_head, b, zx) for u in range(units)], True)[None]
    span_far = [swap_context(span, bit) for bit in far_bits()[:1]]
    og, lse = None, [None] * units
    wait_for(*near_fourth[1:2])
    og, lse[0] = attention_forward(0, place, lens, q, kv_all, og, width)
    span = join([span, *span_far], False)
    for bit in far_bits()[1:]:
        span = join([span, swap_context(span, bit)], False)
    spans = (span, swap_context(span, 1))
    wait_for(*near_fourth[2:])
    held_third = spread_far(held_third)
    core_third = swap_context(held_third, 1)
    held_fourth = join(near_fourth, True)
    state = chain_states(place, spans, state_dim)
    third = placed(third, held_third, core_third)
    og, y_u = mamba_forward(0, place, lens, per_head, zx, b, c, state, skip_row, og, q_dim)
    y, ours = [y_u], [mixer_out(0, og, third, block_len)]
    theirs = [swap_tensor(ours[0])]
    for u in range(1, units):
        og, lse[u] = attention_forward(u, place, lens, q, kv_all, og, width)
        og, y_u = mamba_forward(u, place, lens, per_head, zx, b, c, state, skip_row, og, q_dim)
        y.append(y_u)
        ours.append(mixer_out(u, og, third, block_len))
        theirs.append(swap_tensor(ours[u]))
    held_fourth = spread_far(held_fourth, 3)
    fourth = place_rows(
        place, fourth.reshape(nc, -1, fourth.shape[1]), held_fourth, [swap_context(arr, 1) for arr in held_fourth])

    stacked, dn2, dn2_theirs = None, [], []
    for u in range(units):
        *stacked, dn2_u = feed_forward(u, tokens, ours[u], theirs[u], gains, cotangent, fourth, stacked)
        dn2.append(dn2_u)
        dn2_theirs.append(swap_tensor(dn2_u))
    h1, n2, f, dab = stacked
    wide = 3 * ff_dim
    away, keep_fourth = outer(place, n2, dab, None, 0, wide)
    wait_for(dn2_theirs[0])
    away, keep_fourth = outer(place, cotangent, f, (away, keep_fourth), 2 * ff_dim, wide)
    got_fourth = swap_context(away, 1)

    dm, dh, dog, d_span, local = None, [], [], [], []
    g_gain_two = 0.0
    d_second, dq, dkv, head_grads = None, [None] * units, [None] * units, 0.0
    bits = context_bits()[1:]

    def open_backward(u, dm):
        dm, dh_u, dog_u, terms = middle_backward(u, h1, dn2[u], dn2_theirs[u], gains, cotangent, third, dm)
        dh.append(dh_u)
        dog.append(dog_u)
        local.append(mamba_state(u, per_head, c, zx, dog_u, q_dim)[None, None])
        return dm, terms[0]

    def attend_back(u):
        dq[u], away, keep = attention_backward(u, place, lens, q, dog[u], og, kv_all, lse[u])
        return keep, swap_context(away, 1)

    def close_states(u):
        held = spread_far(local[u])
        return held, swap_context(held, 1)

    def to_owners(keep, got):
        own, *away = split_fsdp(place, keep, got)
        return [own] + [from_next(arr, "fsdp", k + 1) for k, arr in enumerate(away)]

    def share(total):
        held = spread_far(total[None])
        return held, swap_context(held, 1)

    for u in range(units - 1):
        dm, terms = open_backward(u, dm)
        g_gain_two = g_gain_two + terms
        kept = attend_back(u)
        pair = close_states(u)
        if u == 0:
            keep_fourth, got_fourth = reduce_far(place, keep_fourth, got_fourth, bits)
        dkv[u] = reduce_far(place, *kept, bits)
        d_span.append(chain_states(place, spans, state_dim, pair, u)[0])
    dm, terms = open_backward(units - 1, dm)
    g_gain_two = g_gain_two + terms
    ff = feed_forward_out(f, fourth)
    ff_theirs = swap_tensor(ff)
    at_zx = q_dim + ssm_dim
    at_rest = at_zx + 2 * ssm_dim
    wide = wide_second = at_rest + 2 * state_dim + 256
    pair_second = outer(place, dm, og, None, 0, wide)
    for u in range(units):
        if u == units - 1:
            pair = close_states(u)
            parts_fourth = to_owners(keep_fourth, got_fourth)
            d_span.append(chain_states(place, spans, state_dim, pair, u)[0])
        *d_second, grads_u = mamba_backward(
            u, place, lens, per_head, zx, y[u], dog[u], q_dim, b, c, state, d_span[u], skip_row, aux, d_second)
        head_grads = head_grads + grads_u
    dzx, dbc = d_second
    wait_for(ff_theirs)
    pair_second = outer(place, n1, dzx, pair_second, at_zx, wide)
    away, keep_second = outer(place, n1, dbc, pair_second, at_rest, wide)
    got_second = swap_context(away, 1)
    parts, parts_theirs, g_gain_one, dqkv = [None] * units, [None] * units, 0.0, None

    def close_backward(u, dqkv):
        dqkv, parts[u], terms = input_backward(u, dq[u], *dkv[u], dbc, dzx, first, second, tokens, dqkv)
        parts_theirs[u] = swap_tensor(parts[u])
        return dqkv, terms[0]

    for u in range(units - 1):
        dqkv, terms = close_backward(u, dqkv)
        g_gain_one = g_gain_one + terms
    keep_second, got_second = reduce_far(place, keep_second, got_second, bits)
    kept = attend_back(units - 1)
    wait_for(*parts_theirs[: units - 1])
    layer_out = close_forward(h1, ff, ff_theirs)
    g_fourth = sum_parts(parts_fourth)
    dkv[units - 1] = reduce_far(place, *kept, bits)
    own_second, *below = split_fsdp(place, keep_second, got_second)
    chunks = below[::-1]
    ring = from_next(chunks[0], "fsdp")
    fourth_held = spread_far(g_fourth[None])
    fourth_core = swap_context(fourth_held, 1)
    nf = lax.axis_size("fsdp")
    for k in range(1, nf - 2):
        ring = from_next(ring_step(ring, chunks[k]), "fsdp")
    dqkv, terms = close_backward(units - 1, dqkv)
    g_gain_one = g_gain_one + terms
    nf = lax.axis_size("fsdp")
    part = model_dim // (nf * nc)
    g_gain_one = g_gain_one + swap_tensor(g_gain_one)
    head_grads = jnp.tile(jnp.pad(head_grads[:16, :3], ((0, part - 16), (0, 0))), (nf * nc, 1))
    g_gains = jnp.concatenate([jnp.stack([g_gain_one, g_gain_two], axis=1), head_grads], axis=1).astype(LOW)
    g_gains = jnp.pad(g_gains, ((0, 0), (0, 123)))
    wide = at_b + 128
    away, keep_first = outer(place, n1, dqkv, None, 0, wide)
    g_gains = g_gains.reshape((nf, nc // 2, 2, -1, 128))
    mine = ci % 2
    away = away.at[..., at_b:].set(lax.dynamic_index_in_dim(g_gains, 1 - mine, 2, keepdims=False))
    keep_first = keep_first.at[..., at_b:].set(lax.dynamic_index_in_dim(g_gains, mine, 2, keepdims=False))
    got_first = swap_context(away, 1)
    if nf > 2:
        ring = from_next(ring_step(ring, chunks[nf - 2]), "fsdp")
    input_grads = None
    for u in range(units - 1):
        input_grads = finish(u, tokens, parts[u], parts_theirs[u], gains, dh[u], input_grads)
    keep_first, got_first = reduce_far(place, keep_first, got_first, bits)

    def columns(first, width, turned=False):
        return [(first, width)], turned

    def in_turns(which, width, total, first=0):
        return [(first + width * (2 * i + which), width) for i in range(total // width)], False

    wait_for(parts_theirs[units - 1])
    g_gate, g_up, g_down = emit(
        place, fourth_held, fourth_core,
        [in_turns(0, ff_blk, ff_dim), in_turns(1, ff_blk, ff_dim), columns(2 * ff_dim, ff_dim, True)], "emit_fourth")
    parts_first = to_owners(keep_first, got_first)
    g_second = share_columns(ring_step(ring, own_second), at_rest, at_rest + 2 * state_dim)
    g_first = sum_parts(parts_first, (), place)
    u = units - 1
    input_grads = finish(u, tokens, parts[u], parts_theirs[u], gains, dh[u], input_grads)
    last_held = spread_far(jnp.concatenate([g_second, g_first], axis=1)[None])
    last_core = swap_context(last_held, 1)
    at_last = wide_second
    outs = [
        columns(0, q_dim, True), columns(q_dim, ssm_dim, True), in_turns(0, two, ssm_dim, at_zx), in_turns(1, two, ssm_dim, at_zx),
        columns(at_rest, state_dim), columns(at_rest + state_dim, state_dim), columns(at_rest + 2 * state_dim, heads, True)]
    g_attn, g_mixer, g_z, g_x, g_b, g_c, g_dt = emit(place, last_held, last_core, outs, "emit_second")
    g_q, g_k, g_v, g_gains = emit(
        place, last_held, last_core,
        [columns(at_last, q_dim), columns(at_last + at_k, kv_dim, True), columns(at_last + at_v, kv_dim, True),
         columns(at_last + at_b, 16, True)], "emit_first")
    head_grads = g_gains[2:5]
    shape = (micro_count, seq_count, block_len, model_dim)
    return (
        layer_out.reshape(shape), input_grads.reshape(shape), g_gains[0], g_q, g_k.T, g_v.T, g_z, g_x, g_b, g_c, g_dt.T,
        head_grads[0, :heads], head_grads[1, :heads], head_grads[2, :heads], g_attn, g_mixer, g_gains[1], g_gate, g_up, g_down,
    )


def solution(mesh):
    rows, cols = P("fsdp", "tensor"), P("tensor", "fsdp")
    acts = P(None, "fsdp", "context", None)
    return jax.shard_map(
        per_device,
        mesh=mesh,
        in_specs=(
            acts, acts, P(None, "fsdp", None), P("fsdp"), rows, rows, rows, rows, rows, P("fsdp", None),
            P("fsdp", None), rows, P("tensor"), P("tensor"), P("tensor"), cols, cols, P("fsdp"), rows, rows, cols,
        ),
        out_specs=(
            acts, acts, P("fsdp"), rows, rows, rows, rows, rows, P("fsdp", None), P("fsdp", None), rows,
            P("tensor"), P("tensor"), P("tensor"), cols, cols, P("fsdp"), rows, rows, cols,
        ),
        check_vma=False,
    )
```

```python
import jax
import jax.numpy as jnp
from jax import lax
from jax.experimental import pallas as pl
from jax.experimental.pallas import tpu as pltpu
from jax.sharding import PartitionSpec as P

HEAD_WIDTH = 64
EPSILON = 1e-06
LOW = jnp.bfloat16
F32 = jnp.float32
NEGATIVE = -1e30
PRECISE = lax.Precision.HIGHEST


def swap_context(x, bit):
    size = lax.axis_size("context")
    return lax.ppermute(x, "context", [(i, i ^ bit) for i in range(size)])


def from_next(x, axis, step=1):
    size = lax.axis_size(axis)
    return lax.ppermute(x, axis, [((i + step) % size, i) for i in range(size)])


def swap_tensor(x):
    size = lax.axis_size("tensor")
    return lax.ppermute(x, "tensor", [(i, (i + 1) % size) for i in range(size)])


def context_bits():
    size = lax.axis_size("context")
    return [1 << k for k in range(size.bit_length() - 1)]


def reverse_bits(index):
    bits = context_bits()
    return sum(((index // low) % 2) * high for low, high in zip(bits, reversed(bits)))


CHAIN = []
SCALE = 0.4e9


def anywhere(arrays):
    return [pl.BlockSpec(memory_space=pl.ANY)] * len(arrays)


def whole_spec(shape):
    return pl.BlockSpec(shape, lambda i: (0,) * len(shape))


def pair_spec(rows):
    return pl.BlockSpec((rows, 128), lambda i: (0, i))


SCALARS = pl.BlockSpec(memory_space=pltpu.SMEM)


def wait_for(*arrays):
    CHAIN.extend(arrays)


def launch(body, *, out_shape, in_specs, out_specs, name, us, grid=(1,), scratch_shapes=(), input_output_aliases=None):
    single = not isinstance(out_shape, tuple)
    outs = (out_shape,) if single else out_shape
    specs = [out_specs] if single else list(out_specs)

    def call(*args):
        waits = tuple(CHAIN)
        n_in, n_out = len(args), len(outs)
        at = n_in + len(waits)

        def run(*refs):
            body(*refs[:n_in], *refs[at : at + n_out], *refs[at + n_out + 1 :])

        made = pl.pallas_call(
            run,
            grid=grid,
            out_shape=outs + (jax.ShapeDtypeStruct((8, 128), F32),),
            in_specs=list(in_specs) + anywhere(waits),
            out_specs=specs + anywhere((0,)),
            scratch_shapes=list(scratch_shapes),
            input_output_aliases=input_output_aliases or {},
            compiler_params=pltpu.CompilerParams(vmem_limit_bytes=(60 if name.startswith("pack") else 18 if name in ("feed_forward", "outer") else 10) * 2**20),
            cost_estimate=pl.CostEstimate(flops=int(us * SCALE), bytes_accessed=1, transcendentals=0),
            name=name,
        )(*args, *waits)
        CHAIN[:] = made[-1:]
        return made[0] if single else made[:-1]

    return call


def column_block(cols):
    return next(blk for blk in (512, 256, 128) if cols % blk == 0)


def join(parts, axis_new, splits=1):
    if axis_new:
        parts = [part[None] for part in parts]
    counts = [part.shape[0] for part in parts]
    shape = parts[0].shape[1:]
    cols = shape[-1]
    blk = column_block(cols)

    def spec(count):
        return pl.BlockSpec((count, *shape[:-1], blk), lambda j: (0,) * len(shape) + (j,))

    def body(*refs):
        outs = refs[len(counts) :]
        width = blk // len(outs)
        at = 0
        for ref, count in zip(refs, counts):
            for n, out in enumerate(outs):
                out[at : at + count] = ref[..., n * width : (n + 1) * width]
            at += count

    if splits > 1:
        blk = cols
        out = (sum(counts), *shape[:-1], cols // splits)
        return launch(
            body, out_shape=(jax.ShapeDtypeStruct(out, parts[0].dtype),) * splits, in_specs=[spec(count) for count in counts],
            out_specs=[whole_spec(out)] * splits, name="join", us=3,
        )(*parts)
    return launch(
        body, grid=(cols // blk,), out_shape=jax.ShapeDtypeStruct((sum(counts), *shape), parts[0].dtype),
        in_specs=[spec(count) for count in counts], out_specs=spec(sum(counts)), name="join", us=2,
    )(*parts)


def send_near(own, ring=False):
    got = []
    for k in range(1, lax.axis_size("fsdp")):
        got.append(from_next(got[-1] if ring and got else own, "fsdp", 1 if ring else k))
    return got


def far_bits():
    return list(reversed(context_bits()[1:]))


def spread_far(held, splits=1):
    for bit in far_bits():
        held = join([held, swap_context(held, bit)], False, splits if bit == far_bits()[-1] else 1)
    return held


def place_rows(place, shard, mine, other):
    nc, part, cols = shard.shape
    nf = lax.axis_size("fsdp")
    offsets = [reverse_bits(m) for m in range(nc)][: nc // 2]
    pieces = len(mine)
    blk = column_block(cols // pieces)
    steps = cols // pieces // blk

    def body(place_ref, shard_ref, *refs):
        out_ref = refs[-1]
        fi, ci = place_ref[0], place_ref[1]
        out_ref[fi] = shard_ref[...]

        def fill(mine_ref, other_ref):
            for k in range(1, nf):
                z = lax.rem(fi + k, nf)
                for m, off in enumerate(offsets):
                    at = m * (nf - 1) + k - 1
                    out_ref[z, lax.bitwise_xor(ci, off)] = mine_ref[at]
                    out_ref[z, lax.bitwise_xor(ci, off ^ 1)] = other_ref[at]

        for n in range(pieces):
            pl.when(pl.program_id(0) // steps == n)(lambda n=n: fill(refs[n], refs[pieces + n]))

    def columns(*leading):
        return pl.BlockSpec((*leading, blk), lambda j: (0,) * len(leading) + (j,))

    def piece(n):
        return pl.BlockSpec((count, part, blk), lambda j: (0, 0, jnp.clip(j - n * steps, 0, steps - 1)))

    count = mine[0].shape[0]
    full = launch(
        body,
        grid=(cols // blk,),
        out_shape=jax.ShapeDtypeStruct((nf, nc, part, cols), shard.dtype),
        in_specs=[SCALARS, columns(nc, part)] + [piece(n) for n in range(pieces)] * 2,
        out_specs=columns(nf, nc, part),
        name="place_rows",
        us=cols / 600,
    )(place, shard, *mine, *other)
    return full.reshape(nf * nc * part, cols)


def place_blocks(place, mine, other):
    half, units, rows, cols = mine.shape
    nc = 2 * half
    offsets = [reverse_bits(m) for m in range(nc)][:half]

    def body(place_ref, mine_ref, other_ref, out_ref):
        ci = place_ref[1]
        for u in range(units):
            for m, off in enumerate(offsets):
                for ref, bit in ((mine_ref, 0), (other_ref, 1)):
                    at = pl.multiple_of(lax.bitwise_xor(ci, off ^ bit) * rows, rows)
                    out_ref[u, pl.ds(at, rows), :] = ref[m, u]

    return launch(
        body,
        out_shape=jax.ShapeDtypeStruct((units, nc * rows, cols), mine.dtype),
        in_specs=[SCALARS, whole_spec(mine.shape), whole_spec(other.shape)],
        out_specs=whole_spec((units, nc * rows, cols)),
        name="place_blocks",
        us=1,
    )(place, mine, other)


def at_offset(ref_pair, ci, k, nc):
    off = lax.bitwise_xor(ci, k)
    entry, weight, rest = 0, nc // 2, off
    half = lax.div(off, 2)
    width = nc // 2
    index, bit = 0, width // 2
    low = 1
    while bit:
        index = index + lax.rem(lax.div(half, low), 2) * bit
        bit, low = bit // 2, low * 2
    same = lax.rem(off, 2) == 0
    mine, other = ref_pair
    return index, same, mine, other


def chain_states(place, spans, state_dim, local=None, unit=None):
    half, units, height, width = spans[0].shape
    nc = 2 * half
    blk = column_block(width)
    count = units if local is None else 1
    extra = () if local is None else tuple(local)

    def body(place_ref, *refs):
        ci = place_ref[1]
        out_ref = refs[-1]
        for n in range(count):
            u = n if local is None else unit
            total = jnp.zeros((state_dim, blk), F32)
            for k in range(nc - 1) if local is None else range(nc - 1, 0, -1):
                index, same, mine, other = at_offset(refs[:2], ci, k, nc)
                passing = jnp.where(same, mine[index, u, state_dim:].astype(F32), other[index, u, state_dim:].astype(F32))
                if local is None:
                    term = jnp.where(same, mine[index, u, :state_dim].astype(F32), other[index, u, :state_dim].astype(F32))
                    active = k < ci
                else:
                    term = jnp.where(same, refs[2][index, 0].astype(F32), refs[3][index, 0].astype(F32))
                    active = k > ci
                new = (passing[0:1] + passing[1:2]) * total + term
                total = jnp.where(active, new, total)
            out_ref[n] = total.astype(LOW)

    def columns(shape):
        return pl.BlockSpec((*shape[:-1], blk), lambda j: (0,) * (len(shape) - 1) + (j,))

    out = (count, state_dim, width)
    return launch(
        body,
        grid=(width // blk,),
        out_shape=jax.ShapeDtypeStruct(out, LOW),
        in_specs=[SCALARS] + [columns(arr.shape) for arr in (*spans, *extra)],
        out_specs=columns(out),
        name="chain_states",
        us=1.2,
    )(place, *spans, *extra)


def outer(place, left, right, into, at, width, last=None):
    nf, nc = lax.axis_size("fsdp"), lax.axis_size("context")
    tokens, model = left.shape
    cols = right.shape[1]
    part = model // (nf * nc)
    blk = next(b for b in (512, 256, 128) if cols % b == 0 and at % b == 0)
    given = () if into is None else tuple(into)
    lasts = () if last is None else (last,)

    def body(place_ref, left_ref, right_ref, *rest):
        away_ref, keep_ref, turned, made = rest[-4:]

        @pl.when(pl.program_id(0) == 0)
        def _():
            turned[...] = left_ref[...].T

        made[...] = nn_dot(turned[...], right_ref[...])
        if lasts:

            @pl.when(pl.program_id(0) == cols // blk - 1)
            def _():
                for top in range(0, model, part):
                    made[top : top + 8, blk - 128 :] = rest[len(given)][...]

        mine = lax.rem(place_ref[1], 2)
        for z in range(nf):
            for x in range(nc // 2):
                first = (z * nc + 2 * x) * part
                keep_ref[z, x] = made[pl.ds(pl.multiple_of(first + mine * part, part), part), :].astype(LOW)
                away_ref[z, x] = made[pl.ds(pl.multiple_of(first + (1 - mine) * part, part), part), :].astype(LOW)

    shape = jax.ShapeDtypeStruct((nf, nc // 2, part, width), LOW)
    spec = pl.BlockSpec((nf, nc // 2, part, blk), lambda j: (0, 0, 0, at // blk + j))
    return launch(
        body,
        grid=(cols // blk,),
        out_shape=(shape, shape),
        in_specs=[SCALARS, whole_spec((tokens, model)), pl.BlockSpec((tokens, blk), lambda j: (0, j))]
        + anywhere(given) + [whole_spec((8, 128)) for _ in lasts],
        out_specs=[spec, spec],
        input_output_aliases={3: 0, 4: 1} if given else {},
        scratch_shapes=[pltpu.VMEM((model, tokens), LOW), pltpu.VMEM((model, blk), F32)],
        name="outer",
        us=cols / 230,
    )(place, left, right, *given, *lasts)


def split_sum(place, keep, got, bit):
    n, left, rows, cols = keep.shape
    blk = column_block(cols)

    def body(place_ref, keep_ref, got_ref, away_ref, stay_ref):
        mine = lax.rem(lax.div(place_ref[1], bit), 2)
        for z in range(n):
            for j in range(left // 2):
                for ref, b in ((stay_ref, mine), (away_ref, 1 - mine)):
                    i = 2 * j + b
                    ref[z, j] = (keep_ref[z, i].astype(F32) + got_ref[z, i].astype(F32)).astype(LOW)

    def spec(count):
        return pl.BlockSpec((n, count, rows, blk), lambda j: (0, 0, 0, j))

    shape = jax.ShapeDtypeStruct((n, left // 2, rows, cols), LOW)
    return launch(
        body, grid=(cols // blk,), out_shape=(shape, shape), in_specs=[SCALARS, spec(left), spec(left)],
        out_specs=[spec(left // 2)] * 2, name="split_sum", us=cols / 900,
    )(place, keep, got)


def split_fsdp(place, keep, got):
    nf, _, part, cols = keep.shape
    blk = column_block(cols)

    def body(place_ref, keep_ref, got_ref, *outs):
        for k in range(nf):
            z = lax.rem(place_ref[0] + (nf - k), nf)
            outs[k][...] = (keep_ref[z, 0].astype(F32) + got_ref[z, 0].astype(F32)).astype(LOW)

    spec = pl.BlockSpec((nf, 1, part, blk), lambda j: (0, 0, 0, j))
    return launch(
        body, grid=(cols // blk,), out_shape=(jax.ShapeDtypeStruct((part, cols), LOW),) * nf, in_specs=[SCALARS, spec, spec],
        out_specs=[pl.BlockSpec((part, blk), lambda j: (0, j))] * nf, name="split_fsdp", us=cols / 1200,
    )(place, keep, got)


def ring_step(got, own):
    part, cols = own.shape
    blk = column_block(cols)

    def body(got_ref, own_ref, out_ref):
        out_ref[...] = (got_ref[...].astype(F32) + own_ref[...].astype(F32)).astype(LOW)

    spec = pl.BlockSpec((part, blk), lambda j: (0, j))
    return launch(
        body, grid=(cols // blk,), out_shape=jax.ShapeDtypeStruct((part, cols), LOW), in_specs=[spec, spec], out_specs=spec,
        name="ring_step", us=1,
    )(got, own)


def share_columns(total, first, last):
    mid = total[:, first:last]
    mid = (mid.astype(F32) + swap_tensor(mid).astype(F32)).astype(LOW)
    return jnp.concatenate([total[:, :first], mid, total[:, last:]], axis=1)


def sum_parts(parts, shared=(), ordered=None):
    cols = parts[0].shape[1]
    blk = column_block(cols)
    given = () if ordered is None else (ordered,)
    nf = len(parts)

    def body(*refs):
        some = refs[len(given) : -1]
        total = some[0][...].astype(F32)
        for ref in some[1:]:
            total = total + ref[...].astype(F32)
        refs[-1][...] = total.astype(LOW)
        if given:

            @pl.when(pl.program_id(0) == cols // blk - 1)
            def _():
                total = None
                for z in range(nf):
                    k = lax.rem(z + nf - refs[0][0], nf)
                    value = some[0][:, blk - 128 :].astype(F32)
                    for n in range(1, nf):
                        value = jnp.where(k == n, some[n][:, blk - 128 :].astype(F32), value)
                    total = value if total is None else total + value
                refs[-1][:, blk - 128 :] = total.astype(LOW)

    spec = pl.BlockSpec((parts[0].shape[0], blk), lambda j: (0, j))
    total = launch(
        body, grid=(cols // blk,), out_shape=jax.ShapeDtypeStruct(parts[0].shape, LOW),
        in_specs=[SCALARS] * len(given) + [spec] * nf, out_specs=spec, name="sum_parts", us=1.3,
    )(*given, *parts)
    if shared:
        mid = total[:, shared[0] : shared[1]]
        mid = (mid.astype(F32) + swap_tensor(mid).astype(F32)).astype(LOW)
        total = jnp.concatenate([total[:, : shared[0]], mid, total[:, shared[1] :]], axis=1)
    return total


def share_rows(total):
    held = total[None]
    for bit in reversed(context_bits()):
        held = jnp.concatenate([held, swap_context(held, bit)])
    ci = lax.axis_index("context")
    order = [reverse_bits(k) ^ reverse_bits(ci) for k in range(lax.axis_size("context"))]
    rows = jnp.stack([lax.dynamic_index_in_dim(held, m, 0, keepdims=False) for m in order])
    return rows.astype(F32).reshape(-1, total.shape[1])


def reduce_far(place, keep, got, bits):
    for bit in bits:
        away, keep = split_sum(place, keep, got, bit)
        got = swap_context(away, bit)
    return keep, got


def nt_dot(left, right):
    return lax.dot_general(left, right, (((1,), (1,)), ((), ())), preferred_element_type=F32)


def tn_dot(left, right):
    return lax.dot_general(left, right, (((0,), (0,)), ((), ())), preferred_element_type=F32)


def nn_dot(left, right):
    return jnp.dot(left, right, preferred_element_type=F32)


def document_start(lens_ref, unit, position):
    start, end = jnp.zeros_like(position), 0
    for d in range(lens_ref.shape[1]):
        end = end + lens_ref[unit, d]
        start = jnp.where(position >= end, end, start)
    return start


def lower_from(rows):
    u = lax.broadcasted_iota(jnp.int32, (rows, rows), 0)
    t = lax.broadcasted_iota(jnp.int32, (rows, rows), 1)
    return jnp.where(u <= t, 1.0, 0.0)


def project(place, lens, tokens, first, aux, q_dim, kv_dim, state, pairs):
    units = lens.shape[0]
    total, model = tokens.shape
    rows = total // units
    width = first.shape[1]
    at_b = q_dim + 2 * kv_dim
    at_dt = at_b + 2 * state

    def body(place_ref, lens_ref, x_ref, first_ref, aux_ref, n1_ref, q_ref, kv_ref, b_ref, c_ref, head_ref, gains_ref):
        unit = pl.program_id(0)

        @pl.when(unit == 0)
        def _():
            gains_ref[...] = first_ref[:, at_dt:].astype(F32).T[2 * pairs : 2 * pairs + 8]

        x = x_ref[...].astype(F32)
        scale = lax.rsqrt(jnp.mean(x * x, axis=1, keepdims=True) + EPSILON)
        n1_ref[...] = (x * scale * gains_ref[0:1, :]).astype(LOW)
        made = nn_dot(n1_ref[...], first_ref[...])
        q_ref[...] = (made[:, :q_dim].astype(LOW).astype(F32) * 0.125).astype(LOW)
        kv_ref[...] = made[:, q_dim:at_b].astype(LOW)
        b_ref[...] = made[:, at_b : at_b + state].astype(LOW)
        c_ref[...] = made[:, at_b + state : at_dt].astype(LOW)
        raw = made[:, at_dt:].T[:16] + aux_ref[:, 1:2]
        dt = jnp.maximum(raw, 0.0) + jnp.log1p(jnp.exp(-jnp.abs(raw)))
        decay = jnp.dot(-jnp.exp(aux_ref[:, 0:1]) * dt, lower_from(rows), precision=PRECISE, preferred_element_type=F32)
        base = place_ref[1] * rows
        position = base + lax.broadcasted_iota(jnp.int32, (1, rows), 1)
        carried = document_start(lens_ref, unit, position) < base
        closing = position >= document_start(lens_ref, unit, base + rows - 1)
        entering = jnp.where(carried, jnp.exp(decay), 0.0)
        leaving = jnp.where(closing, jnp.exp(decay[:, rows - 1 :] - decay), 0.0)
        for i in range(pairs):
            for at, value in enumerate((decay, dt, entering, leaving)):
                head_ref[i, 2 * at : 2 * at + 2, :] = value[2 * i : 2 * i + 2]

    def of_unit(cols):
        return pl.BlockSpec((rows, cols), lambda u: (u, 0))

    def made_as(cols):
        return jax.ShapeDtypeStruct((total, cols), LOW)

    return launch(
        body,
        grid=(units,),
        out_shape=(
            made_as(model), made_as(q_dim), made_as(2 * kv_dim), made_as(state), made_as(state),
            jax.ShapeDtypeStruct((units, pairs, 8, rows), F32), jax.ShapeDtypeStruct((8, model), F32),
        ),
        in_specs=[SCALARS, SCALARS, of_unit(model), whole_spec((model, width)), whole_spec((16, 2))],
        out_specs=[
            of_unit(model), of_unit(q_dim), of_unit(2 * kv_dim), of_unit(state), of_unit(state),
            pl.BlockSpec((None, pairs, 8, rows), lambda u: (u, 0, 0, 0)), whole_spec((8, model)),
        ],
        us=6.5, name="project",
    )(place, lens, tokens, first, aux)


def attention_forward(unit, place, lens, q, kv_all, into, width):
    units, length, _ = kv_all.shape
    rows, q_dim = q.shape[0] // units, q.shape[1]
    heads = q_dim // HEAD_WIDTH
    given = () if into is None else (into,)

    def body(place_ref, lens_ref, q_ref, kv_ref, *rest):
        o_ref, lse_ref, bias, top, low, acc = rest[-6:]
        top[...] = jnp.full_like(top, NEGATIVE)
        low[...] = jnp.zeros_like(low)
        acc[...] = jnp.zeros_like(acc)
        own = place_ref[1]
        base = own * rows
        start = document_start(lens_ref, unit, base + lax.broadcasted_iota(jnp.int32, (1, rows), 1))
        blocks = own - document_start(lens_ref, unit, base) // rows + 1

        def step(i, carry):
            j = own - i
            at = pl.multiple_of(j * rows, rows)
            keys = kv_ref[pl.ds(at, rows), :HEAD_WIDTH]
            turned = kv_ref[pl.ds(at, rows), :].astype(F32).T[HEAD_WIDTH:].astype(LOW)
            u = at + lax.broadcasted_iota(jnp.int32, (rows, rows), 0)
            t = base + lax.broadcasted_iota(jnp.int32, (rows, rows), 1)
            seen = (u <= t) & (u >= start)
            bias[...] = jnp.where(seen, 0.0, NEGATIVE)
            for h in range(heads):
                lanes = slice(h * HEAD_WIDTH, (h + 1) * HEAD_WIDTH)
                s = nt_dot(keys, q_ref[:, lanes]) + bias[...]
                before = top[h : h + 1, :]
                now = jnp.maximum(before, jnp.max(s, axis=0, keepdims=True))
                p = jnp.exp(s - now)
                scale = jnp.exp(before - now)
                top[h : h + 1, :] = now
                low[h : h + 1, :] = low[h : h + 1, :] * scale + jnp.sum(p, axis=0, keepdims=True)
                acc[lanes, :] = acc[lanes, :] * scale + nn_dot(turned, p.astype(LOW))
            return carry

        lax.fori_loop(0, blocks, step, 0)
        for h in range(heads):
            lanes = slice(h * HEAD_WIDTH, (h + 1) * HEAD_WIDTH)
            acc[lanes, :] = acc[lanes, :] / low[h : h + 1, :]
        o_ref[...] = acc[...].T.astype(LOW)
        lse_ref[...] = top[...] + jnp.log(low[...])

    return launch(
        body,
        grid=(1,),
        out_shape=(jax.ShapeDtypeStruct((units * rows, width), LOW), jax.ShapeDtypeStruct((8, rows), F32)),
        in_specs=[
            SCALARS, SCALARS, pl.BlockSpec((rows, q_dim), lambda i: (unit, 0)),
            pl.BlockSpec((None, length, 2 * HEAD_WIDTH), lambda i: (unit, 0, 0)),
        ] + anywhere(given),
        out_specs=[pl.BlockSpec((rows, q_dim), lambda i: (unit, 0)), whole_spec((8, rows))],
        input_output_aliases={4: 0} if given else {},
        scratch_shapes=[
            pltpu.VMEM((rows, rows), F32),
            pltpu.VMEM((8, rows), F32),
            pltpu.VMEM((8, rows), F32),
            pltpu.VMEM((q_dim, rows), F32),
        ],
        us=10.5, name="attention_forward",
    )(place, lens, q, kv_all, *given)


def attention_backward(unit, place, lens, q, dog, og, kv_all, lse):
    units, length, _ = kv_all.shape
    rows, q_dim = q.shape[0] // units, q.shape[1]
    heads = q_dim // HEAD_WIDTH
    half = (1, length // rows // 2, rows, 2 * HEAD_WIDTH)
    sub = min(256, rows)

    def body(place_ref, lens_ref, q_ref, do_ref, o_ref, kv_ref, lse_ref, *rest):
        dq_ref, away_ref, keep_ref, bias, dq_acc, delta = rest[-6:]
        own = place_ref[1]
        base = own * rows
        start = document_start(lens_ref, unit, base + lax.broadcasted_iota(jnp.int32, (1, rows), 1))
        blocks = own - document_start(lens_ref, unit, base) // rows + 1
        dq_acc[...] = jnp.zeros_like(dq_acc)
        away_ref[...] = jnp.zeros_like(away_ref)
        keep_ref[...] = jnp.zeros_like(keep_ref)
        both = do_ref[...].astype(F32) * o_ref[...].astype(F32)
        lane = lax.broadcasted_iota(jnp.int32, (rows, 128), 1)
        columns = jnp.zeros((rows, 128), F32)
        for h in range(heads):
            total = jnp.sum(both[:, h * HEAD_WIDTH : (h + 1) * HEAD_WIDTH], axis=1, keepdims=True)
            columns = jnp.where(lane == h, total, columns)
        delta[...] = columns.T[:8]

        def step(i, carry):
            j = own - i
            at = pl.multiple_of(j * rows, rows)
            u = at + lax.broadcasted_iota(jnp.int32, (rows, rows), 0)
            t = base + lax.broadcasted_iota(jnp.int32, (rows, rows), 1)
            seen = (u <= t) & (u >= start)
            bias[...] = jnp.where(seen, 0.0, NEGATIVE)
            for r in range(0, rows, sub):
                keys = kv_ref[pl.ds(pl.multiple_of(at + r, sub), sub), :HEAD_WIDTH]
                values = kv_ref[pl.ds(pl.multiple_of(at + r, sub), sub), HEAD_WIDTH:]
                dk = jnp.zeros((sub, HEAD_WIDTH), F32)
                dv = jnp.zeros((sub, HEAD_WIDTH), F32)
                for h in range(heads):
                    lanes = slice(h * HEAD_WIDTH, (h + 1) * HEAD_WIDTH)
                    q_h, do_h = q_ref[:, lanes], do_ref[:, lanes]
                    p = jnp.exp(nt_dot(keys, q_h) + (bias[r : r + sub, :] - lse_ref[h : h + 1, :]))
                    ds = (p * (nt_dot(values, do_h) - delta[h : h + 1, :])).astype(LOW)
                    dv = dv + nn_dot(p.astype(LOW), do_h)
                    dk = dk + nn_dot(ds, q_h)
                    dq_acc[:, lanes] = dq_acc[:, lanes] + tn_dot(ds, keys)
                dkv = jnp.concatenate([dk, dv], axis=1).astype(LOW)

                @pl.when(lax.rem(own - j, 2) == 0)
                def _():
                    keep_ref[0, j // 2, r : r + sub, :] = dkv

                @pl.when(lax.rem(own - j, 2) == 1)
                def _():
                    away_ref[0, j // 2, r : r + sub, :] = dkv
            return carry

        lax.fori_loop(0, blocks, step, 0)
        dq_ref[...] = (dq_acc[...] * 0.125).astype(LOW)

    return launch(
        body,
        out_shape=(jax.ShapeDtypeStruct((rows, q_dim), LOW),) + (jax.ShapeDtypeStruct(half, LOW),) * 2,
        grid=(1,),
        in_specs=[
            SCALARS, SCALARS, pl.BlockSpec((rows, q_dim), lambda i: (unit, 0)), whole_spec((rows, q_dim)),
            pl.BlockSpec((rows, q_dim), lambda i: (unit, 0)), pl.BlockSpec((None, length, 2 * HEAD_WIDTH), lambda i: (unit, 0, 0)),
            whole_spec((8, rows)),
        ],
        out_specs=[whole_spec((rows, q_dim)), whole_spec(half), whole_spec(half)],
        scratch_shapes=[
            pltpu.VMEM((rows, rows), F32),
            pltpu.VMEM((rows, q_dim), F32),
            pltpu.VMEM((8, rows), F32),
        ],
        us=17, name="attention_backward",
    )(place, lens, q, dog, og, kv_all, lse)


def halves(columns, first, lane):
    return jnp.where(lane < 64, columns[:, first : first + 1], columns[:, first + 1 : first + 2])


def mamba_state(unit, per_head, left, zx, right=None, first=0):
    _, pairs, _, rows = per_head.shape
    state = left.shape[1]
    rights = () if right is None else (right,)
    height = state if rights else state + 16

    def body(head_ref, left_ref, zx_ref, *rest):
        out_ref = rest[-1]
        lane = lax.broadcasted_iota(jnp.int32, (rows, 128), 1)
        turned = left_ref[...].astype(F32).T.astype(LOW)
        for i in range(pairs):
            lanes = slice(128 * i, 128 * (i + 1))
            by_col = head_ref[i].T
            if rights:
                z = zx_ref[:, 256 * i : 256 * i + 128].astype(F32)
                value = rest[0][:, first + 128 * i : first + 128 * (i + 1)].astype(F32) * z * jax.nn.sigmoid(z)
                weight = halves(by_col, 4, lane)
            else:
                value = zx_ref[:, 256 * i + 128 : 256 * (i + 1)].astype(F32)
                weight = halves(by_col, 2, lane) * halves(by_col, 6, lane)
                passing = halves(by_col[rows - 16 :], 4, lane[:16])[15:]
                high = passing.astype(LOW).astype(F32)
                row = lax.broadcasted_iota(jnp.int32, (16, 128), 0)
                out_ref[state:, lanes] = jnp.where(row == 0, high, jnp.where(row == 1, passing - high, 0.0)).astype(LOW)
            out_ref[:state, lanes] = nn_dot(turned, (value * weight).astype(LOW)).astype(LOW)

    return launch(
        body,
        grid=(1,),
        out_shape=jax.ShapeDtypeStruct((height, 128 * pairs), LOW),
        in_specs=[
            pl.BlockSpec((None, pairs, 8, rows), lambda i: (unit, 0, 0, 0)), pl.BlockSpec((rows, state), lambda i: (unit, 0)),
            pl.BlockSpec((rows, 256 * pairs), lambda i: (unit, 0)),
        ] + [whole_spec(r.shape) for r in rights],
        out_specs=whole_spec((height, 128 * pairs)),
        us=2, name="mamba_state",
    )(per_head, left, zx, *rights)


def same_document(place_ref, lens_ref, unit, rows, t_axis):
    base = place_ref[1] * rows
    shape = (1, rows) if t_axis else (rows, 1)
    start = document_start(lens_ref, unit, base + lax.broadcasted_iota(jnp.int32, shape, t_axis)) - base
    t = lax.broadcasted_iota(jnp.int32, (rows, rows), t_axis)
    u = lax.broadcasted_iota(jnp.int32, (rows, rows), 1 - t_axis)
    return (u <= t) & (u >= start)


def mamba_forward(unit, place, lens, per_head, zx, b, c, state_in, skip, into, first):
    _, pairs, _, rows = per_head.shape
    blk = min(256, rows)
    state = b.shape[1]

    def body(place_ref, lens_ref, head_ref, zx_ref, b_ref, c_ref, state_ref, skip_ref, *rest):
        g_ref, y_ref, inner, x_dt = rest[-4:]

        @pl.when(pl.program_id(0) == 0)
        def _():
            seen = same_document(place_ref, lens_ref, unit, rows, 0)
            inner[...] = jnp.where(seen, nt_dot(c_ref[...], b_ref[...]), 0.0)

        lane = lax.broadcasted_iota(jnp.int32, (rows, 128), 1)
        by_row = head_ref[...]
        by_col = by_row.T
        xs_f = zx_ref[:, 128:].astype(F32)
        x_dt[...] = (xs_f * halves(by_col, 2, lane)).astype(LOW)
        read = nn_dot(c_ref[...], state_ref[...]) * halves(by_col, 4, lane)
        for i in range(rows // blk):
            part = slice(i * blk, (i + 1) * blk)
            sums = []
            for h in range(2):
                total = None
                for j in range(i + 1):
                    other = slice(j * blk, (j + 1) * blk)
                    gap = by_col[part, h : h + 1] - by_row[h : h + 1, other]
                    kernel = jnp.exp(jnp.minimum(gap, 0.0)) * inner[part, other]
                    term = nn_dot(kernel.astype(LOW), x_dt[other, :])
                    total = term if total is None else total + term
                sums.append(total)
            y = jnp.where(lane[part] < 64, sums[0], sums[1]) + read[part]
            y_ref[part, :] = y
            z_f = zx_ref[part, :128].astype(F32)
            g_ref[part, :] = ((y + skip_ref[...] * xs_f[part]) * z_f * jax.nn.sigmoid(z_f)).astype(LOW)

    return launch(
        body,
        grid=(pairs,),
        out_shape=(jax.ShapeDtypeStruct(into.shape, LOW), jax.ShapeDtypeStruct((rows, 128 * pairs), F32)),
        in_specs=[
            SCALARS, SCALARS, pl.BlockSpec((None, None, 8, rows), lambda i: (unit, i, 0, 0)), pl.BlockSpec((rows, 256), lambda i: (unit, i)),
            pl.BlockSpec((rows, state), lambda i: (unit, 0)), pl.BlockSpec((rows, state), lambda i: (unit, 0)),
            pl.BlockSpec((None, state, 128), lambda i: (unit, 0, i)), pair_spec(1),
        ] + anywhere((into,)),
        out_specs=[pl.BlockSpec((rows, 128), lambda i: (unit, first // 128 + i)), pair_spec(rows)],
        input_output_aliases={8: 0},
        scratch_shapes=[pltpu.VMEM((rows, rows), F32), pltpu.VMEM((rows, 128), LOW)],
        us=7.5, name="mamba_forward",
    )(place, lens, per_head, zx, b, c, state_in, skip, into)


def mamba_backward(unit, place, lens, per_head, zx, y, dog, first, b, c, state_in, later, skip, aux, into):
    _, pairs, _, rows = per_head.shape
    blk = min(256, rows)
    state = b.shape[1]
    given = () if into is None else tuple(into)

    def body(place_ref, lens_ref, head_ref, zx_ref, y_ref, dg_ref, b_ref, c_ref, state_ref, later_ref, skip_ref, aux_ref, *rest):
        dzx_ref, dbc_ref, grads_ref, inner, d_inner, dy_low, x_low, db, dc, stats = rest[-10:]
        pair = pl.program_id(0)

        @pl.when(pair == 0)
        def _():
            seen = same_document(place_ref, lens_ref, unit, rows, 1)
            inner[...] = jnp.where(seen, nt_dot(b_ref[...], c_ref[...]), 0.0)
            d_inner[...] = jnp.zeros_like(d_inner)
            db[...] = jnp.zeros_like(db)
            dc[...] = jnp.zeros_like(dc)

        lane = lax.broadcasted_iota(jnp.int32, (rows, 128), 1)
        by_row = head_ref[pair]
        by_col = by_row.T
        xs_f = zx_ref[:, 128:].astype(F32)
        z_f = zx_ref[:, :128].astype(F32)
        sig = jax.nn.sigmoid(z_f)
        d_gate = dg_ref[...].astype(F32)
        d_y = d_gate * z_f * sig
        y_core = y_ref[...]
        dzx_ref[:, :128] = (d_gate * (y_core + skip_ref[...] * xs_f) * sig * (1.0 + z_f * (1.0 - sig))).astype(LOW)
        dy_low[...] = d_y.astype(LOW)
        dt = halves(by_col, 2, lane)
        x_dt = xs_f * dt
        x_low[...] = x_dt.astype(LOW)
        closing = halves(by_col, 6, lane)
        from_later = nn_dot(b_ref[...], later_ref[...]) * closing
        db[...] += nt_dot((x_dt * closing).astype(LOW), later_ref[...])
        dc[...] += nt_dot((d_y * halves(by_col, 4, lane)).astype(LOW), state_ref[...])
        count = rows // blk
        columns = jnp.zeros((rows, 128), F32)
        d_x_parts = []
        for j in range(count):
            part = slice(j * blk, (j + 1) * blk)
            sums = []
            for h in range(2):
                own = (lane[part] < 64) if h == 0 else (lane[part] >= 64)
                x_h = jnp.where(own, x_low[part, :].astype(F32), 0.0).astype(LOW)
                total = None
                for i in range(j, count):
                    other = slice(i * blk, (i + 1) * blk)
                    gap = by_row[h : h + 1, other] - by_col[part, h : h + 1]
                    decay = jnp.exp(jnp.minimum(gap, 0.0))
                    term = nn_dot((decay * inner[part, other]).astype(LOW), dy_low[other, :])
                    total = term if total is None else total + term
                    d_inner[part, other] += decay * nt_dot(x_h, dy_low[other, :])
                sums.append(total)
            d_x_parts.append(jnp.where(lane[part] < 64, sums[0], sums[1]))
        d_x = jnp.concatenate(d_x_parts, axis=0) if count > 1 else d_x_parts[0]
        d_x = d_x + from_later
        dzx_ref[:, 128:] = (d_x * dt + skip_ref[...] * d_y).astype(LOW)
        rounded_x = x_low[...].astype(F32)
        rounded_dy = dy_low[...].astype(F32)
        carried_back = jnp.sum(later_ref[...].astype(F32) * state_ref[...].astype(F32), axis=0, keepdims=True)
        row = lax.broadcasted_iota(jnp.int32, (rows, 1), 0)
        for at, value in enumerate((d_x * xs_f, rounded_dy * y_core - rounded_x * d_x, rounded_x * from_later, d_y * xs_f)):
            for h in range(2):
                own = (lane < 64) if h == 0 else (lane >= 64)
                total = jnp.sum(jnp.where(own, value, 0.0), axis=1, keepdims=True)
                if at == 2:
                    own = (lane[:1] < 64) if h == 0 else (lane[:1] >= 64)
                    passed = jnp.sum(jnp.where(own, carried_back, 0.0), axis=1, keepdims=True)
                    total = total + jnp.where(row == rows - 1, passed * by_row[4 + h : 5 + h, rows - 1 :], 0.0)
                columns = jnp.where(lane == 2 * at + h, total, columns)
        stats[pair] = columns.T[:8]

        @pl.when(pair == pairs - 1)
        def _():
            seen = same_document(place_ref, lens_ref, unit, rows, 1)
            low = jnp.where(seen, d_inner[...], 0.0).astype(LOW)
            dbc_ref[:, :state] = (db[...] + nn_dot(low, c_ref[...])).astype(LOW)
            dbc_ref[:, state : 2 * state] = (dc[...] + tn_dot(low, b_ref[...])).astype(LOW)

            def heads_of(ref, at):
                blank = jnp.zeros((16 - 2 * pairs, rows), F32)
                parts = [ref[i, 2 * at : 2 * at + 2, :] for i in range(pairs)]
                return jnp.concatenate(parts + [blank] * (2 * pairs < 16), axis=0)

            dt = heads_of(head_ref, 1)
            rate = -jnp.exp(aux_ref[:, 0:1])
            position = lax.broadcasted_iota(jnp.int32, (1, rows), 1)
            d_end = jnp.sum(heads_of(stats, 2), axis=1, keepdims=True)
            d_decay = heads_of(stats, 1) + jnp.where(position == rows - 1, d_end, 0.0)
            d_rate = lax.dot_general(
                d_decay, lower_from(rows), (((1,), (1,)), ((), ())), precision=PRECISE, preferred_element_type=F32)
            d_raw = (heads_of(stats, 0) + rate * d_rate) * (1.0 - jnp.exp(-dt))
            turned = jnp.concatenate([d_raw, jnp.zeros((112, rows), F32)], axis=0).T
            dbc_ref[:, 2 * state : 2 * state + 128] = turned.astype(LOW)
            dbc_ref[:, 2 * state + 128 :] = jnp.zeros((rows, 128), LOW)
            lanes = lax.broadcasted_iota(jnp.int32, (16, 128), 1)
            sums = jnp.zeros((16, 128), F32)
            for at, value in enumerate((d_rate * rate * dt, d_raw, heads_of(stats, 3))):
                sums = jnp.where(lanes == at, jnp.sum(value, axis=1, keepdims=True), sums)
            grads_ref[...] = sums

    total = zx.shape[0]
    return launch(
        body,
        grid=(pairs,),
        out_shape=(
            jax.ShapeDtypeStruct(zx.shape, LOW), jax.ShapeDtypeStruct((total, 2 * state + 256), LOW),
            jax.ShapeDtypeStruct((16, 128), F32),
        ),
        in_specs=[
            SCALARS, SCALARS, pl.BlockSpec((None, pairs, 8, rows), lambda i: (unit, 0, 0, 0)),
            pl.BlockSpec((rows, 256), lambda i: (unit, i)), pair_spec(rows),
            pl.BlockSpec((rows, 128), lambda i: (0, first // 128 + i)),
            pl.BlockSpec((rows, state), lambda i: (unit, 0)), pl.BlockSpec((rows, state), lambda i: (unit, 0)),
            pl.BlockSpec((None, state, 128), lambda i: (unit, 0, i)), pair_spec(state), pair_spec(1), whole_spec((16, 2)),
        ] + anywhere(given),
        out_specs=[
            pl.BlockSpec((rows, 256), lambda i: (unit, i)), pl.BlockSpec((rows, 2 * state + 256), lambda i: (unit, 0)),
            whole_spec((16, 128)),
        ],
        input_output_aliases={12: 0, 13: 1} if given else {},
        scratch_shapes=[
            pltpu.VMEM((rows, rows), F32), pltpu.VMEM((rows, rows), F32), pltpu.VMEM((rows, 128), LOW), pltpu.VMEM((rows, 128), LOW),
            pltpu.VMEM((rows, state), F32), pltpu.VMEM((rows, state), F32), pltpu.VMEM((pairs, 8, rows), F32),
        ],
        us=16.3, name="mamba_backward",
    )(place, lens, per_head, zx, y, dog, b, c, state_in, later, skip, aux, *given)


def feed_forward(unit, x, ours, theirs, gains, dy, weights, into):
    rows, model = ours.shape
    total = x.shape[0]
    hidden = weights.shape[1] // 3
    blk = min(256, hidden)
    count = hidden // blk
    given = () if into is None else tuple(into)

    def body(x_ref, ours_ref, theirs_ref, gains_ref, dy_ref, ab_ref, down_ref, *rest):
        h1_ref, n2_ref, f_ref, dab_ref, dn2_ref, dn2_acc = rest[-6:]

        @pl.when(pl.program_id(0) == 0)
        def _():
            h1 = x_ref[...].astype(F32) + (ours_ref[...].astype(F32) + theirs_ref[...].astype(F32))
            scale = lax.rsqrt(jnp.mean(h1 * h1, axis=1, keepdims=True) + EPSILON)
            h1_ref[...] = h1
            n2_ref[...] = (h1 * scale * gains_ref[1:2, :]).astype(LOW)

        ab = nn_dot(n2_ref[...], ab_ref[...])
        a, b = ab[:, :blk], ab[:, blk:]
        sig = jax.nn.sigmoid(a)
        silu = a * sig
        f = (silu * b).astype(LOW)
        f_ref[...] = f
        df = nn_dot(dy_ref[...], down_ref[...])
        dab_ref[:, :blk] = (df * b * sig * (1.0 + a * (1.0 - sig))).astype(LOW)
        dab_ref[:, blk:] = (df * silu).astype(LOW)
        dn2 = nt_dot(dab_ref[...], ab_ref[...])

        @pl.when(pl.program_id(0) == 0)
        def _():
            dn2_acc[...] = dn2

        @pl.when(pl.program_id(0) > 0)
        def _():
            dn2_acc[...] += dn2

        @pl.when(pl.program_id(0) == count - 1)
        def _():
            dn2_ref[...] = dn2_acc[...].astype(LOW)

    at_unit = pl.BlockSpec((rows, model), lambda j: (unit, 0))
    return launch(
        body,
        grid=(count,),
        out_shape=(
            jax.ShapeDtypeStruct((total, model), F32), jax.ShapeDtypeStruct((total, model), LOW),
            jax.ShapeDtypeStruct((total, hidden), LOW), jax.ShapeDtypeStruct((total, 2 * hidden), LOW),
            jax.ShapeDtypeStruct((rows, model), LOW),
        ),
        in_specs=[
            at_unit, whole_spec((rows, model)), whole_spec((rows, model)), whole_spec((8, model)), at_unit,
            pl.BlockSpec((model, 2 * blk), lambda j: (0, j)), pl.BlockSpec((model, blk), lambda j: (0, 2 * count + j)),
        ] + anywhere(given),
        out_specs=[
            at_unit, at_unit, pl.BlockSpec((rows, blk), lambda j: (unit, j)), pl.BlockSpec((rows, 2 * blk), lambda j: (unit, j)),
            whole_spec((rows, model)),
        ],
        input_output_aliases={7: 0, 8: 1, 9: 2, 10: 3} if given else {},
        scratch_shapes=[pltpu.VMEM((rows, model), F32)],
        us=14, name="feed_forward",
    )(x, ours, theirs, gains, dy, weights, weights, *given)


def feed_forward_out(f, weights):
    total, hidden = f.shape
    model = weights.shape[0]
    blk = min(512, total)

    def body(f_ref, down_ref, *rest):
        rest[-1][...] = nt_dot(f_ref[...], down_ref[...]).astype(LOW)

    return launch(
        body,
        grid=(total // blk,),
        out_shape=jax.ShapeDtypeStruct((total, model), LOW),
        in_specs=[pl.BlockSpec((blk, hidden), lambda i: (i, 0)), pl.BlockSpec((model, hidden), lambda i: (0, 2))],
        out_specs=pl.BlockSpec((blk, model), lambda i: (i, 0)),
        us=5, name="feed_forward_out",
    )(f, weights)


def norm_gradient(hidden, gain, d_normed):
    inv = lax.rsqrt(jnp.mean(hidden * hidden, axis=1, keepdims=True) + EPSILON)
    weighted = gain * d_normed
    mean = jnp.mean(weighted * hidden, axis=1, keepdims=True)
    normed = hidden * inv
    return inv * weighted - normed * (inv * inv * mean), jnp.sum(d_normed * normed, axis=0, keepdims=True)


def middle_backward(unit, h1, ours, theirs, gains, dy, third, into):
    rows, model = ours.shape
    width = third.shape[1]
    given = () if into is None else (into,)

    def body(h1_ref, ours_ref, theirs_ref, gains_ref, dy_ref, third_ref, *rest):
        dm_ref, dh_ref, dog_ref, sum_ref = rest[-4:]
        dn2 = ours_ref[...].astype(F32) + theirs_ref[...].astype(F32)
        dh, terms = norm_gradient(h1_ref[...], gains_ref[1:2, :], dn2)
        dh = dh + dy_ref[...].astype(F32)
        dh_ref[...] = dh
        dm = dh.astype(LOW)
        dm_ref[...] = dm
        dog_ref[...] = nn_dot(dm, third_ref[...]).astype(LOW)
        sum_ref[...] = jnp.broadcast_to(terms, sum_ref.shape)

    at_unit = pl.BlockSpec((rows, model), lambda i: (unit, 0))
    full = whole_spec((rows, model))
    return launch(
        body,
        grid=(1,),
        out_shape=(
            jax.ShapeDtypeStruct(h1.shape, LOW), jax.ShapeDtypeStruct((rows, model), F32),
            jax.ShapeDtypeStruct((rows, width), LOW), jax.ShapeDtypeStruct((8, model), F32),
        ),
        in_specs=[at_unit, full, full, whole_spec((8, model)), at_unit, whole_spec((model, width))] + anywhere(given),
        out_specs=[at_unit, full, whole_spec((rows, width)), whole_spec((8, model))],
        input_output_aliases={6: 0} if given else {},
        us=5.4, name="middle_backward",
    )(h1, ours, theirs, gains, dy, third, *given)


def input_backward(unit, dq, keep, got, dbc, dzx, first, second, x, into):
    rows, q_dim = dq.shape
    model = first.shape[0]
    blk = 256 if model % 256 == 0 else model
    rest_width = dbc.shape[1]
    width = q_dim + keep.shape[-1]
    rest = first.shape[1] - width
    given = () if into is None else (into,)

    def body(dq_ref, keep_ref, got_ref, dbc_ref, dzx_ref, first_ref, second_ref, x_ref, *others):
        dqkv_ref, part_ref, sum_ref, inv = others[-4:]
        j = pl.program_id(0)

        @pl.when(j == 0)
        def _():
            x = x_ref[...].astype(F32)
            scale = lax.rsqrt(jnp.mean(x * x, axis=1, keepdims=True) + EPSILON)
            inv[...] = jnp.broadcast_to(scale, inv.shape)
            dqkv_ref[:, :q_dim] = dq_ref[...]
            dqkv_ref[:, q_dim:] = (keep_ref[0, 0].astype(F32) + got_ref[0, 0].astype(F32)).astype(LOW)

        part = nt_dot(dqkv_ref[...], first_ref[:, :width]) + nt_dot(dbc_ref[:, :rest], first_ref[:, width:])
        part = part + nt_dot(dzx_ref[...], second_ref[...])
        part_ref[...] = part.astype(LOW)
        x = x_ref[:, pl.ds(pl.multiple_of(j * blk, blk), blk)].astype(F32)
        terms = jnp.sum(part * x * inv[:, :1], axis=0, keepdims=True)
        sum_ref[...] = jnp.broadcast_to(terms, sum_ref.shape)

    return launch(
        body,
        grid=(model // blk,),
        out_shape=(
            jax.ShapeDtypeStruct((x.shape[0], width), LOW), jax.ShapeDtypeStruct((rows, model), LOW), jax.ShapeDtypeStruct((8, model), F32),
        ),
        in_specs=[
            whole_spec((rows, q_dim)), whole_spec(keep.shape), whole_spec(keep.shape), pl.BlockSpec((rows, rest_width), lambda j: (unit, 0)),
            pl.BlockSpec((rows, dzx.shape[1]), lambda j: (unit, 0)), pl.BlockSpec((blk, first.shape[1]), lambda j: (j, 0)),
            pl.BlockSpec((blk, second.shape[1]), lambda j: (j, 0)), pl.BlockSpec((rows, model), lambda j: (unit, 0)),
        ] + anywhere(given),
        out_specs=[
            pl.BlockSpec((rows, width), lambda j: (unit, 0)), pl.BlockSpec((rows, blk), lambda j: (0, j)),
            pl.BlockSpec((8, blk), lambda j: (0, j)),
        ],
        input_output_aliases={8: 0} if given else {},
        scratch_shapes=[pltpu.VMEM((rows, 128), F32)],
        us=6.5, name="input_backward",
    )(dq, keep, got, dbc, dzx, first, second, x, *given)


def finish(unit, x, ours, theirs, gains, dh, into):
    rows, model = ours.shape
    given = () if into is None else (into,)

    def body(x_ref, ours_ref, theirs_ref, gains_ref, dh_ref, *rest):
        dn1 = ours_ref[...].astype(F32) + theirs_ref[...].astype(F32)
        dx, _ = norm_gradient(x_ref[...].astype(F32), gains_ref[0:1, :], dn1)
        rest[-1][...] = dx + dh_ref[...]

    at_unit = pl.BlockSpec((rows, model), lambda i: (unit, 0))
    full = whole_spec((rows, model))
    return launch(
        body,
        grid=(1,),
        out_shape=jax.ShapeDtypeStruct(x.shape, F32),
        in_specs=[at_unit, full, full, whole_spec((8, model)), full] + anywhere(given),
        out_specs=at_unit,
        input_output_aliases={5: 0} if given else {},
        us=4.2, name="finish",
    )(x, ours, theirs, gains, dh, *given)


def pack(place, parts, cols, name):
    arrays = []
    for arr, *_ in parts:
        if not any(arr is other for other in arrays):
            arrays.append(arr)
    where = [next(i for i, other in enumerate(arrays) if other is part[0]) for part in parts]
    nc = lax.axis_size("context")
    rows = arrays[0].shape[1] if parts[0][4] else arrays[0].shape[0]
    filled = max(part[1] + part[2] for part in parts)

    def body(place_ref, *refs):
        out_ref, own_ref = refs[-2:]
        if filled < cols:
            start = filled - filled % 128
            out_ref[:, start:] = jnp.zeros((rows, cols - start), LOW)
        for n, (_, at, width, first, turned) in zip(where, parts):
            if turned:
                out_ref[:, at : at + width] = refs[n][...].astype(F32).T.astype(LOW)
            else:
                out_ref[:, at : at + width] = refs[n][:, first : first + width]
        own_ref[...] = out_ref[pl.ds(pl.multiple_of(place_ref[1] * (rows // nc), rows // nc), rows // nc), :]

    return launch(
        body, out_shape=(jax.ShapeDtypeStruct((rows, cols), LOW), jax.ShapeDtypeStruct((rows // nc, cols), LOW)),
        in_specs=[SCALARS] + [whole_spec(arr.shape) for arr in arrays],
        out_specs=[whole_spec((rows, cols)), whole_spec((rows // nc, cols))], name=name, us=2,
    )(place, *arrays)


def emit(place, held, got, outs, name):
    half, part, _ = held.shape
    low = min(first for pieces, _ in outs for first, _ in pieces)
    low -= low % 128
    cols = max(first + width for pieces, _ in outs for first, width in pieces) - low
    cols += -cols % 128
    nc = 2 * half
    rows = nc * part
    offsets = [reverse_bits(m) for m in range(nc)][:half]
    widths = [sum(width for _, width in pieces) for pieces, _ in outs]

    def body(place_ref, held_ref, got_ref, *refs):
        whole = refs[-1]
        ci = place_ref[1]
        for m, off in enumerate(offsets):
            for ref, bit in ((held_ref, 0), (got_ref, 1)):
                at = pl.multiple_of(lax.bitwise_xor(ci, off ^ bit) * part, part)
                whole[pl.ds(at, part), :] = ref[m, :, low : low + cols].astype(F32)
        for ref, (pieces, turned) in zip(refs, outs):
            to = 0
            for first, width in pieces:
                if turned:
                    ref[to : to + width, :] = whole[:, first - low : first - low + width].T
                else:
                    ref[:, to : to + width] = whole[:, first - low : first - low + width]
                to += width

    shapes = [(width, rows) if turned else (rows, width) for width, (_, turned) in zip(widths, outs)]
    return launch(
        body, out_shape=tuple(jax.ShapeDtypeStruct(shape, F32) for shape in shapes),
        in_specs=[SCALARS, whole_spec(held.shape), whole_spec(held.shape)], out_specs=[whole_spec(shape) for shape in shapes],
        scratch_shapes=[pltpu.VMEM((rows, cols), F32)], name=name, us=3,
    )(place, held, got)


def close_forward(h1, ours, theirs):
    total, model = h1.shape
    blk = min(256, total)

    def body(h1_ref, ours_ref, theirs_ref, out_ref):
        out_ref[...] = (h1_ref[...] + (ours_ref[...].astype(F32) + theirs_ref[...].astype(F32))).astype(LOW)

    spec = pl.BlockSpec((blk, model), lambda i: (i, 0))
    return launch(
        body, grid=(total // blk,), out_shape=jax.ShapeDtypeStruct((total, model), LOW), in_specs=[spec] * 3, out_specs=spec,
        name="close_forward", us=4,
    )(h1, ours, theirs)


def project_mixer(n1, second):
    tokens, model = n1.shape
    cols = second.shape[1]
    blk = column_block(cols)

    def body(n1_ref, second_ref, out_ref):
        out_ref[...] = nn_dot(n1_ref[...], second_ref[...]).astype(LOW)

    return launch(
        body, grid=(cols // blk,), out_shape=jax.ShapeDtypeStruct((tokens, cols), LOW),
        in_specs=[whole_spec((tokens, model)), pl.BlockSpec((model, blk), lambda j: (0, j))],
        out_specs=pl.BlockSpec((tokens, blk), lambda j: (0, j)), name="project_mixer", us=5,
    )(n1, second)


def mixer_out(unit, og, third, rows):
    width = og.shape[1]
    model = third.shape[0]
    blk = column_block(model)

    def body(og_ref, third_ref, out_ref):
        out_ref[...] = nt_dot(og_ref[...], third_ref[...]).astype(LOW)

    return launch(
        body, grid=(model // blk,), out_shape=jax.ShapeDtypeStruct((rows, model), LOW),
        in_specs=[pl.BlockSpec((rows, width), lambda j: (unit, 0)), pl.BlockSpec((blk, width), lambda j: (j, 0))],
        out_specs=pl.BlockSpec((rows, blk), lambda j: (0, j)), name="mixer_out", us=2,
    )(og, third)


def turns(first, second, width):
    count = first.shape[-1] // width
    parts = [arr[..., width * i : width * (i + 1)] for i in range(count) for arr in (first, second)]
    return jnp.concatenate(parts, axis=-1)


def unturned(mixed, width, which):
    count = mixed.shape[-1] // (2 * width)
    return jnp.concatenate([mixed[..., width * (2 * i + which) : width * (2 * i + which + 1)] for i in range(count)], axis=-1)


def per_device(
    tokens, cotangent, doc_lengths, mixer_gain, w_query, key_matrix, value_matrix, mamba_gate_weight,
    mamba_input_weight, w_bproj, w_cproj, w_dt, a_log, dt_bias, d_skip, w_attn_out, w_mixer_out,
    ffn_gain, w_gate, w_up, w_down,
):
    CHAIN.clear()
    micro_count, seq_count, block_len, model_dim = tokens.shape
    rows_here = mixer_gain.shape[0]
    heads = w_dt.shape[1]
    ssm_dim = mamba_gate_weight.shape[1]
    head_dim = ssm_dim // heads
    q_dim = w_query.shape[1]
    kv_dim = key_matrix.shape[1]
    state_dim = w_bproj.shape[1]
    ff_dim = w_gate.shape[1]
    ff_blk = min(256, ff_dim)
    ci = lax.axis_index("context")
    nc = lax.axis_size("context")
    full_len = nc * block_len
    units = micro_count * seq_count
    pairs = heads // 2
    tokens_here = units * block_len
    at_b = q_dim + 2 * kv_dim
    at_c = at_b + state_dim
    at_dt = at_c + state_dim
    at_gain = at_dt + heads
    first_width = at_gain + 2 + -(at_gain + 2) % 128

    place = jnp.stack([lax.axis_index("fsdp"), ci]).astype(jnp.int32)
    at_k, at_v = q_dim, q_dim + kv_dim
    two = 2 * head_dim
    first, own_first = pack(
        place,
        [(w_query, 0, q_dim, 0, False), (key_matrix.T, at_k, kv_dim, 0, True), (value_matrix.T, at_v, kv_dim, 0, True),
         (w_bproj, at_b, state_dim, 0, False), (w_cproj, at_c, state_dim, 0, False), (w_dt.T, at_dt, heads, 0, True),
         (jnp.stack([mixer_gain, ffn_gain]), at_gain, 2, 0, True)],
        first_width, "pack_first")
    near_first = send_near(own_first)
    second, own_second = pack(
        place,
        [(arr, (2 * i + n) * two, two, i * two, False)
         for i in range(pairs) for n, arr in enumerate((mamba_gate_weight, mamba_input_weight))],
        2 * ssm_dim, "pack_second")
    third, own_third = pack(
        place, [(w_attn_out, 0, q_dim, 0, True), (w_mixer_out, q_dim, ssm_dim, 0, True)], q_dim + ssm_dim, "pack_third")
    fourth, own_fourth = pack(
        place,
        [(arr, (2 * i + n) * ff_blk, ff_blk, i * ff_blk, False) for i in range(ff_dim // ff_blk) for n, arr in enumerate((w_gate, w_up))]
        + [(w_down, 2 * ff_dim, ff_dim, 0, True)],
        3 * ff_dim, "pack_fourth")
    lens = doc_lengths.reshape(units, -1)
    aux = jnp.pad(jnp.stack([a_log, dt_bias], axis=1), ((0, 16 - heads), (0, 0)))
    skip_row = jnp.repeat(d_skip, head_dim)[None]
    tokens = tokens.reshape(tokens_here, model_dim)
    cotangent = cotangent.reshape(tokens_here, model_dim)
    width = q_dim + ssm_dim

    def placed(shard, mine, other):
        return place_rows(place, shard.reshape(nc, -1, shard.shape[1]), [mine], [other])

    held_first = join(near_first, True)
    near_second = send_near(own_second)
    wait_for(*near_second)
    held_first = spread_far(held_first)
    core_first = swap_context(held_first, 1)
    held_second = join(near_second, True)
    first = placed(first, held_first, core_first)
    n1, q, kv, b, c, per_head, gains = project(place, lens, tokens, first, aux, q_dim, kv_dim, state_dim, pairs)
    kv = kv.reshape(1, units, block_len, 2 * kv_dim)
    kv_far = [swap_context(kv, bit) for bit in far_bits()[:1]]
    near_third = send_near(own_third)
    near_fourth = send_near(own_fourth, True)
    wait_for(*near_third)
    kv_held = join([kv, *kv_far], False)
    for bit in far_bits()[1:]:
        kv_held = join([kv_held, swap_context(kv_held, bit)], False)
    kv_core = swap_context(kv_held, 1)
    held_second = spread_far(held_second)
    core_second = swap_context(held_second, 1)
    kv_all = place_blocks(place, kv_held, kv_core)
    held_third = join(near_third, True)
    wait_for(near_fourth[0])
    second = placed(second, held_second, core_second)
    zx = project_mixer(n1, second)
    span = join([mamba_state(u, per_head, b, zx) for u in range(units)], True)[None]
    span_far = [swap_context(span, bit) for bit in far_bits()[:1]]
    og, lse = None, [None] * units
    wait_for(*near_fourth[1:2])
    og, lse[0] = attention_forward(0, place, lens, q, kv_all, og, width)
    span = join([span, *span_far], False)
    for bit in far_bits()[1:]:
        span = join([span, swap_context(span, bit)], False)
    spans = (span, swap_context(span, 1))
    wait_for(*near_fourth[2:])
    held_third = spread_far(held_third)
    core_third = swap_context(held_third, 1)
    held_fourth = join(near_fourth, True)
    state = chain_states(place, spans, state_dim)
    third = placed(third, held_third, core_third)
    og, y_u = mamba_forward(0, place, lens, per_head, zx, b, c, state, skip_row, og, q_dim)
    y, ours = [y_u], [mixer_out(0, og, third, block_len)]
    theirs = [swap_tensor(ours[0])]
    for u in range(1, units):
        og, lse[u] = attention_forward(u, place, lens, q, kv_all, og, width)
        og, y_u = mamba_forward(u, place, lens, per_head, zx, b, c, state, skip_row, og, q_dim)
        y.append(y_u)
        ours.append(mixer_out(u, og, third, block_len))
        theirs.append(swap_tensor(ours[u]))
    held_fourth = spread_far(held_fourth, 3)
    fourth = place_rows(
        place, fourth.reshape(nc, -1, fourth.shape[1]), held_fourth, [swap_context(arr, 1) for arr in held_fourth])

    stacked, dn2, dn2_theirs = None, [], []
    for u in range(units):
        *stacked, dn2_u = feed_forward(u, tokens, ours[u], theirs[u], gains, cotangent, fourth, stacked)
        dn2.append(dn2_u)
        dn2_theirs.append(swap_tensor(dn2_u))
    h1, n2, f, dab = stacked
    wide = 3 * ff_dim
    away, keep_fourth = outer(place, n2, dab, None, 0, wide)
    wait_for(dn2_theirs[0])
    away, keep_fourth = outer(place, cotangent, f, (away, keep_fourth), 2 * ff_dim, wide)
    got_fourth = swap_context(away, 1)

    dm, dh, dog, d_span, local = None, [], [], [], []
    g_gain_two = 0.0
    d_second, dq, dkv, head_grads = None, [None] * units, [None] * units, 0.0
    bits = context_bits()[1:]

    def open_backward(u, dm):
        dm, dh_u, dog_u, terms = middle_backward(u, h1, dn2[u], dn2_theirs[u], gains, cotangent, third, dm)
        dh.append(dh_u)
        dog.append(dog_u)
        local.append(mamba_state(u, per_head, c, zx, dog_u, q_dim)[None, None])
        return dm, terms[0]

    def attend_back(u):
        dq[u], away, keep = attention_backward(u, place, lens, q, dog[u], og, kv_all, lse[u])
        return keep, swap_context(away, 1)

    def close_states(u):
        held = spread_far(local[u])
        return held, swap_context(held, 1)

    def to_owners(keep, got):
        own, *away = split_fsdp(place, keep, got)
        return [own] + [from_next(arr, "fsdp", k + 1) for k, arr in enumerate(away)]

    def share(total):
        held = spread_far(total[None])
        return held, swap_context(held, 1)

    for u in range(units - 1):
        dm, terms = open_backward(u, dm)
        g_gain_two = g_gain_two + terms
        kept = attend_back(u)
        pair = close_states(u)
        if u == 0:
            keep_fourth, got_fourth = reduce_far(place, keep_fourth, got_fourth, bits)
        dkv[u] = reduce_far(place, *kept, bits)
        d_span.append(chain_states(place, spans, state_dim, pair, u)[0])
    dm, terms = open_backward(units - 1, dm)
    g_gain_two = g_gain_two + terms
    ff = feed_forward_out(f, fourth)
    ff_theirs = swap_tensor(ff)
    at_zx = q_dim + ssm_dim
    at_rest = at_zx + 2 * ssm_dim
    wide = wide_second = at_rest + 2 * state_dim + 256
    for u in range(units):
        if u == units - 1:
            pair_second = outer(place, dm, og, None, 0, wide)
            pair = close_states(u)
            parts_fourth = to_owners(keep_fourth, got_fourth)
            d_span.append(chain_states(place, spans, state_dim, pair, u)[0])
        *d_second, grads_u = mamba_backward(
            u, place, lens, per_head, zx, y[u], dog[u], q_dim, b, c, state, d_span[u], skip_row, aux, d_second)
        head_grads = head_grads + grads_u
    dzx, dbc = d_second
    wait_for(ff_theirs)
    pair_second = outer(place, n1, dzx, pair_second, at_zx, wide)
    away, keep_second = outer(place, n1, dbc, pair_second, at_rest, wide)
    got_second = swap_context(away, 1)
    parts, parts_theirs, g_gain_one, dqkv = [None] * units, [None] * units, 0.0, None

    def close_backward(u, dqkv):
        dqkv, parts[u], terms = input_backward(u, dq[u], *dkv[u], dbc, dzx, first, second, tokens, dqkv)
        parts_theirs[u] = swap_tensor(parts[u])
        return dqkv, terms[0]

    for u in range(units - 1):
        dqkv, terms = close_backward(u, dqkv)
        g_gain_one = g_gain_one + terms
    keep_second, got_second = reduce_far(place, keep_second, got_second, bits)
    kept = attend_back(units - 1)
    wait_for(*parts_theirs[: units - 1])
    layer_out = close_forward(h1, ff, ff_theirs)
    g_fourth = sum_parts(parts_fourth)
    dkv[units - 1] = reduce_far(place, *kept, bits)
    own_second, *below = split_fsdp(place, keep_second, got_second)
    chunks = below[::-1]
    ring = from_next(chunks[0], "fsdp")
    fourth_held = spread_far(g_fourth[None])
    fourth_core = swap_context(fourth_held, 1)
    nf = lax.axis_size("fsdp")
    for k in range(1, nf - 2):
        ring = from_next(ring_step(ring, chunks[k]), "fsdp")
    dqkv, terms = close_backward(units - 1, dqkv)
    g_gain_one = g_gain_one + terms
    nf = lax.axis_size("fsdp")
    part = model_dim // (nf * nc)
    g_gain_one = g_gain_one + swap_tensor(g_gain_one)
    head_grads = jnp.tile(jnp.pad(head_grads[:16, :3], ((0, part - 16), (0, 0))), (nf * nc, 1))
    g_gains = jnp.concatenate([jnp.stack([g_gain_one, g_gain_two], axis=1), head_grads], axis=1).astype(LOW)
    g_gains = jnp.pad(g_gains, ((0, 0), (0, 123)))
    wide = at_b + 128
    away, keep_first = outer(place, n1, dqkv, None, 0, wide)
    g_gains = g_gains.reshape((nf, nc // 2, 2, -1, 128))
    mine = ci % 2
    away = away.at[..., at_b:].set(lax.dynamic_index_in_dim(g_gains, 1 - mine, 2, keepdims=False))
    keep_first = keep_first.at[..., at_b:].set(lax.dynamic_index_in_dim(g_gains, mine, 2, keepdims=False))
    got_first = swap_context(away, 1)
    if nf > 2:
        ring = from_next(ring_step(ring, chunks[nf - 2]), "fsdp")
    input_grads = None
    for u in range(units - 1):
        input_grads = finish(u, tokens, parts[u], parts_theirs[u], gains, dh[u], input_grads)
    keep_first, got_first = reduce_far(place, keep_first, got_first, bits)

    def columns(first, width, turned=False):
        return [(first, width)], turned

    def in_turns(which, width, total, first=0):
        return [(first + width * (2 * i + which), width) for i in range(total // width)], False

    wait_for(parts_theirs[units - 1])
    g_gate, g_up, g_down = emit(
        place, fourth_held, fourth_core,
        [in_turns(0, ff_blk, ff_dim), in_turns(1, ff_blk, ff_dim), columns(2 * ff_dim, ff_dim, True)], "emit_fourth")
    parts_first = to_owners(keep_first, got_first)
    g_second = share_columns(ring_step(ring, own_second), at_rest, at_rest + 2 * state_dim)
    g_first = sum_parts(parts_first, (), place)
    u = units - 1
    input_grads = finish(u, tokens, parts[u], parts_theirs[u], gains, dh[u], input_grads)
    last_held = spread_far(jnp.concatenate([g_second, g_first], axis=1)[None])
    last_core = swap_context(last_held, 1)
    at_last = wide_second
    outs = [
        columns(0, q_dim, True), columns(q_dim, ssm_dim, True), in_turns(0, two, ssm_dim, at_zx), in_turns(1, two, ssm_dim, at_zx),
        columns(at_rest, state_dim), columns(at_rest + state_dim, state_dim), columns(at_rest + 2 * state_dim, heads, True)]
    g_attn, g_mixer, g_z, g_x, g_b, g_c, g_dt = emit(place, last_held, last_core, outs, "emit_second")
    g_q, g_k, g_v, g_gains = emit(
        place, last_held, last_core,
        [columns(at_last, q_dim), columns(at_last + at_k, kv_dim, True), columns(at_last + at_v, kv_dim, True),
         columns(at_last + at_b, 16, True)], "emit_first")
    head_grads = g_gains[2:5]
    shape = (micro_count, seq_count, block_len, model_dim)
    return (
        layer_out.reshape(shape), input_grads.reshape(shape), g_gains[0], g_q, g_k.T, g_v.T, g_z, g_x, g_b, g_c, g_dt.T,
        head_grads[0, :heads], head_grads[1, :heads], head_grads[2, :heads], g_attn, g_mixer, g_gains[1], g_gate, g_up, g_down,
    )


def solution(mesh):
    rows, cols = P("fsdp", "tensor"), P("tensor", "fsdp")
    acts = P(None, "fsdp", "context", None)
    return jax.shard_map(
        per_device,
        mesh=mesh,
        in_specs=(
            acts, acts, P(None, "fsdp", None), P("fsdp"), rows, rows, rows, rows, rows, P("fsdp", None),
            P("fsdp", None), rows, P("tensor"), P("tensor"), P("tensor"), cols, cols, P("fsdp"), rows, rows, cols,
        ),
        out_specs=(
            acts, acts, P("fsdp"), rows, rows, rows, rows, rows, P("fsdp", None), P("fsdp", None), rows,
            P("tensor"), P("tensor"), P("tensor"), cols, cols, P("fsdp"), rows, rows, cols,
        ),
        check_vma=False,
    )
```
